32 devices in a mesh: seq: 4 (over y, x), fsdp: 8 (over z, core).
Axes of the slice: x: 2, y: 2, z: 4, core: 2. Of those that a mesh axis runs over, the one named last changes fastest.
Arguments:
- patches: bfloat16 [8, 2176, 1176], P('fsdp', 'seq'), may hold values from -6 to 6
- send_slot: int32 [8, 68], P('fsdp', 'seq'), may hold values from 0 to 67, as said below
- segments: int32 [8, 68], P('fsdp'), may hold values from 0 to 7, never falling along the last dimension, each value on 1 to 24 neighbouring positions
- stem_weight: bfloat16 [3584, 1176], P('fsdp'), may hold values from -0.1875 to 0.1875
- norm_gain: bfloat16 [3584], P('fsdp'), may hold values from 0.099609375 to 1.8984375
- conv_kernel: bfloat16 [5, 3584], P(None, 'fsdp'), may hold values from -3 to 3
- cotangent: bfloat16 [8, 2176, 3584], P('fsdp', 'seq'), may hold values from -6 to 6
Outputs:
- features: bfloat16 [8, 2176, 3584], P('fsdp', 'seq')
- grad_patches: bfloat16 [8, 2176, 1176], P('fsdp', 'seq')
- grad_weight: bfloat16 [3584, 1176], P('fsdp')
- grad_channels: float32 [6, 3584], P(None, 'fsdp')
The draws below stay inside these ranges and needn't reach their ends.
Inputs may be any that keep to these rules, and one draw needn't show every extreme that they name: `send_slot`: each row is a permutation of the packed slots. At most 8 frame slots of one device go to one device's packed slots, and every device sends exactly 8 to some device; within a row the number that device s sends to device (s + o) modulo the seq axis size depends on o alone. `segments`: ids never fall along a row; a clip holds 1 to 24 slots, one exactly 24.
All inputs are finite; a program needn't handle non-finite values.
Results may differ from the reference program's by a relative error of at most 0.0056.
Values may be sent and summed in bfloat16 or wider, within the bound.
No kernel may reach another device: no remote copies, remote signals or barrier semaphores. Data moves between devices by JAX's collectives and lax.ppermute only.
A program may use at most 192 MiB of HBM per device.

```python
import math
import jax
import jax.numpy as jnp
import numpy as np
from jax import lax

D = 3584
P_SIZE = 1176
SP = 32
SLOTS_DEV = 17
CLIP_MOST = 24
TOK_DEV = 544
SEQ_SLOTS = 68
SEQ_ROWS = 2176
CLIPS = 8
ALL_TOKENS = 17408
N_SEQ = 4
N_FSDP = 8


def owner_plan(key):
    device_total = N_SEQ
    slot_total = SLOTS_DEV
    capacity = 2 * SLOTS_DEV // N_SEQ
    subkeys = jax.random.split(key, 4)
    copies = jnp.arange(device_total * capacity, dtype=jnp.int32)
    offsets = copies // capacity
    forced = jax.random.randint(subkeys[0], (), 0, device_total, dtype=jnp.int32)
    shuffled = jax.random.permutation(subkeys[1], device_total * capacity).astype(jnp.int32)
    scores = jnp.where(offsets == forced, copies % capacity - capacity, shuffled)
    chosen = offsets[jnp.argsort(scores)[:slot_total]]
    row_keys = jax.random.split(subkeys[2], device_total)
    slot_offsets = jax.vmap(lambda row_key: chosen[jax.random.permutation(row_key, slot_total)])(row_keys)
    owner_index = (jnp.arange(device_total, dtype=jnp.int32)[:, None] + slot_offsets) % device_total
    flat_owner = owner_index.reshape(-1)
    onehot = (flat_owner[:, None] == jnp.arange(device_total, dtype=jnp.int32)[None, :]).astype(jnp.int32)
    arrival = jnp.sum((jnp.cumsum(onehot, axis=0) - onehot) * onehot, axis=1)
    order_keys = jax.random.split(subkeys[3], device_total)
    orders = jax.vmap(lambda row_key: jax.random.permutation(row_key, slot_total))(order_keys).astype(jnp.int32)
    return (flat_owner * slot_total + orders[flat_owner, arrival]).astype(jnp.int32)


def draw_send_slot(key, part):
    base_key = jax.random.fold_in(key, 11)
    return jax.vmap(owner_plan)(jax.random.split(base_key, N_FSDP))


def strengthened(values, key, source, target, blocks, factor):
    owner, partner = [(jnp.arange(values.shape[axis_at]) // (values.shape[axis_at] // blocks)).reshape([-1 if axis == axis_at else 1 for axis in range(values.ndim)]) for axis_at in (source, target)]
    chosen = jax.random.permutation(key, blocks)[partner]
    strong = (owner == chosen) | (owner == (partner + blocks // 2) % blocks)
    return jnp.where(strong, factor * values, values)


def levels(own_key, shape, cuts, low, top_value):
    gain = 1.0
    for axis_at, shards_of in cuts:
        draws = jax.random.uniform(jax.random.fold_in(jax.random.fold_in(own_key, 6), axis_at), (shards_of,), jnp.float32, low / len(cuts), top_value / len(cuts))
        gain = gain * jnp.repeat(jnp.exp(draws), shape[axis_at] // shards_of).reshape((-1,) + (1,) * (len(shape) - 1 - axis_at))
    return gain


def split_up(number_of, total, reach, lean):
    weights = [(1 << 20) // math.isqrt(standing ** lean) + 1 for standing in range(2, number_of + 1)]
    surplus, counts = total - reach - (number_of - 1), [1] * (number_of - 1)
    while surplus > 0:
        free = [i for i in range(number_of - 1) if counts[i] < reach]
        mass, left = sum([weights[i] for i in free]), surplus
        for i in free:
            more = min(reach - counts[i], max(1, left * weights[i] // mass), surplus)
            counts[i] = counts[i] + more
            surplus = surplus - more
    return np.array([reach] + counts)


def ragged(rng, number_of, total, reach, skew):
    if number_of == 2:
        one = jax.random.randint(rng, (), max(1, total - reach), min(reach, total - 1) + 1)
        return jnp.stack([one, total - one])
    sizes = jnp.asarray(split_up(number_of, total, reach, skew), jnp.int32)
    pairs = (number_of - 1) // 2
    giver, sink = sizes[1:1 + 2 * pairs:2], sizes[2:2 + 2 * pairs:2]
    margin = jnp.minimum(giver - 1, reach - sink)
    moved = jax.random.randint(jax.random.fold_in(rng, 1), (pairs,), 0, 1 << 20) % (margin + 1)
    sizes = sizes.at[1:1 + 2 * pairs:2].set(giver - moved).at[2:2 + 2 * pairs:2].set(sink + moved)
    return sizes[jax.random.permutation(jax.random.fold_in(rng, 2), number_of)]


def bell_draw(own_key, shape, deviation, most, cuts=(), kind=jnp.bfloat16):
    values = jax.random.normal(own_key, shape, jnp.float32) * deviation
    if len(cuts) > 0:
        values = levels(own_key, shape, cuts, -0.22, 0.18) * values
    return jnp.clip(values, min=-most, max=most).astype(kind)


def heavy_noise(key, dims, deviation, bound, cuts, heavy, kind=jnp.bfloat16):
    values = deviation * jax.random.normal(key, dims, jnp.float32)
    if cuts:
        values = values * levels(key, dims, cuts, -0.22, 0.18)
    return jnp.clip(strengthened(values, jax.random.fold_in(key, 3), *heavy), -bound, bound).astype(kind)


def setup_inputs(seed: int = 0) -> dict:
    arg_keys = jax.random.split(jax.random.key(seed), 8)
    return {
        "patches": bell_draw(arg_keys[0], (N_FSDP, SEQ_ROWS, P_SIZE), 1.0, 6.0, ((0, 8), (1, 4))),
        "send_slot": draw_send_slot(jax.random.fold_in(arg_keys[7], 71), 0),
        "segments": jax.vmap(lambda own: jnp.searchsorted(jnp.cumsum(ragged(own, CLIPS, SEQ_SLOTS, CLIP_MOST, 1)), jnp.arange(SEQ_SLOTS), side="right"))(jax.random.split(arg_keys[2], N_FSDP)).reshape((N_FSDP, SEQ_SLOTS)).astype(jnp.int32),
        "stem_weight": bell_draw(arg_keys[3], (D, P_SIZE), P_SIZE ** -0.5, 0.1875, ((0, 8),)),
        "norm_gain": jnp.clip(1.0 + 0.18 * jax.random.normal(arg_keys[4], (D,), jnp.float32), 0.099609375, 1.8984375).astype(jnp.bfloat16),
        "conv_kernel": bell_draw(arg_keys[5], (5, D), 0.5, 3.0, ((1, 8),)),
        "cotangent": heavy_noise(arg_keys[6], (N_FSDP, SEQ_ROWS, D), 1.0, 6.0, ((0, 8), (1, 4)), (0, 2, 8, 2.0)),
    }


EPSILON = 1e-06

def slot_mask(segment_row, centre):
    slot_total = segment_row.shape[0]
    safe_centre = jnp.clip(centre, 0, slot_total - 1)
    columns = []
    for offset in range(5):
        neighbour = centre + (offset - 2)
        inside = (neighbour >= 0) & (neighbour < slot_total) & (centre >= 0) & (centre < slot_total)
        same_clip = segment_row[jnp.clip(neighbour, 0, slot_total - 1)] == segment_row[safe_centre]
        columns.append((inside & same_clip).astype(jnp.float32))
    return jnp.stack(columns, axis=1)

def temporal_mix(padded, clip_mask, kernel, slot_total):
    kernel_wide = kernel.astype(jnp.float32)
    result = padded[0:slot_total].astype(jnp.float32) * (clip_mask[:, 0][:, None, None] * kernel_wide[0][None, None, :])
    for offset in range(1, 5):
        addend = padded[offset:offset + slot_total].astype(jnp.float32) * (clip_mask[:, offset][:, None, None] * kernel_wide[offset][None, None, :])
        result = result + addend
    return result

def temporal_back(slope_padded, mask_padded, kernel, slot_total):
    kernel_wide = kernel.astype(jnp.float32)
    result = jnp.zeros((slot_total,) + slope_padded.shape[1:], jnp.float32)
    for offset in range(5):
        first_row = 4 - offset
        weights_row = mask_padded[first_row:first_row + slot_total, offset][:, None, None] * kernel_wide[offset][None, None, :]
        result = result + slope_padded[first_row:first_row + slot_total].astype(jnp.float32) * weights_row
    return result

def kernel_terms(slope_blocks, padded, clip_mask, slot_total):
    stacked = []
    for offset in range(5):
        product = lax.optimization_barrier(jnp.sum(slope_blocks.astype(jnp.float32) * padded[offset:offset + slot_total].astype(jnp.float32), axis=1))
        stacked.append(product * clip_mask[:, offset][:, None])
    return jnp.stack(stacked, axis=1)

def reference(patches, send_slot, segments, stem_weight, norm_gain, conv_kernel, cotangent):
    gain_wide = norm_gain.astype(jnp.float32)
    centre = jnp.arange(SEQ_SLOTS, dtype=jnp.int32)
    extended = jnp.arange(-2, SEQ_SLOTS + 2, dtype=jnp.int32)
    pad_slots = ((2, 2), (0, 0), (0, 0))

    def one_group(totals, inputs):
        weight_total, chan_total = totals
        patch_rows, destination, segment_row, upstream = inputs
        frames = patch_rows.reshape(SEQ_SLOTS, SP, P_SIZE)
        packed = jnp.zeros_like(frames).at[destination].set(frames).reshape(SEQ_ROWS, P_SIZE)
        stem_out = jnp.dot(packed, stem_weight.T, preferred_element_type=jnp.float32)
        inv_rms = lax.rsqrt(lax.optimization_barrier(jnp.mean(stem_out * stem_out, axis=1, keepdims=True)) + EPSILON)
        unit_rows = stem_out * inv_rms
        normed = (unit_rows * gain_wide).astype(jnp.bfloat16)
        clip_mask = slot_mask(segment_row, centre)
        padded = jnp.pad(normed.reshape(SEQ_SLOTS, SP, D), pad_slots)
        mixed_rows = temporal_mix(padded, clip_mask, conv_kernel, SEQ_SLOTS).reshape(SEQ_ROWS, D)
        features = (stem_out + jax.nn.silu(mixed_rows)).astype(jnp.bfloat16)
        gate_value = jax.nn.sigmoid(mixed_rows)
        upstream_wide = upstream.astype(jnp.float32)
        slope_low = (upstream_wide * gate_value * (1.0 + mixed_rows * (1.0 - gate_value))).astype(jnp.bfloat16)
        slope_blocks = slope_low.reshape(SEQ_SLOTS, SP, D)
        mask_padded = slot_mask(segment_row, extended)
        d_normed = temporal_back(jnp.pad(slope_blocks, pad_slots), mask_padded, conv_kernel, SEQ_SLOTS).reshape(SEQ_ROWS, D)
        gated = d_normed * gain_wide
        d_stem = upstream_wide + inv_rms * (gated - unit_rows * lax.optimization_barrier(jnp.mean(gated * unit_rows, axis=1, keepdims=True)))
        d_stem_low = d_stem.astype(jnp.bfloat16)
        grad_rows = jnp.dot(d_stem_low, stem_weight, preferred_element_type=jnp.float32).astype(jnp.bfloat16)
        gain_part = lax.optimization_barrier(jnp.sum((d_normed * unit_rows).reshape(N_SEQ, TOK_DEV, D), axis=1))
        kernel_part = lax.optimization_barrier(jnp.sum(kernel_terms(slope_blocks, padded, clip_mask, SEQ_SLOTS).reshape(N_SEQ, SLOTS_DEV, 5, D), axis=1))
        chan_part = jnp.concatenate([gain_part[:, None, :], kernel_part], axis=1)
        chan_total = chan_total + lax.optimization_barrier(jnp.sum(chan_part, axis=0))

        def device_term(running, pieces):
            grad_piece, input_piece = pieces
            weight_part = lax.dot_general(grad_piece, input_piece, (((0,), (0,)), ((), ())), preferred_element_type=jnp.float32)
            return (running + weight_part, None)
        weight_total, unused = lax.scan(device_term, weight_total, (d_stem_low.reshape(N_SEQ, TOK_DEV, D), packed.reshape(N_SEQ, TOK_DEV, P_SIZE)))
        return ((weight_total, chan_total), (features, grad_rows))
    zeros_weight = jnp.zeros((D, P_SIZE), jnp.float32)
    zeros_chan = jnp.zeros((6, D), jnp.float32)
    totals, outputs = lax.scan(one_group, (zeros_weight, zeros_chan), (patches, send_slot, segments, cotangent))
    grad_scale = 1.0 / ALL_TOKENS ** 0.5
    grad_weight = (totals[0] * grad_scale).astype(jnp.bfloat16)
    grad_channels = totals[1] * grad_scale
    return (outputs[0], outputs[1], grad_weight, grad_channels)
```

```python
import functools
import math

import jax
import jax.numpy as jnp
from jax import lax
from jax.experimental import pallas as pl
from jax.experimental.pallas import tpu as pltpu
from jax.sharding import PartitionSpec as P

EPSILON = 1e-06
BF16 = jnp.bfloat16
F32 = jnp.float32
LANES = 128
AXES = ("seq", "fsdp")
VMEM_BYTES = 56 * 1024 * 1024


def round_up(value, unit):
    return (value + unit - 1) // unit * unit


def kernel_params(**more):
    return pltpu.CompilerParams(vmem_limit_bytes=VMEM_BYTES, **more)


def sent(value, route):
    seq_size, fsdp_size = lax.axis_size("seq"), lax.axis_size("fsdp")
    pairs = []
    for s in range(seq_size):
        for f in range(fsdp_size):
            target = route(s, f)
            if target is not None:
                pairs.append((s * fsdp_size + f, target[0] * fsdp_size + target[1]))
    return lax.ppermute(value, AXES, pairs)


def swapped(value, seq_bits, fsdp_bits):
    return sent(value, lambda s, f: (s ^ seq_bits, f ^ fsdp_bits))


def bits_of(size):
    return [1 << i for i in range(size.bit_length() - 1)]


def by_position(pieces, me):
    stack = jnp.stack(pieces, axis=0)
    count = len(pieces)
    tail = stack.shape[1:]
    for bit in bits_of(count):
        view = stack.reshape((count // (2 * bit), 2, bit) + tail)
        flipped = jnp.concatenate([view[:, 1:], view[:, :1]], axis=1)
        stack = jnp.where((me & bit) != 0, flipped, view).reshape((count,) + tail)
    return stack


def outbox_kernel(order_ref, frames_ref, *out_refs):
    width = frames_ref.shape[2]
    for peer, out in enumerate(out_refs):
        capacity, rows, padded = out.shape
        out[:, :, padded - LANES :] = jnp.zeros((capacity, rows, LANES), out.dtype)
        for k in range(capacity):
            out[k, :, :width] = frames_ref[order_ref[peer * capacity + k]]


def place_kernel(pick_ref, frames_ref, *refs):
    inbox, out = refs[:-1], refs[-1]
    slots, _, width = frames_ref.shape
    padded = out.shape[2]
    capacity = inbox[0].shape[0]
    out[:, :, padded - LANES :] = jnp.zeros((slots, out.shape[1], LANES), out.dtype)

    def one(p, carry):
        index = pick_ref[p]

        @pl.when(index < slots)
        def _():
            out[p, :, :width] = frames_ref[index]

        for peer, box in enumerate(inbox):
            first = slots + peer * capacity

            @pl.when((index >= first) & (index < first + capacity))
            def _():
                out[p] = box[index - first]

        return carry

    lax.fori_loop(0, slots, one, 0)


def scalar_call(kernel, out_shape, scalars, arrays):
    return pl.pallas_call(
        kernel,
        grid_spec=pltpu.PrefetchScalarGridSpec(
            num_scalar_prefetch=1,
            grid=(),
            in_specs=[pl.BlockSpec(memory_space=pltpu.VMEM)] * len(arrays),
            out_specs=jax.tree.map(lambda _: pl.BlockSpec(memory_space=pltpu.VMEM), out_shape),
        ),
        out_shape=out_shape,
        compiler_params=kernel_params(),
    )(scalars, *arrays)


def pack_slots(frames, destination, seq_index, seq_size, padded):
    slots, rows, width = frames.shape
    capacity = 2 * slots // seq_size
    owner = (destination // slots) ^ seq_index
    rank = jnp.sum(
        ((owner[:, None] == owner[None, :]) & (destination[None, :] < destination[:, None])).astype(
            jnp.int32
        ),
        axis=1,
    )
    peers = jnp.arange(1, seq_size, dtype=jnp.int32)
    places = jnp.arange(capacity, dtype=jnp.int32)
    hit = (owner[None, None, :] == peers[:, None, None]) & (
        rank[None, None, :] == places[None, :, None]
    )
    numbers = jnp.arange(slots, dtype=jnp.int32)
    order = jnp.sum(jnp.where(hit, numbers, 0), axis=2).reshape(-1)
    outbox = scalar_call(
        outbox_kernel,
        [jax.ShapeDtypeStruct((capacity, rows, padded), BF16)] * (seq_size - 1),
        order,
        [frames],
    )
    inbox = [swapped(box, o + 1, 0) for o, box in enumerate(outbox)]
    rows_of = jnp.stack(
        [destination] + [swapped(destination, o, 0) for o in range(1, seq_size)], axis=0
    )
    match = rows_of[:, :, None] == (seq_index * slots + numbers)[None, None, :]
    source = jnp.sum(
        jnp.where(match, jnp.arange(seq_size, dtype=jnp.int32)[:, None, None], 0), axis=(0, 1)
    )
    local = jnp.sum(jnp.where(match, numbers[None, :, None], 0), axis=(0, 1))
    arrival = jnp.sum(
        ((source[:, None] == source[None, :]) & (numbers[None, :] < numbers[:, None])).astype(
            jnp.int32
        ),
        axis=1,
    )
    pick = jnp.where(source == 0, local, slots + (source - 1) * capacity + arrival)
    return scalar_call(
        place_kernel,
        jax.ShapeDtypeStruct((slots, rows, padded), BF16),
        pick,
        [frames] + inbox,
    )


def gather_weights(own, seq_index, chip, chips, seq_size):
    shard = own.shape[0]
    shared = shard * 4 // 7 // seq_size // 8 * 8
    whole = shard - seq_size * shared
    piece = jnp.concatenate(
        [own[:whole], lax.dynamic_slice_in_dim(own, whole + seq_index * shared, shared, axis=0)],
        axis=0,
    )
    rising, falling = {0: piece}, {0: piece}
    for k in range(1, chips):
        rising[k] = sent(
            rising[k - 1], lambda s, f: (s, f + 2) if k - 1 <= f // 2 < chips - 1 else None
        )
        falling[k] = sent(
            falling[k - 1], lambda s, f: (s, f - 2) if 0 < f // 2 <= chips - k else None
        )
    low = chip < chips // 2
    far = jnp.maximum(chip, chips - 1 - chip)
    towards = jnp.where(low, 1, -1)
    shards, chip_of = [own], [chip]
    for k in range(1, chips):
        value = jnp.where(low, falling[k], rising[k])
        origin = chip + towards * k
        for reach in range(chips // 2, k):
            near = jnp.where(low, rising[k - reach], falling[k - reach])
            value = jnp.where(far == reach, near, value)
            origin = jnp.where(far == reach, chip - towards * (k - reach), origin)
        part = value[whole:]
        parts = [part] + [swapped(part, o, 0) for o in range(1, seq_size)]
        ordered = by_position(parts, seq_index).reshape(seq_size * shared, -1)
        shards.append(jnp.concatenate([value[:whole], ordered], axis=0))
        chip_of.append(origin)
    return shards, chip_of


def load_weights(place_ref, shard_refs, weights, sems):
    chips = len(shard_refs) // 2
    shard = shard_refs[0].shape[0]
    core = place_ref[chips]
    for k in range(chips):
        for h in range(2):
            lane = core if h == 0 else 1 - core
            first = pl.multiple_of((2 * place_ref[k] + lane) * shard, 16)
            pltpu.make_async_copy(
                shard_refs[2 * k + h],
                weights.at[pl.ds(first, shard), :],
                sems.at[2 * place_ref[k] + lane],
            ).start()


def wait_weights(shard_ref, weights, sems, f):
    shard = shard_ref.shape[0]
    pltpu.make_async_copy(
        shard_ref, weights.at[pl.ds(f * shard, shard), :], sems.at[f]
    ).wait()


def stem_kernel(
    place_ref, packed_ref, low_ref, high_ref, *refs, chips, channels, tile
):
    shard_refs = refs[: 2 * chips]
    normed_ref, inv_ref, chan_ref, stem_ref = refs[2 * chips : 2 * chips + 4]
    inputs, weights, acc, squares, inverse, sems, out_sems = refs[2 * chips + 4 :]
    tokens, padded = packed_ref.shape
    edge = low_ref.shape[0]
    width = padded - LANES + 24
    load_weights(place_ref, shard_refs, weights, sems)
    inputs[0:edge] = low_ref[...]
    inputs[edge : edge + tokens] = packed_ref[...]
    inputs[edge + tokens : 2 * edge + tokens] = high_ref[...]
    extra = inputs.shape[0] - 2 * edge - tokens
    row = lax.broadcasted_iota(jnp.int32, (extra, padded), 0)
    column = lax.broadcasted_iota(jnp.int32, (extra, padded), 1)
    inputs[2 * edge + tokens :] = jnp.where(
        (column == row + width) & (row < 6), 1.0, 0.0
    ).astype(BF16)
    squares[...] = jnp.zeros_like(squares)

    def one(j, carry):
        first = pl.multiple_of(j * tile, tile)
        result = lax.dot_general(
            inputs[...],
            weights[pl.ds(first, tile), :],
            (((1,), (1,)), ((), ())),
            preferred_element_type=F32,
        )
        acc[:, pl.ds(first, tile)] = result
        total = squares[...]
        for t in range(tile // LANES):
            part = result[:, t * LANES : (t + 1) * LANES]
            total = total + part * part
        squares[...] = total
        return carry

    group = channels // chips
    steps = channels // tile
    begin, copies = 0, []
    for z in range(chips):
        wait_weights(shard_refs[0], weights, sems, 2 * z)
        wait_weights(shard_refs[0], weights, sems, 2 * z + 1)
        end = (z + 1) * group // tile
        lax.fori_loop(begin, end, one, 0)
        lanes = pl.ds(begin * tile, (end - begin) * tile)
        copy = pltpu.make_async_copy(
            acc.at[pl.ds(edge, tokens), lanes], stem_ref.at[:, lanes], out_sems.at[z]
        )
        copy.start()
        copies.append(copy)
        begin = end
    rows = 2 * edge + tokens
    mean = jnp.sum(squares[...], axis=1, keepdims=True) / channels
    inverse[...] = jnp.broadcast_to(lax.rsqrt(mean + EPSILON), inverse.shape)
    inv_ref[...] = inverse[edge : edge + tokens]
    chan_ref[...] = acc[rows : rows + 8, :]

    def norm(t, carry):
        lanes = pl.ds(pl.multiple_of(t * LANES, LANES), LANES)
        gain = acc[rows : rows + 1, lanes]
        normed_ref[:, lanes] = (acc[0:rows, lanes] * inverse[0:rows] * gain).astype(BF16)
        return carry

    lax.fori_loop(0, channels // LANES, norm, 0)
    for copy in copies:
        copy.wait()


def stem(packed, low, high, shards, places, channels):
    tokens, padded = packed.shape
    edge = low.shape[0]
    chips = len(shards) // 2
    rows = 2 * edge + tokens
    return pl.pallas_call(
        functools.partial(stem_kernel, chips=chips, channels=channels, tile=256),
        grid_spec=pltpu.PrefetchScalarGridSpec(
            num_scalar_prefetch=1,
            grid=(),
            in_specs=[pl.BlockSpec(memory_space=pltpu.VMEM)] * 3
            + [pl.BlockSpec(memory_space=pl.ANY)] * len(shards),
            out_specs=[pl.BlockSpec(memory_space=pltpu.VMEM)] * 3
            + [pl.BlockSpec(memory_space=pl.ANY)],
            scratch_shapes=[
                pltpu.VMEM((rows + 16, padded), BF16),
                pltpu.VMEM((channels, padded), BF16),
                pltpu.VMEM((rows + 16, channels), F32),
                pltpu.VMEM((rows + 16, LANES), F32),
                pltpu.VMEM((rows + 16, LANES), F32),
                pltpu.SemaphoreType.DMA((2 * chips,)),
                pltpu.SemaphoreType.DMA((chips,)),
            ],
        ),
        out_shape=[
            jax.ShapeDtypeStruct((rows, channels), BF16),
            jax.ShapeDtypeStruct((tokens, LANES), F32),
            jax.ShapeDtypeStruct((8, channels), F32),
            jax.ShapeDtypeStruct((tokens, channels), F32),
        ],
        compiler_params=kernel_params(),
    )(places, packed, low, high, *shards)


def gate_of(value):
    return 0.5 * jnp.tanh(0.5 * value) + 0.5


def mixed_at(window, taps, mask_ref, g):
    total = window[0] * (taps[0] * mask_ref[5 * g])
    for k in range(1, 5):
        total = total + window[k] * (taps[k] * mask_ref[5 * g + k])
    return total


def edge_kernel(mask_ref, normed_ref, cot_ref, chan_ref, out_ref, *, slots, rows):
    edges = (0, 1, slots - 2, slots - 1)

    def one(t, carry):
        lanes = pl.ds(pl.multiple_of(t * LANES, LANES), LANES)
        taps = [chan_ref[1 + k : 2 + k, lanes] for k in range(5)]
        for i, g in enumerate(edges):
            window = [
                normed_ref[(g + k) * rows : (g + k + 1) * rows, lanes].astype(F32) for k in range(5)
            ]
            mixed = mixed_at(window, taps, mask_ref, g)
            gate = gate_of(mixed)
            up = cot_ref[g * rows : (g + 1) * rows, lanes].astype(F32)
            slope = up * gate * (1.0 + mixed * (1.0 - gate))
            out_ref[i * rows : (i + 1) * rows, lanes] = slope.astype(BF16)
        return carry

    lax.fori_loop(0, out_ref.shape[1] // LANES, one, 0)


def forward_kernel(
    mask_ref, normed_ref, stem_ref, cot_ref, chan_ref, feat_ref, slope_ref, part_ref, *, slots, rows
):
    def one(t, carry):
        lanes = pl.ds(pl.multiple_of(t * LANES, LANES), LANES)
        taps = [chan_ref[1 + k : 2 + k, lanes] for k in range(5)]

        def slot(i):
            return normed_ref[i * rows : (i + 1) * rows, lanes].astype(F32)

        window = [slot(i) for i in range(4)]
        sums = [jnp.zeros((8, LANES), F32) for _ in range(5)]
        for g in range(slots):
            window.append(slot(g + 4))
            mixed = mixed_at(window, taps, mask_ref, g)
            gate = gate_of(mixed)
            here = slice(g * rows, (g + 1) * rows)
            feat_ref[here, lanes] = (stem_ref[here, lanes] + mixed * gate).astype(BF16)
            up = cot_ref[here, lanes].astype(F32)
            slope = (up * gate * (1.0 + mixed * (1.0 - gate))).astype(BF16)
            slope_ref[here, lanes] = slope
            wide = slope.astype(F32)
            for k in range(5):
                product = (wide * window[k]).reshape(rows // 8, 8, LANES)
                sums[k] = sums[k] + jnp.sum(product, axis=0) * mask_ref[5 * g + k]
            window = window[1:]
        part_ref[0:1, lanes] = jnp.zeros((1, LANES), F32)
        for k in range(5):
            part_ref[1 + k : 2 + k, lanes] = jnp.sum(sums[k], axis=0, keepdims=True)
        part_ref[6:8, lanes] = jnp.zeros((2, LANES), F32)
        return carry

    lax.fori_loop(0, feat_ref.shape[1] // LANES, one, 0)


def column_call(kernel, scalars, arrays, out_rows, block):
    channels = arrays[0].shape[1]

    def spec(count):
        return pl.BlockSpec((count, block), lambda j, *_: (0, j))

    return pl.pallas_call(
        kernel,
        grid_spec=pltpu.PrefetchScalarGridSpec(
            num_scalar_prefetch=1,
            grid=(channels // block,),
            in_specs=[spec(a.shape[0]) for a in arrays],
            out_specs=[spec(count) for count, _ in out_rows],
        ),
        out_shape=[jax.ShapeDtypeStruct((count, channels), kind) for count, kind in out_rows],
        compiler_params=kernel_params(),
    )(scalars, *arrays)


def backward_kernel(
    mask_ref,
    core_ref,
    slope_ref,
    low_ref,
    high_ref,
    stem_ref,
    inv_ref,
    cot_ref,
    chan_ref,
    give_ref,
    keep_ref,
    part_ref,
    gated,
    row_sums,
    *,
    slots,
    rows,
    channels,
):
    phase, j = pl.program_id(0), pl.program_id(1)
    blocks = pl.num_programs(1)
    block = stem_ref.shape[1]

    @pl.when(phase == 0)
    def _():
        @pl.when(j == 0)
        def _():
            row_sums[...] = jnp.zeros_like(row_sums)

        def one(t, carry):
            lanes = pl.ds(pl.multiple_of(t * LANES, LANES), LANES)
            taps = [chan_ref[5 - k : 6 - k, lanes] for k in range(5)]
            gain = chan_ref[0:1, lanes]

            def slot(i):
                if i < 2:
                    return low_ref[i * rows : (i + 1) * rows, lanes].astype(F32)
                if i < slots + 2:
                    return slope_ref[(i - 2) * rows : (i - 1) * rows, lanes].astype(F32)
                first = (i - slots - 2) * rows
                return high_ref[first : first + rows, lanes].astype(F32)

            window = [slot(i) for i in range(4)]
            total = jnp.zeros((8, LANES), F32)
            for g in range(slots):
                window.append(slot(g + 4))
                here = slice(g * rows, (g + 1) * rows)
                d_normed = mixed_at(window, taps, mask_ref, g)
                unit = stem_ref[here, lanes] * inv_ref[here, :]
                product = d_normed * unit
                total = total + jnp.sum(product.reshape(rows // 8, 8, LANES), axis=0)
                gated[j, here, lanes] = d_normed * gain
                row_sums[here, :] = row_sums[here, :] + product * gain
                window = window[1:]
            part_ref[0:1, lanes] = jnp.sum(total, axis=0, keepdims=True)
            return carry

        lax.fori_loop(0, block // LANES, one, 0)
        part_ref[1:8, :] = jnp.zeros((7, block), F32)

    @pl.when(phase == 1)
    def _():
        @pl.when(j == 0)
        def _():
            mean = jnp.sum(row_sums[...], axis=1, keepdims=True) / channels
            row_sums[...] = jnp.broadcast_to(mean, row_sums.shape)

        def fill(out_ref):
            def one(t, carry):
                lanes = pl.ds(pl.multiple_of(t * LANES, LANES), LANES)
                inv = inv_ref[...]
                unit = stem_ref[:, lanes] * inv
                d_stem = cot_ref[:, lanes].astype(F32) + inv * (
                    gated[j, :, lanes] - unit * row_sums[...]
                )
                out_ref[:, lanes] = d_stem.astype(BF16)
                return carry

            lax.fori_loop(0, block // LANES, one, 0)

        @pl.when(j < blocks // 2)
        def _():
            fill(give_ref)

        @pl.when(j >= blocks // 2)
        def _():
            fill(keep_ref)


def backward(mask, core, slope, low, high, stem_out, inv, cot, chan, slots, blocks):
    tokens, channels = slope.shape
    block = channels // blocks
    half = blocks // 2

    def column(phase, j, mask_ref, core_ref):
        return (j + (1 - core_ref[0]) * half) % blocks

    def always(count):
        return pl.BlockSpec((count, block), lambda p, j, m, c: (0, column(p, j, m, c)))

    def first(count):
        return pl.BlockSpec(
            (count, block), lambda p, j, m, c: (0, column(p, jnp.where(p == 0, j, blocks - 1), m, c))
        )

    def second(count):
        return pl.BlockSpec(
            (count, block), lambda p, j, m, c: (0, column(p, jnp.where(p == 0, 0, j), m, c))
        )

    fixed = pl.BlockSpec((tokens, LANES), lambda p, j, m, c: (0, 0))
    return pl.pallas_call(
        functools.partial(
            backward_kernel, slots=slots, rows=tokens // slots, channels=channels
        ),
        grid_spec=pltpu.PrefetchScalarGridSpec(
            num_scalar_prefetch=2,
            grid=(2, blocks),
            in_specs=[
                first(tokens),
                first(low.shape[0]),
                first(high.shape[0]),
                always(tokens),
                fixed,
                second(tokens),
                first(8),
            ],
            out_specs=[
                pl.BlockSpec(
                    (tokens, block),
                    lambda p, j, m, c: (0, jnp.where(p == 0, 0, jnp.minimum(j, half - 1))),
                ),
                pl.BlockSpec(
                    (tokens, block),
                    lambda p, j, m, c: (0, jnp.where(p == 0, 0, jnp.maximum(j - half, 0))),
                ),
                first(8),
            ],
            scratch_shapes=[
                pltpu.VMEM((blocks, tokens, block), F32),
                pltpu.VMEM((tokens, LANES), F32),
            ],
        ),
        out_shape=[
            jax.ShapeDtypeStruct((tokens, channels // 2), BF16),
            jax.ShapeDtypeStruct((tokens, channels // 2), BF16),
            jax.ShapeDtypeStruct((8, channels), F32),
        ],
        compiler_params=kernel_params(),
    )(mask, core, slope, low, high, stem_out, inv, cot, chan)


def pixel_kernel(place_ref, keep_ref, give_ref, *refs, chips, width):
    shard_refs = refs[: 2 * chips]
    out_ref, weights, sems = refs[2 * chips :]
    core = place_ref[chips]
    half = keep_ref.shape[1]
    load_weights(place_ref, shard_refs, weights, sems)
    for f in range(2 * chips):
        wait_weights(shard_refs[0], weights, sems, f)
    own = pl.multiple_of(core * half, LANES)
    other = pl.multiple_of((1 - core) * half, LANES)
    tile = 256

    def product(lanes):
        return jnp.dot(
            keep_ref[...], weights[pl.ds(own, half), lanes], preferred_element_type=F32
        ) + jnp.dot(give_ref[...], weights[pl.ds(other, half), lanes], preferred_element_type=F32)

    def one(j, carry):
        lanes = pl.ds(pl.multiple_of(j * tile, tile), tile)
        out_ref[:, lanes] = product(lanes).astype(BF16)
        return carry

    full = width // tile
    lax.fori_loop(0, full, one, 0)
    last = round_up(width - full * tile, LANES)
    rest = product(slice(full * tile, full * tile + last))
    out_ref[:, full * tile :] = rest[:, : width - full * tile].astype(BF16)


def pixel_grads(keep, give, shards, places, width):
    tokens, half = keep.shape
    chips = len(shards) // 2
    padded = shards[0].shape[1]
    return pl.pallas_call(
        functools.partial(pixel_kernel, chips=chips, width=width),
        grid_spec=pltpu.PrefetchScalarGridSpec(
            num_scalar_prefetch=1,
            grid=(),
            in_specs=[pl.BlockSpec(memory_space=pltpu.VMEM)] * 2
            + [pl.BlockSpec(memory_space=pl.ANY)] * len(shards),
            out_specs=pl.BlockSpec(memory_space=pltpu.VMEM),
            scratch_shapes=[
                pltpu.VMEM((2 * half, padded), BF16),
                pltpu.SemaphoreType.DMA((2 * chips,)),
            ],
        ),
        out_shape=jax.ShapeDtypeStruct((tokens, width), BF16),
        compiler_params=kernel_params(),
    )(places, keep, give, *shards)


def weight_kernel(packed_ref, packed_other_ref, keep_ref, got_ref, out_ref):
    groups, height, group = out_ref.shape
    tile = 256
    for m in range(0, height, tile):
        count = min(tile, height - m)
        lanes = slice(m, m + round_up(count, LANES))
        mine = packed_ref[:, lanes].T
        theirs = packed_other_ref[:, lanes].T
        for g in range(groups):
            columns = slice(g * group, (g + 1) * group)
            total = jnp.dot(mine, keep_ref[:, columns], preferred_element_type=F32) + jnp.dot(
                theirs, got_ref[:, columns], preferred_element_type=F32
            )
            out_ref[g, m : m + count, :] = total[:count].astype(BF16)


def weight_partial(packed, packed_other, keep, got, groups, height):
    half = keep.shape[1]
    return pl.pallas_call(
        weight_kernel,
        in_specs=[pl.BlockSpec(memory_space=pltpu.VMEM)] * 4,
        out_specs=pl.BlockSpec(memory_space=pltpu.VMEM),
        out_shape=jax.ShapeDtypeStruct((groups, height, half // groups), BF16),
        compiler_params=kernel_params(),
    )(packed, packed_other, keep, got)


def wide_sum(a, b):
    return a.astype(F32) + b.astype(F32)


def halved(value, axis, bit_set, seq_bits, fsdp_bits):
    keep = lax.dynamic_index_in_dim(value, bit_set, axis, keepdims=False)
    give = lax.dynamic_index_in_dim(value, 1 - bit_set, axis, keepdims=False)
    return wide_sum(keep, swapped(give, seq_bits, fsdp_bits)).astype(BF16)


def scatter_weight(partial, seq_index, chip, core, chips, seq_size, scale):
    groups, height, group = partial.shape
    seq_bits = bits_of(seq_size)
    reduced = []
    for g in range(groups):
        order = seq_bits[::-1] if g % 2 == 0 else seq_bits
        left = list(seq_bits[::-1])
        value = partial[g].reshape((2,) * len(seq_bits) + (height // seq_size, group))
        for bit in order:
            axis = left.index(bit)
            left.pop(axis)
            value = halved(value, axis, (seq_index & bit) // bit, bit, 0)
        reduced.append(value)
    value = jnp.stack(reduced, axis=0)
    low_bits = bits_of(chips)[:-1]
    for bit in low_bits:
        count = value.shape[0]
        value = value.reshape((count // 2, 2) + value.shape[1:])
        value = halved(value, 1, (chip & bit) // bit, 0, 2 * bit)
    value = value[0]
    top = chips // 2
    arrived = sent(
        value, lambda s, f: (s, f ^ (2 * top)) if (f // 2) // top != f % 2 else None
    )
    total = (wide_sum(value, arrived) * scale).astype(BF16)
    shard = group // 2
    mine = lax.dynamic_slice_in_dim(total, core * shard, shard, axis=1)
    other = lax.dynamic_slice_in_dim(total, (1 - core) * shard, shard, axis=1)
    from_core = swapped(other, 0, 1)
    return jnp.where(chip // top == core, mine, from_core)


def shards(patches, send_slot, segments, stem_weight, norm_gain, conv_kernel, cotangent):
    seq_size, fsdp_size = lax.axis_size("seq"), lax.axis_size("fsdp")
    seq_index, fsdp_index = lax.axis_index("seq"), lax.axis_index("fsdp")
    chips, chip, core = fsdp_size // 2, fsdp_index // 2, fsdp_index % 2
    slots = send_slot.shape[1]
    tokens, width = patches.shape[1], patches.shape[2]
    rows = tokens // slots
    edge = 2 * rows
    shard = stem_weight.shape[0]
    channels = shard * fsdp_size
    padded = round_up(width + 6, LANES)
    cot = cotangent[0]

    own = jnp.concatenate(
        [
            stem_weight,
            norm_gain[:, None],
            conv_kernel.T,
            jnp.zeros((shard, padded - width - 6), BF16),
        ],
        axis=1,
    )
    lane_shards, chip_of = gather_weights(own, seq_index, chip, chips, seq_size)
    all_shards = []
    for piece in lane_shards:
        all_shards += [piece, swapped(piece, 0, 1)]
    places = jnp.stack(chip_of + [core]).astype(jnp.int32)

    packed = pack_slots(
        patches[0].reshape(slots, rows, width), send_slot[0], seq_index, seq_size, padded
    ).reshape(tokens, padded)
    packed_other = swapped(packed, 0, 1)

    def following(s, f):
        return (s + 1, f) if s + 1 < seq_size else None

    def preceding(s, f):
        return (s - 1, f) if s > 0 else None

    packed_low = sent(packed[tokens - edge :], following)
    packed_high = sent(packed[:edge], preceding)
    normed, inv, chan, stem_out = stem(
        packed, packed_low, packed_high, all_shards, places, channels
    )

    ids = segments[0]
    total_slots = ids.shape[0]
    centre = seq_index * slots + jnp.arange(slots, dtype=jnp.int32)
    near = centre[:, None] + jnp.arange(-2, 3, dtype=jnp.int32)[None, :]
    inside = (near >= 0) & (near < total_slots)
    same = ids[jnp.clip(near, 0, total_slots - 1)] == ids[centre][:, None]
    mask = (inside & same).astype(F32).reshape(-1)

    (slope_edge,) = column_call(
        functools.partial(edge_kernel, slots=slots, rows=rows),
        mask,
        [normed, cot, chan],
        [(4 * rows, BF16)],
        512,
    )
    slope_low = sent(slope_edge[edge:], following)
    slope_high = sent(slope_edge[:edge], preceding)
    features, slope, kernel_part = column_call(
        functools.partial(forward_kernel, slots=slots, rows=rows),
        mask,
        [normed, stem_out, cot, chan],
        [(tokens, BF16), (tokens, BF16), (8, F32)],
        512,
    )
    give, keep, gain_part = backward(
        mask,
        core.astype(jnp.int32).reshape(1),
        slope,
        slope_low,
        slope_high,
        stem_out,
        inv,
        cot,
        chan,
        slots,
        4,
    )
    got = swapped(give, 0, 1)
    height = round_up(width, 64)
    partial = weight_partial(packed, packed_other, keep, got, chips // 2, height)
    grad_rows = pixel_grads(keep, give, all_shards, places, width)

    scale = 1.0 / math.sqrt(tokens * seq_size * fsdp_size)
    rows_mine = scatter_weight(partial, seq_index, chip, core, chips, seq_size, scale)
    pieces = [rows_mine] + [swapped(rows_mine, o, 0) for o in range(1, seq_size)]
    grad_weight = by_position(pieces, seq_index).reshape(height, shard)[:width].T

    chan_sum = kernel_part + gain_part
    for bit in bits_of(fsdp_size):
        chan_sum = chan_sum + swapped(chan_sum, 0, bit)
    for bit in bits_of(seq_size):
        chan_sum = chan_sum + swapped(chan_sum, bit, 0)
    grad_channels = (
        lax.dynamic_slice_in_dim(chan_sum, fsdp_index * shard, shard, axis=1)[:6] * scale
    )
    return (features[None], grad_rows[None], grad_weight, grad_channels)


def solution(mesh):
    in_specs = (
        P("fsdp", "seq", None),
        P("fsdp", "seq"),
        P("fsdp", None),
        P("fsdp", None),
        P("fsdp"),
        P(None, "fsdp"),
        P("fsdp", "seq", None),
    )
    out_specs = (P("fsdp", "seq", None), P("fsdp", "seq", None), P("fsdp", None), P(None, "fsdp"))
    return jax.shard_map(shards, mesh=mesh, in_specs=in_specs, out_specs=out_specs, check_vma=False)
```

```python
import functools
import math

import jax
import jax.numpy as jnp
from jax import lax
from jax.experimental import pallas as pl
from jax.experimental.pallas import tpu as pltpu
from jax.sharding import PartitionSpec as P

EPSILON = 1e-06
BF16 = jnp.bfloat16
F32 = jnp.float32
LANES = 128
AXES = ("seq", "fsdp")
VMEM_BYTES = 60 * 1024 * 1024


def round_up(value, unit):
    return (value + unit - 1) // unit * unit


def kernel_params(**more):
    return pltpu.CompilerParams(vmem_limit_bytes=VMEM_BYTES, **more)


def sent(value, route):
    seq_size, fsdp_size = lax.axis_size("seq"), lax.axis_size("fsdp")
    pairs = []
    for s in range(seq_size):
        for f in range(fsdp_size):
            target = route(s, f)
            if target is not None:
                pairs.append((s * fsdp_size + f, target[0] * fsdp_size + target[1]))
    return lax.ppermute(value, AXES, pairs)


def swapped(value, seq_bits, fsdp_bits):
    return sent(value, lambda s, f: (s ^ seq_bits, f ^ fsdp_bits))


def together(*values):
    flat, tree = jax.tree.flatten(values)
    return jax.tree.unflatten(tree, lax.optimization_barrier(tuple(flat)))


def bits_of(size):
    return [1 << i for i in range(size.bit_length() - 1)]


def by_position(pieces, me):
    stack = jnp.stack(pieces, axis=0)
    count = len(pieces)
    tail = stack.shape[1:]
    for bit in bits_of(count):
        view = stack.reshape((count // (2 * bit), 2, bit) + tail)
        flipped = jnp.concatenate([view[:, 1:], view[:, :1]], axis=1)
        stack = jnp.where((me & bit) != 0, flipped, view).reshape((count,) + tail)
    return stack


def outbox_kernel(order_ref, spot_ref, frames_ref, *out_refs):
    rows, width = frames_ref.shape[1:]
    for peer, out in enumerate(out_refs):
        capacity, _, padded = out.shape
        lane = lax.broadcasted_iota(jnp.int32, (rows, LANES), 1) + (padded - LANES)
        for k in range(capacity):
            spot = spot_ref[peer * capacity + k]
            out[k, :, padded - LANES :] = jnp.where(lane == width, spot, 0.0).astype(BF16)
            out[k, :, :width] = frames_ref[order_ref[peer * capacity + k]]


def place_kernel(pick_ref, frames_ref, *refs):
    inbox, out = refs[:-1], refs[-1]
    slots, rows, width = frames_ref.shape
    total, padded = out.shape
    tokens = slots * rows
    capacity = inbox[0].shape[0]
    out[:tokens, padded - LANES :] = jnp.zeros((tokens, LANES), out.dtype)
    row = lax.broadcasted_iota(jnp.int32, (total - tokens, padded), 0)
    column = lax.broadcasted_iota(jnp.int32, (total - tokens, padded), 1)
    out[tokens:, :] = jnp.where((column == row + width) & (row < 6), 1.0, 0.0).astype(BF16)

    def one(p, carry):
        index = pick_ref[p]
        here = pl.ds(pl.multiple_of(p * rows, 16), rows)

        @pl.when(index < slots)
        def _():
            out[here, :width] = frames_ref[index]

        for peer, box in enumerate(inbox):
            first = slots + peer * capacity

            @pl.when((index >= first) & (index < first + capacity))
            def _():
                out[here, :width] = box[index - first, :, :width]

        return carry

    lax.fori_loop(0, slots, one, 0)


def scalar_call(kernel, out_shape, scalars, arrays):
    return pl.pallas_call(
        kernel,
        grid_spec=pltpu.PrefetchScalarGridSpec(
            num_scalar_prefetch=len(scalars),
            grid=(),
            in_specs=[pl.BlockSpec(memory_space=pltpu.VMEM)] * len(arrays),
            out_specs=jax.tree.map(lambda _: pl.BlockSpec(memory_space=pltpu.VMEM), out_shape),
        ),
        out_shape=out_shape,
        compiler_params=kernel_params(),
    )(*scalars, *arrays)


def outgoing(frames, destination, seq_index, seq_size, padded):
    slots, rows, _ = frames.shape
    capacity = 2 * slots // seq_size
    owner = (destination // slots) ^ seq_index
    rank = jnp.sum(
        ((owner[:, None] == owner[None, :]) & (destination[None, :] < destination[:, None])).astype(
            jnp.int32
        ),
        axis=1,
    )
    peers = jnp.arange(1, seq_size, dtype=jnp.int32)
    places = jnp.arange(capacity, dtype=jnp.int32)
    hit = (owner[None, None, :] == peers[:, None, None]) & (
        rank[None, None, :] == places[None, :, None]
    )
    order = jnp.sum(jnp.where(hit, jnp.arange(slots, dtype=jnp.int32), 0), axis=2).reshape(-1)
    spot = jnp.sum(jnp.where(hit, destination % slots + 1, 0), axis=2).reshape(-1) - 1
    return scalar_call(
        outbox_kernel,
        [jax.ShapeDtypeStruct((capacity, rows, padded), BF16)] * (seq_size - 1),
        [order, spot.astype(F32)],
        [frames],
    )


def arrivals(destination, spots, seq_index):
    slots = destination.shape[0]
    numbers = jnp.arange(slots, dtype=jnp.int32)
    local = (destination == seq_index * slots + numbers[:, None]).astype(jnp.int32)
    boxed = (spots.astype(jnp.int32).reshape(-1) == numbers[:, None]).astype(jnp.int32)
    places = slots + jnp.arange(boxed.shape[1], dtype=jnp.int32)
    return jnp.sum(local * numbers, axis=1) + jnp.sum(boxed * places, axis=1)


def chain_step(rising, falling, k, chips):
    return (
        sent(rising, lambda s, f: (s, f + 2) if k - 1 <= f // 2 < chips - 1 else None),
        sent(falling, lambda s, f: (s, f - 2) if 0 < f // 2 <= chips - k else None),
    )


def chain_slot(rising, falling, k, chip, chips):
    low = chip < chips // 2
    far = jnp.maximum(chip, chips - 1 - chip)
    towards = jnp.where(low, 1, -1)
    options = [falling[k], rising[k]]
    which = jnp.where(low, 0, 1)
    origin = chip + towards * k
    for reach in range(chips // 2, k):
        which = jnp.where(far == reach, len(options) + jnp.where(low, 1, 0), which)
        options += [falling[k - reach], rising[k - reach]]
        origin = jnp.where(far == reach, chip - towards * (k - reach), origin)
    return options, which, origin


def chosen(options, which):
    value = options[0]
    for i, option in enumerate(options[1:], 1):
        value = jnp.where(which == i, option, value)
    return value


def load_weights(place_ref, shard_refs, weights, sems, by_chip):
    pairs = len(shard_refs) // 2
    shard = shard_refs[0].shape[0]
    core = place_ref[0]
    for k in range(pairs):
        for h in range(2):
            lane = core if h == 0 else 1 - core
            row = 2 * (place_ref[1 + k] if by_chip else k) + lane
            first = pl.multiple_of(row * shard, 16)
            pltpu.make_async_copy(
                shard_refs[2 * k + h], weights.at[pl.ds(first, shard), :], sems.at[row]
            ).start()


def wait_weights(shard_ref, weights, sems, pair):
    shard = shard_ref.shape[0]
    for row in (2 * pair, 2 * pair + 1):
        pltpu.make_async_copy(
            shard_ref, weights.at[pl.ds(row * shard, shard), :], sems.at[row]
        ).wait()


def pair_product(inputs, weights, first, count, store, squares):
    total = squares[...]
    for begin in range(0, count, 256):
        size = min(256, count - begin)
        result = lax.dot_general(
            inputs[...],
            weights[first + begin : first + begin + size, :],
            (((1,), (1,)), ((), ())),
            preferred_element_type=F32,
        )
        store(begin, size, result)
        for t in range(0, size, LANES):
            part = result[:, t : t + LANES]
            total = total + part * part
    squares[...] = total


def early_kernel(place_ref, *refs, count, pairs):
    row_refs, shard_refs = refs[:count], refs[count : count + 2 * pairs]
    acc_ref, squares, weights, rows_all, sems = refs[count + 2 * pairs :]
    group = acc_ref.shape[2]
    load_weights(place_ref, shard_refs, weights, sems, False)
    begin = 0
    for ref in row_refs:
        rows_all[begin : begin + ref.shape[0]] = ref[...]
        begin += ref.shape[0]
    squares[...] = jnp.zeros_like(squares)
    for k in range(pairs):
        wait_weights(shard_refs[0], weights, sems, k)

        def store(begin, size, result, k=k):
            acc_ref[k, :, begin : begin + size] = result

        pair_product(rows_all, weights, k * group, group, store, squares)


VMEM_SPEC = pl.BlockSpec(memory_space=pltpu.VMEM)
ANY_SPEC = pl.BlockSpec(memory_space=pl.ANY)


def stem_early(row_arrays, shards, core_id):
    padded = row_arrays[0].shape[1]
    rows = sum(a.shape[0] for a in row_arrays)
    pairs = len(shards) // 2
    group = 2 * shards[0].shape[0]
    return pl.pallas_call(
        functools.partial(early_kernel, count=len(row_arrays), pairs=pairs),
        grid_spec=pltpu.PrefetchScalarGridSpec(
            num_scalar_prefetch=1,
            grid=(),
            in_specs=[VMEM_SPEC] * len(row_arrays) + [ANY_SPEC] * len(shards),
            out_specs=[VMEM_SPEC] * 2,
            scratch_shapes=[
                pltpu.VMEM((pairs * group, padded), BF16),
                pltpu.VMEM((rows, padded), BF16),
                pltpu.SemaphoreType.DMA((2 * pairs,)),
            ],
        ),
        out_shape=[
            jax.ShapeDtypeStruct((pairs, rows, group), F32),
            jax.ShapeDtypeStruct((rows, LANES), F32),
        ],
        compiler_params=kernel_params(),
    )(core_id, *row_arrays, *shards)


def gate_of(value):
    return 0.5 * jnp.tanh(0.5 * value) + 0.5


def mixed_at(window, taps, mask_ref, first):
    total = window[0] * (taps[0] * mask_ref[first])
    for k in range(1, 5):
        total = total + window[k] * (taps[k] * mask_ref[first + k])
    return total


def layer_kernel(
    place_ref, mask_ref, main_ref, low_ref, high_ref, cot_ref, cot_low_ref, cot_high_ref, *refs,
    pairs, late, slots, channels
):
    shard_refs, refs = refs[: 2 * late], refs[2 * late :]
    if pairs:
        early_main, early_halo, main_squares, halo_squares = refs[:4]
        refs = refs[4:]
    part_ref, feat_ref, stem_ref, give_ref, keep_ref = refs[:5]
    weights, rows_all, acc, cots, feats, d_stem, lanes_of_core, gated, slopes, squares, inverse = refs[5:16]
    sems, in_sems, cot_sems, out_sems = refs[16:]
    group = 2 * shard_refs[0].shape[0]
    tokens = cot_ref.shape[0]
    rows = tokens // slots
    halo, edge = low_ref.shape[0], cot_low_ref.shape[0]
    extra = main_ref.shape[0] - tokens
    body = tokens + 2 * halo
    core = place_ref[0]
    load_weights(place_ref, shard_refs, weights, sems, not pairs)
    loads = [
        pltpu.make_async_copy(cot_low_ref, cots.at[pl.ds(0, edge), :], cot_sems.at[0]),
        pltpu.make_async_copy(cot_ref, cots.at[pl.ds(edge, tokens), :], cot_sems.at[1]),
        pltpu.make_async_copy(cot_high_ref, cots.at[pl.ds(edge + tokens, edge), :], cot_sems.at[2]),
    ]
    if pairs:
        for k in range(pairs):
            lanes = pl.ds(pl.multiple_of(place_ref[1 + k] * group, LANES), group)
            for i, (ref, src, dst, size) in enumerate(
                (
                    (early_main, 0, halo, tokens),
                    (early_main, tokens, body, extra),
                    (early_halo, 0, 0, halo),
                    (early_halo, halo, halo + tokens, halo),
                )
            ):
                loads.append(
                    pltpu.make_async_copy(
                        ref.at[k, pl.ds(src, size), :],
                        acc.at[pl.ds(dst, size), lanes],
                        in_sems.at[k, i],
                    )
                )
    for copy in loads:
        copy.start()
    rows_all[0:halo] = low_ref[...]
    rows_all[halo : halo + tokens] = main_ref[0:tokens]
    rows_all[halo + tokens : body] = high_ref[...]
    rows_all[body : body + extra] = main_ref[tokens:]
    if pairs:
        squares[0:halo] = halo_squares[0:halo]
        squares[halo : halo + tokens] = main_squares[0:tokens]
        squares[halo + tokens : body] = halo_squares[halo:]
        squares[body:] = main_squares[tokens:]
        wait_weights(shard_refs[0], weights, sems, 0)

        def store(begin, size, result):
            first = pl.multiple_of(place_ref[1 + pairs] * group + begin, LANES)
            acc[:, pl.ds(first, size)] = result

        pair_product(rows_all, weights, 0, group, store, squares)
    else:
        squares[...] = jnp.zeros_like(squares)
        for z in range(late):
            wait_weights(shard_refs[0], weights, sems, z)
        tile = 256

        def one(j, carry):
            first = pl.multiple_of(j * tile, tile)
            result = lax.dot_general(
                rows_all[...],
                weights[pl.ds(first, tile), :],
                (((1,), (1,)), ((), ())),
                preferred_element_type=F32,
            )
            acc[:, pl.ds(first, tile)] = result
            total = squares[...]
            for t in range(0, tile, LANES):
                total = total + result[:, t : t + LANES] * result[:, t : t + LANES]
            squares[...] = total
            return carry

        lax.fori_loop(0, channels // tile, one, 0)
    mean = jnp.sum(squares[...], axis=1, keepdims=True) / channels
    inverse[...] = jnp.broadcast_to(lax.rsqrt(mean + EPSILON), inverse.shape)
    squares[...] = jnp.zeros_like(squares)
    for copy in loads:
        copy.wait()

    def columns(t, carry):
        lanes = pl.ds(pl.multiple_of(t * LANES, LANES), LANES)
        gain = acc[body : body + 1, lanes]
        taps = [acc[body + 1 + k : body + 2 + k, lanes] for k in range(5)]

        def normed(i):
            here = slice(i * rows, (i + 1) * rows)
            return (acc[here, lanes] * inverse[here] * gain).astype(BF16).astype(F32)

        window = [normed(i) for i in range(4)]
        sums = [jnp.zeros((8, LANES), F32) for _ in range(5)]
        for i in range(slots + 4):
            window.append(normed(i + 4))
            mixed = mixed_at(window, taps, mask_ref, 5 * i)
            gate = gate_of(mixed)
            smooth = mixed * gate
            here = slice(i * rows, (i + 1) * rows)
            up = cots[here, lanes].astype(F32)
            slope = (up * (gate + smooth - smooth * gate)).astype(BF16).astype(F32)
            slopes[here] = slope
            if 2 <= i < slots + 2:
                own = slice((i - 2) * rows, (i - 1) * rows)
                stem = acc[halo + (i - 2) * rows : halo + (i - 1) * rows, lanes]
                feats[own, lanes] = (stem + smooth).astype(BF16)
                for k in range(5):
                    product = (slope * window[k]).reshape(rows // 8, 8, LANES)
                    sums[k] = sums[k] + jnp.sum(product, axis=0) * mask_ref[5 * i + k]
            window = window[1:]
        for k in range(5):
            part_ref[1 + k : 2 + k, lanes] = jnp.sum(sums[k], axis=0, keepdims=True)
        part_ref[6:8, lanes] = jnp.zeros((2, LANES), F32)
        total = jnp.zeros((8, LANES), F32)
        for p in range(slots):
            window = [slopes[(p + o) * rows : (p + o + 1) * rows] for o in range(5)]
            own = slice(p * rows, (p + 1) * rows)
            here = slice(halo + p * rows, halo + (p + 1) * rows)
            d_normed = mixed_at(window, taps[::-1], mask_ref, 5 * (p + 2))
            product = d_normed * (acc[here, lanes] * inverse[here])
            total = total + jnp.sum(product.reshape(rows // 8, 8, LANES), axis=0)
            gated[own, lanes] = d_normed * gain
            squares[own] = squares[own] + product * gain
        part_ref[0:1, lanes] = jnp.sum(total, axis=0, keepdims=True)
        return carry

    copies = []
    parts = 4
    size = channels // parts
    for i in range(parts):
        lax.fori_loop(i * size // LANES, (i + 1) * size // LANES, columns, 0)
        lanes = pl.ds(i * size, size)
        copy = pltpu.make_async_copy(feats.at[:, lanes], feat_ref.at[:, lanes], out_sems.at[i])
        copy.start()
        copies.append(copy)
    mean = jnp.sum(squares[0:tokens], axis=1, keepdims=True) / channels
    squares[0:tokens] = jnp.broadcast_to(mean, (tokens, LANES))

    def finish_columns(t, carry):
        lanes = pl.ds(pl.multiple_of(t * LANES, LANES), LANES)
        inv = inverse[halo : halo + tokens]
        unit = acc[halo : halo + tokens, lanes] * inv
        value = cots[edge : edge + tokens, lanes].astype(F32) + inv * (
            gated[:, lanes] - unit * squares[0:tokens]
        )
        d_stem[:, lanes] = value.astype(BF16)
        return carry

    lax.fori_loop(0, channels // LANES, finish_columns, 0)
    copies.append(pltpu.make_async_copy(d_stem, stem_ref, out_sems.at[parts]))
    copies[-1].start()
    shard = group // 2
    room = lanes_of_core.shape[2] // (channels // group)
    for f in range(channels // shard):
        first = f // 2 * room
        lanes_of_core[f % 2, :, first : first + shard] = d_stem[:, f * shard : (f + 1) * shard]
        if room > shard:
            lanes_of_core[f % 2, :, first + shard : first + room] = jnp.zeros(
                (tokens, room - shard), BF16
            )
    for h, ref in enumerate((keep_ref, give_ref)):
        copy = pltpu.make_async_copy(
            lanes_of_core.at[(core + h) % 2], ref, out_sems.at[parts + 1 + h]
        )
        copy.start()
        copies.append(copy)
    for copy in copies:
        copy.wait()


def layer(main, low, high, cot, cot_low, cot_high, shards, early, places, mask, slots, channels):
    tokens = cot.shape[0]
    padded = main.shape[1]
    halo, edge = low.shape[0], cot_low.shape[0]
    total = main.shape[0] + 2 * halo
    late = len(shards) // 2
    pairs = early[0].shape[0] if early else 0
    shard = shards[0].shape[0]
    half = channels // (2 * shard) * round_up(shard, LANES)
    return pl.pallas_call(
        functools.partial(layer_kernel, pairs=pairs, late=late, slots=slots, channels=channels),
        grid_spec=pltpu.PrefetchScalarGridSpec(
            num_scalar_prefetch=2,
            grid=(),
            in_specs=[VMEM_SPEC] * 3
            + [ANY_SPEC] * 3
            + [ANY_SPEC] * len(shards)
            + ([ANY_SPEC] * 2 + [VMEM_SPEC] * 2 if pairs else []),
            out_specs=[VMEM_SPEC] + [ANY_SPEC] * 4,
            scratch_shapes=[
                pltpu.VMEM((late * 2 * shards[0].shape[0], padded), BF16),
                pltpu.VMEM((total, padded), BF16),
                pltpu.VMEM((total, channels), F32),
                pltpu.VMEM((tokens + 2 * edge, channels), BF16),
                pltpu.VMEM((tokens, channels), BF16),
                pltpu.VMEM((tokens, channels), BF16),
                pltpu.VMEM((2, tokens, half), BF16),
                pltpu.VMEM((tokens, channels), F32),
                pltpu.VMEM((tokens + 2 * edge, LANES), F32),
                pltpu.VMEM((total, LANES), F32),
                pltpu.VMEM((total, LANES), F32),
                pltpu.SemaphoreType.DMA((2 * late,)),
                pltpu.SemaphoreType.DMA((max(pairs, 1), 4)),
                pltpu.SemaphoreType.DMA((3,)),
                pltpu.SemaphoreType.DMA((7,)),
            ],
        ),
        out_shape=[
            jax.ShapeDtypeStruct((8, channels), F32),
            jax.ShapeDtypeStruct((tokens, channels), BF16),
            jax.ShapeDtypeStruct((tokens, channels), BF16),
            jax.ShapeDtypeStruct((tokens, half), BF16),
            jax.ShapeDtypeStruct((tokens, half), BF16),
        ],
        compiler_params=kernel_params(),
    )(places, mask, main, low, high, cot, cot_low, cot_high, *shards, *early)


def pixel_kernel(place_ref, d_stem_ref, *refs, chips, begin, tile):
    shard_refs, refs = refs[: 2 * chips], refs[2 * chips :]
    before = refs[0] if begin else None
    out_ref, weights, sems = refs[1:] if begin else refs
    width = out_ref.shape[1] - begin
    lanes = pl.ds(begin, weights.shape[1])
    load_weights(place_ref, [r.at[:, lanes] for r in shard_refs], weights, sems, True)
    for z in range(chips):
        wait_weights(shard_refs[0].at[:, lanes], weights, sems, z)
    if begin:
        out_ref[:, :begin] = before[...]
    for first in range(0, width, tile):
        size = min(tile, width - first)
        columns = slice(first, first + round_up(size, LANES))
        value = jnp.dot(d_stem_ref[...], weights[:, columns], preferred_element_type=F32)
        out_ref[:, begin + first : begin + first + size] = value[:, :size].astype(BF16)


def pixel_grads(d_stem, shards, places, begin, end, before=None):
    tokens, channels = d_stem.shape
    chips = len(shards) // 2
    lanes = round_up(end - begin, LANES)
    return pl.pallas_call(
        functools.partial(pixel_kernel, chips=chips, begin=begin, tile=256),
        grid_spec=pltpu.PrefetchScalarGridSpec(
            num_scalar_prefetch=1,
            grid=(),
            in_specs=[VMEM_SPEC]
            + [ANY_SPEC] * len(shards)
            + ([VMEM_SPEC] if begin else []),
            out_specs=VMEM_SPEC,
            scratch_shapes=[
                pltpu.VMEM((channels, lanes), BF16),
                pltpu.SemaphoreType.DMA((2 * chips,)),
            ],
        ),
        out_shape=jax.ShapeDtypeStruct((tokens, end), BF16),
        compiler_params=kernel_params(),
    )(places, d_stem, *shards, *([before] if begin else []))


def turn_kernel(first_ref, second_ref, out_ref, *, tokens):
    height, depth = out_ref.shape
    out_ref[:, 2 * tokens :] = jnp.zeros((height, depth - 2 * tokens), BF16)
    both = jnp.concatenate([first_ref[:tokens], second_ref[:tokens]], axis=0)
    for m in range(0, first_ref.shape[1], LANES):
        count = min(LANES, height - m)
        if count > 0:
            out_ref[m : m + count, : 2 * tokens] = both[:, m : m + LANES].T[:count]


def turned(packed, packed_other, height, tokens):
    return pl.pallas_call(
        functools.partial(turn_kernel, tokens=tokens),
        in_specs=[VMEM_SPEC] * 2,
        out_specs=VMEM_SPEC,
        out_shape=jax.ShapeDtypeStruct((height, round_up(2 * tokens, LANES)), BF16),
        compiler_params=kernel_params(),
    )(packed, packed_other)


def halves_beside(value, shard):
    rows = value.shape[0] // 2
    return value[:rows, :shard], value[rows:, :shard]


def weight_kernel(where_ref, pixels_ref, keep_ref, got_ref, *refs, bits, share, line_share, shard, give):
    outs, (d_stem, left, line, sems, left_sems) = refs[:3], refs[3:]
    tokens = keep_ref.shape[0]
    seq_index, chip = where_ref[0], where_ref[1]
    seq_size = 2 * outs[0].shape[1]
    half = seq_size // 2
    chips = 2 * outs[0].shape[0]
    room = d_stem.shape[1] // chips
    arrive = [[] for _ in range(chips + 1)]
    for g, bit in enumerate(bits):
        mine = (seq_index // bit) % 2
        wanted = 1 - mine if give else mine
        for i in range(half):
            p = (i // bit) * (2 * bit) + i % bit + bit * wanted
            arrive[g * (chips // 2)].append(
                pltpu.make_async_copy(
                    pixels_ref.at[pl.ds(pl.multiple_of(p * share, 16), share), :],
                    left.at[g, pl.ds(i * share, share), :],
                    left_sems.at[g, i],
                )
            )
        for z in range(g * (chips // 2), (g + 1) * (chips // 2)):
            lanes = pl.ds(z * room, room)
            for h, ref in enumerate((keep_ref, got_ref)):
                arrive[z].append(
                    pltpu.make_async_copy(
                        ref.at[:, lanes],
                        d_stem.at[pl.ds(h * tokens, tokens), lanes],
                        sems.at[2 * z + h],
                    )
                )
    arrive[chips].append(
        pltpu.make_async_copy(
            pixels_ref.at[pl.ds(seq_size * share, line.shape[0]), :], line, sems.at[2 * chips]
        )
    )
    for copy in sum(arrive, []):
        copy.start()
    extra = d_stem.shape[0] - 2 * tokens
    d_stem[2 * tokens :, :] = jnp.zeros((extra, d_stem.shape[1]), BF16)

    def fill(out, value, count, rows):
        for i in range(count):
            low, high = halves_beside(value[i * rows : (i + 1) * rows], shard)
            out[i, :, :shard] = low.astype(out.dtype)
            out[i, :, shard:] = high.astype(out.dtype)

    for g in range(2):
        for z in range(chips // 2):
            for copy in arrive[g * (chips // 2) + z]:
                copy.wait()
            first = (g * (chips // 2) + z) * room
            value = jnp.dot(
                left[g], d_stem[:, first : first + room], preferred_element_type=F32
            )
            fill(outs[g].at[z], value, half, share)
    for copy in arrive[chips]:
        copy.wait()
    mine = chip % 2
    wanted = 1 - mine if give else mine
    for i in range(chips // 2):
        columns = pl.ds(pl.multiple_of((2 * i + wanted) * room, LANES), room)
        value = jnp.dot(line[...], d_stem[:, columns], preferred_element_type=F32)
        fill(outs[2].at[i], value, seq_size, line_share)


def weight_part(pixels, keep, got, where, chips, seq_size, shard, share, line_share, bits, give):
    half = keep.shape[1]
    height, depth = pixels.shape
    kind = BF16 if give else F32
    plane = jax.ShapeDtypeStruct((chips // 2, seq_size // 2, share // 2, 2 * shard), kind)
    line = jax.ShapeDtypeStruct((chips // 2, seq_size, line_share // 2, 2 * shard), kind)
    return pl.pallas_call(
        functools.partial(
            weight_kernel, bits=bits, share=share, line_share=line_share, shard=shard, give=give
        ),
        grid_spec=pltpu.PrefetchScalarGridSpec(
            num_scalar_prefetch=1,
            grid=(),
            in_specs=[ANY_SPEC] * 3,
            out_specs=[VMEM_SPEC] * 3,
            scratch_shapes=[
                pltpu.VMEM((depth, half), BF16),
                pltpu.VMEM((2, seq_size // 2 * share, depth), BF16),
                pltpu.VMEM((seq_size * line_share, depth), BF16),
                pltpu.SemaphoreType.DMA((2 * chips + 1,)),
                pltpu.SemaphoreType.DMA((2, seq_size // 2)),
            ],
        ),
        out_shape=[plane, plane, line],
        compiler_params=kernel_params(),
    )(where, pixels, keep, got)


def bit_at(index, bit):
    return (index // bit) % 2


def sums_kernel(at_ref, *refs, plan):
    count = sum(n for alternatives, _, _ in plan for n in alternatives)
    ins, outs = list(refs[:count]), list(refs[count:])
    for alternatives, selector, keep in plan:
        totals = []
        for n in alternatives:
            terms, ins = ins[:n], ins[n:]
            total = terms[0][...].astype(F32)
            for term in terms[1:]:
                total = total + term[...].astype(F32)
            totals.append(total)
        if selector is None:
            give = kept = totals[0]
        else:
            upper = at_ref[selector] == 1
            give = jnp.where(upper, totals[0], totals[1])
            kept = jnp.where(upper, totals[1], totals[0])
        out = outs.pop(0)
        out[...] = give.astype(out.dtype)
        if keep:
            outs.pop(0)[...] = kept


def sums(units):
    scalars, arrays, in_specs, outs, plan = [], [], [], [], []

    def scalar(value):
        scalars.append(value)
        return len(scalars) - 1

    def spec(array, places):
        lead = [None if at is not None else array.shape[d] for d, at in enumerate(places)]
        return pl.BlockSpec(
            tuple(lead) + tuple(array.shape[-2:]),
            lambda i, at_ref: tuple(0 if p is None else at_ref[p] for p in places) + (0, 0),
        )

    for alternatives, selector, kind in units:
        for terms in alternatives:
            for array, index in terms:
                places = [None if at is None else scalar(at) for at in index]
                arrays.append(array)
                in_specs.append(spec(array, places))
                shape = tuple(
                    array.shape[d] for d, at in enumerate(index) if at is None
                ) + tuple(array.shape[-2:])
        keep = len(alternatives) > 1
        plan.append(
            ([len(t) for t in alternatives], scalar(selector) if keep else None, keep)
        )
        outs.append(jax.ShapeDtypeStruct(shape, kind))
        if keep:
            outs.append(jax.ShapeDtypeStruct(shape, F32))
    if not scalars:
        scalars = [jnp.int32(0)]

    def whole(shape):
        return pl.BlockSpec(shape, lambda i, at_ref: (0,) * len(shape))

    results = list(
        pl.pallas_call(
            functools.partial(sums_kernel, plan=plan),
            grid_spec=pltpu.PrefetchScalarGridSpec(
                num_scalar_prefetch=1,
                grid=(1,),
                in_specs=in_specs,
                out_specs=[whole(o.shape) for o in outs],
            ),
            out_shape=outs,
            compiler_params=kernel_params(),
        )(jnp.stack([jnp.asarray(s, jnp.int32) for s in scalars]), *arrays)
    )
    return [(results.pop(0), results.pop(0) if keep else None) for _, _, keep in plan]


def at_own(terms, mine, done, label=None):
    return [
        (array, [1 - mine[b] if b == label else mine[b] if b in done else None for b in labels])
        for array, labels in terms
    ]


def split_view(array, labels):
    return array.reshape((2,) * len(labels) + tuple(array.shape[-2:]))


def route_of(label):
    axis, bit = label
    if axis == "seq":
        return lambda s, f: (s ^ bit, f)
    return lambda s, f: (s, f ^ (2 * bit))


def without(labels, done):
    return [label for label in labels if label not in done]


def halving(gives, keeps, labels, orders, mine, last=None):
    came = yield gives, [route_of(order[0]) for order in orders]
    terms = []
    for keep, (arrived, _, _), order in zip(keeps, came, orders):
        rest = without(labels, order[:1])
        terms.append([(split_view(keep, rest), rest), (split_view(arrived, rest), rest)])
    for i in range(1, len(orders[0])):
        units = [
            ([at_own(t, mine, order[:i], order[i])], None, BF16) for t, order in zip(terms, orders)
        ]
        came = yield units, [route_of(order[i]) for order in orders]
        for t, (arrived, _, _), order in zip(terms, came, orders):
            rest = without(labels, order[: i + 1])
            t.append((split_view(arrived, rest), rest))
    final = [at_own(t, mine, order) for t, order in zip(terms, orders)]
    if last is not None:
        ((arrived, kept, _),) = yield [(final, mine[last], BF16)], [route_of(last)]
        final = [[(kept, []), (arrived, [])]]
    yield final[0], None


def all_sum(value, routes):
    ((came, _, give),) = yield [value], routes[:1]
    for route in routes[1:]:
        ((came, _, give),) = yield [([[(give, []), (came, [])]], None, F32)], [route]
    yield (give, came), None


def in_rounds(chains, beside):
    waiting = [next(chain) for chain in chains]
    first, done = True, None
    while any(routes is not None for _, routes in waiting):
        units = [u for values, routes in waiting if routes is not None for u in values]
        routes = [r for _, some in waiting if some is not None for r in some]
        ready = [(value, None) for value in units] if first else sums(units)
        first = False
        came = [sent(give, route) for (give, _), route in zip(ready, routes)]
        if beside:
            if done is not None:
                ready, done = together(ready, done)
            done = beside[0](done)
            beside = beside[1:]
            came, done = together(came, done)
        else:
            (came,) = together(came)
        arrived = [(value, kept, give) for value, (give, kept) in zip(came, ready)]
        for i, (values, some) in enumerate(waiting):
            if some is not None:
                mine, arrived = arrived[: len(values)], arrived[len(values) :]
                waiting[i] = chains[i].send(mine)
    return [values for values, _ in waiting], done


def finish_kernel(at_ref, *refs, counts, scale):
    ins, out_ref = list(refs[:-1]), refs[-1]
    shard = out_ref.shape[1]
    begin = 0
    for n in counts:
        terms, ins = ins[:n], ins[n:]
        total = terms[0][...].astype(F32)
        for term in terms[1:]:
            total = total + term[...].astype(F32)
        total = (total * scale).astype(BF16)
        for part in (total[:, :shard], total[:, shard:]):
            out_ref[begin : begin + part.shape[0], :] = part
            begin += part.shape[0]


def finish(chains, scale):
    scalars, arrays, in_specs, height = [], [], [], 0
    for terms in chains:
        for array, index in terms:
            first = len(scalars)
            scalars += index
            arrays.append(array)
            in_specs.append(
                pl.BlockSpec(
                    (None,) * len(index) + tuple(array.shape[-2:]),
                    lambda i, at_ref, first=first, n=len(index): tuple(
                        at_ref[first + d] for d in range(n)
                    )
                    + (0, 0),
                )
            )
        height += 2 * terms[0][0].shape[-2]
    shard = arrays[0].shape[-1] // 2
    return pl.pallas_call(
        functools.partial(finish_kernel, counts=[len(t) for t in chains], scale=scale),
        grid_spec=pltpu.PrefetchScalarGridSpec(
            num_scalar_prefetch=1,
            grid=(1,),
            in_specs=in_specs,
            out_specs=pl.BlockSpec((height, shard), lambda i, at_ref: (0, 0)),
        ),
        out_shape=jax.ShapeDtypeStruct((height, shard), BF16),
        compiler_params=kernel_params(),
    )(jnp.stack([jnp.asarray(s, jnp.int32) for s in scalars]), *arrays)


def shards(patches, send_slot, segments, stem_weight, norm_gain, conv_kernel, cotangent):
    seq_size, fsdp_size = lax.axis_size("seq"), lax.axis_size("fsdp")
    seq_index, fsdp_index = lax.axis_index("seq"), lax.axis_index("fsdp")
    chips, chip, core = fsdp_size // 2, fsdp_index // 2, fsdp_index % 2
    slots = send_slot.shape[1]
    tokens, width = patches.shape[1], patches.shape[2]
    rows = tokens // slots
    edge = 2 * rows
    shard = stem_weight.shape[0]
    channels = shard * fsdp_size
    padded = round_up(width + 6, LANES)
    capacity = 2 * slots // seq_size
    cot = cotangent[0]
    core_id = core.astype(jnp.int32).reshape(1)

    def following(s, f):
        return (s + 1, f) if s + 1 < seq_size else None

    def preceding(s, f):
        return (s - 1, f) if s > 0 else None

    tail, head = cot[tokens - edge :], cot[:edge]
    own = jnp.concatenate(
        [
            stem_weight,
            norm_gain[:, None],
            conv_kernel.T,
            jnp.zeros((shard, padded - width - 6), BF16),
        ],
        axis=1,
    )
    own, tail, patches = together(own, tail, patches)
    frames = patches[0].reshape(slots, rows, width)
    boxes = outgoing(frames, send_slot[0], seq_index, seq_size, padded)
    rising, falling = {0: own}, {0: own}
    own_core = swapped(own, 0, 1)
    boxes, own_core = together(boxes, own_core)
    inbox = [None] * (seq_size - 1)
    direct = [o for o in range(1, seq_size) if o.bit_count() % 2 == 1]
    others = [o for o in range(1, seq_size) if o.bit_count() % 2 == 0]
    split = 2 * shard % LANES == 0 and chips == 4
    lane_shards, core_shards, chip_of = [own], [own_core], [chip]
    early = []
    spots = [None] * (seq_size - 1)

    def arrive(numbers, boxes):
        for o, box in zip(numbers, boxes):
            inbox[o - 1], spots[o - 1] = box, box[:, 0, width]

    def add_shard(k):
        options, which, origin = chain_slot(rising, falling, k, chip, chips)
        lane_shards.append(chosen(options, which))
        core_shards.append(swapped(lane_shards[-1], 0, 1))
        chip_of.append(origin)

    for k in range(1, chips):
        rising[k], falling[k] = chain_step(rising[k - 1], falling[k - 1], k, chips)
        if k == 1:
            came = [swapped(boxes[o - 1], o, 0) for o in direct]
            rising, falling, came, boxes, tail, head = together(
                rising, falling, came, boxes, tail, head
            )
            arrive(direct, came)
        elif k == 2:
            came = [swapped(boxes[o - 1], o, 0) for o in others]
            cot_low = sent(tail, following)
            if split:
                add_shard(1)
            rising, falling, cot_low, came, core_shards, lane_shards, spots, head = together(
                rising, falling, cot_low, came, core_shards, lane_shards, spots, head
            )
            arrive(others, came)
            cot_high = sent(head, preceding)
            pick = arrivals(send_slot[0], jnp.stack(spots, axis=0), seq_index)
            main = scalar_call(
                place_kernel,
                jax.ShapeDtypeStruct((tokens + 16, padded), BF16),
                [pick],
                [frames] + inbox,
            )
            if split:
                add_shard(2)
                main, lane_shards, core_shards = together(main, lane_shards, core_shards)
            low = sent(main[tokens - 2 * edge : tokens], following)
            high = sent(main[: 2 * edge], preceding)
        elif k == 3 and split:
            pairs = [v for both in zip(lane_shards, core_shards) for v in both]
            early_main, main_squares = stem_early([main], pairs, core_id)
            rising, falling, early_main, low, high, cot_high, main = together(
                rising, falling, early_main, low, high, cot_high, main
            )
        else:
            rising, falling = together(rising, falling)
    for k in range(len(lane_shards), chips):
        add_shard(k)
    height = round_up(width, 64 * seq_size)
    main_other = swapped(main, 0, 1)
    places = jnp.stack([core] + chip_of).astype(jnp.int32)
    all_pairs = [v for both in zip(lane_shards, core_shards) for v in both]
    late_pairs = all_pairs
    if split:
        late_pairs = all_pairs[len(pairs) :]
        early_halo, halo_squares = stem_early([low, high], pairs, core_id)
        early_halo, main_other = together(early_halo, main_other)
        early = [early_main, early_halo, main_squares, halo_squares]

    ids = segments[0]
    total_slots = ids.shape[0]
    centre = seq_index * slots + jnp.arange(-2, slots + 2, dtype=jnp.int32)
    near = centre[:, None] + jnp.arange(-2, 3, dtype=jnp.int32)[None, :]
    inside = (near >= 0) & (near < total_slots) & ((centre >= 0) & (centre < total_slots))[:, None]
    same = (
        ids[jnp.clip(near, 0, total_slots - 1)] == ids[jnp.clip(centre, 0, total_slots - 1)][:, None]
    )
    mask = (inside & same).astype(F32).reshape(-1)
    chan_part, features, d_stem, give, keep = layer(
        main, low, high, cot, cot_low, cot_high, late_pairs, early, places, mask, slots, channels
    )
    chan_part = chan_part + swapped(chan_part, 0, 1)
    got = swapped(give, 0, 1)
    pixels = turned(main, main_other, height, tokens)
    middle = round_up(width // 2, LANES)

    seq_bits = bits_of(seq_size)
    chip_bits = bits_of(chips)
    line_share = height // seq_size // 4 // 32 * 32
    share = height // seq_size - line_share
    where = jnp.stack([seq_index, chip]).astype(jnp.int32)
    first_bits = [seq_bits[0], seq_bits[-1]]
    sizes = (chips, seq_size, shard, share, line_share, first_bits)
    gives = weight_part(pixels, keep, got, where, *sizes, True)
    keeps = weight_part(pixels, keep, got, where, *sizes, False)
    scale = 1.0 / math.sqrt(tokens * seq_size * fsdp_size)
    mine = {("seq", b): bit_at(seq_index, b) for b in seq_bits}
    mine |= {("chip", b): bit_at(chip, b) for b in chip_bits}
    seq_labels = [("seq", b) for b in seq_bits]
    chip_labels = [("chip", b) for b in chip_bits]
    orders = [order + chip_labels[:-1] for order in (seq_labels, seq_labels[::-1])]
    chains = [
        halving(
            gives[:2],
            keeps[:2],
            chip_labels[:-1][::-1] + seq_labels[::-1],
            orders,
            mine,
            chip_labels[-1],
        ),
        halving(
            gives[2:],
            keeps[2:],
            chip_labels[::-1] + seq_labels[::-1],
            [chip_labels + seq_labels],
            mine,
        ),
        all_sum(chan_part, [route_of(label) for label in seq_labels + chip_labels]),
    ]
    (plane, line, chan), grad_rows = in_rounds(
        chains,
        [
            lambda _: pixel_grads(d_stem, all_pairs, places, 0, middle),
            lambda before: pixel_grads(d_stem, all_pairs, places, middle, width, before),
        ],
    )
    rows_mine = finish([plane, line], scale)
    pieces = [rows_mine] + [swapped(rows_mine, o, 0) for o in range(1, seq_size)]
    stack = by_position(pieces, seq_index)
    grad_weight = jnp.concatenate(
        [stack[:, :share].reshape(-1, shard), stack[:, share:].reshape(-1, shard)], axis=0
    )[:width].T
    first = fsdp_index * shard
    grad_channels = scale * (
        lax.dynamic_slice_in_dim(chan[0], first, shard, axis=1)[:6]
        + lax.dynamic_slice_in_dim(chan[1], first, shard, axis=1)[:6]
    )
    return (features[None], grad_rows[None], grad_weight, grad_channels)


def solution(mesh):
    in_specs = (
        P("fsdp", "seq", None),
        P("fsdp", "seq"),
        P("fsdp", None),
        P("fsdp", None),
        P("fsdp"),
        P(None, "fsdp"),
        P("fsdp", "seq", None),
    )
    out_specs = (P("fsdp", "seq", None), P("fsdp", "seq", None), P("fsdp", None), P(None, "fsdp"))
    return jax.shard_map(shards, mesh=mesh, in_specs=in_specs, out_specs=out_specs, check_vma=False)
```

```python
import functools
import math

import jax
import jax.numpy as jnp
from jax import lax
from jax.experimental import pallas as pl
from jax.experimental.pallas import tpu as pltpu
from jax.sharding import PartitionSpec as P

EPSILON = 1e-06
BF16 = jnp.bfloat16
F32 = jnp.float32
LANES = 128
AXES = ("seq", "fsdp")


def round_up(value, unit):
    return (value + unit - 1) // unit * unit


def kernel_params(mebibytes):
    return pltpu.CompilerParams(vmem_limit_bytes=mebibytes * 1024 * 1024)


def sent(value, route):
    seq_size, fsdp_size = lax.axis_size("seq"), lax.axis_size("fsdp")
    pairs = []
    for s in range(seq_size):
        for f in range(fsdp_size):
            target = route(s, f)
            if target is not None:
                pairs.append((s * fsdp_size + f, target[0] * fsdp_size + target[1]))
    return lax.ppermute(value, AXES, pairs)


def swapped(value, seq_bits, fsdp_bits):
    return sent(value, lambda s, f: (s ^ seq_bits, f ^ fsdp_bits))


def together(*values):
    flat, tree = jax.tree.flatten(values)
    return jax.tree.unflatten(tree, lax.optimization_barrier(tuple(flat)))


def bits_of(size):
    return [1 << i for i in range(size.bit_length() - 1)]


def by_position(pieces, me):
    stack = jnp.stack(pieces, axis=0)
    count = len(pieces)
    tail = stack.shape[1:]
    for bit in bits_of(count):
        view = stack.reshape((count // (2 * bit), 2, bit) + tail)
        flipped = jnp.concatenate([view[:, 1:], view[:, :1]], axis=1)
        stack = jnp.where((me & bit) != 0, flipped, view).reshape((count,) + tail)
    return stack


def outbox_kernel(order_ref, spot_ref, frames_ref, *out_refs):
    rows, width = frames_ref.shape[1:]
    for peer, out in enumerate(out_refs):
        capacity, _, padded = out.shape
        lane = lax.broadcasted_iota(jnp.int32, (rows, LANES), 1) + (padded - LANES)
        for k in range(capacity):
            spot = spot_ref[peer * capacity + k]
            out[k, :, padded - LANES :] = jnp.where(lane == width, spot, 0.0).astype(BF16)
            out[k, :, :width] = frames_ref[order_ref[peer * capacity + k]]


def place_kernel(pick_ref, frames_ref, *refs):
    inbox, (out, head, tail) = refs[:-3], refs[-3:]
    slots, rows, width = frames_ref.shape
    total, padded = out.shape
    tokens = slots * rows
    capacity = inbox[0].shape[0]
    out[:tokens, padded - LANES :] = jnp.zeros((tokens, LANES), out.dtype)
    row = lax.broadcasted_iota(jnp.int32, (total - tokens, padded), 0)
    column = lax.broadcasted_iota(jnp.int32, (total - tokens, padded), 1)
    out[tokens:, :] = jnp.where((column == row + width) & (row < 6), 1.0, 0.0).astype(BF16)

    def one(p, carry):
        index = pick_ref[p]
        here = pl.ds(pl.multiple_of(p * rows, 16), rows)

        @pl.when(index < slots)
        def _():
            out[here, :width] = frames_ref[index]

        for peer, box in enumerate(inbox):
            first = slots + peer * capacity

            @pl.when((index >= first) & (index < first + capacity))
            def _():
                out[here, :width] = box[index - first, :, :width]

        return carry

    lax.fori_loop(0, slots, one, 0)
    head[...] = out[: head.shape[0]]
    tail[...] = out[tokens - tail.shape[0] : tokens]


def scalar_call(kernel, out_shape, scalars, arrays):
    return pl.pallas_call(
        kernel,
        grid_spec=pltpu.PrefetchScalarGridSpec(
            num_scalar_prefetch=len(scalars),
            grid=(),
            in_specs=[pl.BlockSpec(memory_space=pltpu.VMEM)] * len(arrays),
            out_specs=jax.tree.map(lambda _: pl.BlockSpec(memory_space=pltpu.VMEM), out_shape),
        ),
        out_shape=out_shape,
        compiler_params=kernel_params(60),
    )(*scalars, *arrays)


def outgoing(frames, destination, seq_index, seq_size, padded):
    slots, rows, _ = frames.shape
    capacity = 2 * slots // seq_size
    owner = (destination // slots) ^ seq_index
    rank = jnp.sum(
        ((owner[:, None] == owner[None, :]) & (destination[None, :] < destination[:, None])).astype(
            jnp.int32
        ),
        axis=1,
    )
    peers = jnp.arange(1, seq_size, dtype=jnp.int32)
    places = jnp.arange(capacity, dtype=jnp.int32)
    hit = (owner[None, None, :] == peers[:, None, None]) & (
        rank[None, None, :] == places[None, :, None]
    )
    order = jnp.sum(jnp.where(hit, jnp.arange(slots, dtype=jnp.int32), 0), axis=2).reshape(-1)
    spot = jnp.sum(jnp.where(hit, destination % slots + 1, 0), axis=2).reshape(-1) - 1
    return scalar_call(
        outbox_kernel,
        [jax.ShapeDtypeStruct((capacity, rows, padded), BF16)] * (seq_size - 1),
        [order, spot.astype(F32)],
        [frames],
    )


def arrivals(destination, spots, seq_index):
    slots = destination.shape[0]
    numbers = jnp.arange(slots, dtype=jnp.int32)
    local = (destination == seq_index * slots + numbers[:, None]).astype(jnp.int32)
    boxed = (spots.astype(jnp.int32).reshape(-1) == numbers[:, None]).astype(jnp.int32)
    places = slots + jnp.arange(boxed.shape[1], dtype=jnp.int32)
    return jnp.sum(local * numbers, axis=1) + jnp.sum(boxed * places, axis=1)


def chain_step(rising, falling, k, chips):
    return (
        sent(rising, lambda s, f: (s, f + 2) if k - 1 <= f // 2 < chips - 1 else None),
        sent(falling, lambda s, f: (s, f - 2) if 0 < f // 2 <= chips - k else None),
    )


def chain_slot(rising, falling, k, chip, chips):
    low = chip < chips // 2
    far = jnp.maximum(chip, chips - 1 - chip)
    towards = jnp.where(low, 1, -1)
    options = [falling[k], rising[k]]
    which = jnp.where(low, 0, 1)
    origin = chip + towards * k
    for reach in range(chips // 2, k):
        which = jnp.where(far == reach, len(options) + jnp.where(low, 1, 0), which)
        options += [falling[k - reach], rising[k - reach]]
        origin = jnp.where(far == reach, chip - towards * (k - reach), origin)
    return options, which, origin


def chosen(options, which):
    value = options[0]
    for i, option in enumerate(options[1:], 1):
        value = jnp.where(which == i, option, value)
    return value


def load_weights(place_ref, shard_refs, weights, sems, by_chip):
    pairs = len(shard_refs) // 2
    shard = shard_refs[0].shape[0]
    core = place_ref[0]
    for k in range(pairs)[::-1]:
        for h in range(2):
            lane = core if h == 0 else 1 - core
            row = 2 * (place_ref[1 + k] if by_chip else k) + lane
            first = pl.multiple_of(row * shard, 16)
            pltpu.make_async_copy(
                shard_refs[2 * k + h], weights.at[pl.ds(first, shard), :], sems.at[row]
            ).start()


def wait_weights(shard_ref, weights, sems, pair):
    shard = shard_ref.shape[0]
    for row in (2 * pair, 2 * pair + 1):
        pltpu.make_async_copy(
            shard_ref, weights.at[pl.ds(row * shard, shard), :], sems.at[row]
        ).wait()


def pair_product(inputs, weights, first, count, store, squares):
    total = squares[...]
    for begin in range(0, count, 256):
        size = min(256, count - begin)
        result = lax.dot_general(
            inputs[...],
            weights[first + begin : first + begin + size, :],
            (((1,), (1,)), ((), ())),
            preferred_element_type=F32,
        )
        store(begin, size, result)
        for t in range(0, size, LANES):
            part = result[:, t : t + LANES]
            total = total + part * part
    squares[...] = total


def early_kernel(place_ref, rows_ref, *refs, pairs):
    shard_refs = refs[: 2 * pairs]
    acc_ref, squares, weights, sems = refs[2 * pairs :]
    group = acc_ref.shape[2]
    load_weights(place_ref, shard_refs, weights, sems, False)
    squares[...] = jnp.zeros_like(squares)
    for k in range(pairs):
        wait_weights(shard_refs[0], weights, sems, k)

        def store(begin, size, result, k=k):
            acc_ref[k, :, begin : begin + size] = result

        pair_product(rows_ref, weights, k * group, group, store, squares)


VMEM_SPEC = pl.BlockSpec(memory_space=pltpu.VMEM)
ANY_SPEC = pl.BlockSpec(memory_space=pl.ANY)


def stem_early(rows_in, shards, core_id):
    rows, padded = rows_in.shape
    pairs = len(shards) // 2
    group = 2 * shards[0].shape[0]
    return pl.pallas_call(
        functools.partial(early_kernel, pairs=pairs),
        grid_spec=pltpu.PrefetchScalarGridSpec(
            num_scalar_prefetch=1,
            grid=(),
            in_specs=[VMEM_SPEC] + [ANY_SPEC] * len(shards),
            out_specs=[VMEM_SPEC] * 2,
            scratch_shapes=[
                pltpu.VMEM((pairs * group, padded), BF16),
                pltpu.SemaphoreType.DMA((2 * pairs,)),
            ],
        ),
        out_shape=[
            jax.ShapeDtypeStruct((pairs, rows, group), F32),
            jax.ShapeDtypeStruct((rows, LANES), F32),
        ],
        compiler_params=kernel_params(24),
    )(core_id, rows_in, *shards)


def gate_of(value):
    return 0.5 * jnp.tanh(0.5 * value) + 0.5


def mixed_at(window, taps, mask_ref, first):
    total = window[0] * (taps[0] * mask_ref[first])
    for k in range(1, 5):
        total = total + window[k] * (taps[k] * mask_ref[first + k])
    return total


def layer_kernel(
    place_ref, mask_ref, main_ref, low_ref, high_ref, cot_ref, cot_low_ref, cot_high_ref, *refs,
    pairs, late, slots, channels
):
    shard_refs, refs = refs[: 2 * (pairs + late)], refs[2 * (pairs + late) :]
    if pairs:
        early_ref, early_squares, refs = refs[0], refs[1], refs[2:]
    part_ref, feat_ref, stem_ref, give_ref, keep_ref = refs[:5]
    weights, rows_all, acc, cots, feats, d_stem, lanes_of_core, gated, slopes, squares, inverse = refs[5:16]
    sems, in_sems, cot_sems, out_sems, stem_sems = refs[16:]
    group = 2 * shard_refs[0].shape[0]
    chips = channels // group
    tokens = cot_ref.shape[0]
    rows = tokens // slots
    halo, edge = low_ref.shape[0], cot_low_ref.shape[0]
    own_row = 2 * halo
    body = own_row + tokens
    core = place_ref[0]
    load_weights(place_ref, shard_refs, weights, sems, not pairs)
    if pairs:
        for k in range(pairs):
            lanes = pl.ds(pl.multiple_of(place_ref[1 + k] * group, LANES), group)
            pltpu.make_async_copy(
                early_ref.at[k],
                acc.at[pl.ds(own_row, early_ref.shape[1]), lanes],
                in_sems.at[place_ref[1 + k]],
            ).start()
    parts = 4
    size = channels // parts
    cot_loads = []
    for i in range(parts):
        lanes = pl.ds(i * size, size)
        first = 0
        for h, ref in enumerate((cot_low_ref, cot_ref, cot_high_ref)):
            count = ref.shape[0]
            cot_loads.append(
                pltpu.make_async_copy(
                    ref.at[:, lanes], cots.at[pl.ds(first, count), lanes], cot_sems.at[i, h]
                )
            )
            first += count
    for copy in cot_loads:
        copy.start()
    rows_all[0:halo] = low_ref[...]
    rows_all[halo:own_row] = high_ref[...]
    rows_all[own_row:] = main_ref[...]
    squares[...] = jnp.zeros_like(squares)
    if pairs:
        squares[own_row:] = early_squares[...]
        for k in [pairs] + list(range(pairs)):
            count = rows_all.shape[0] if k == pairs else own_row
            wait_weights(shard_refs[0], weights, sems, k)

            def store(begin, width, result, k=k, count=count):
                first = pl.multiple_of(place_ref[1 + k] * group + begin, LANES)
                acc[0:count, pl.ds(first, width)] = result

            pair_product(
                rows_all.at[0:count], weights, k * group, group, store, squares.at[0:count]
            )
    else:
        for z in range(late):
            wait_weights(shard_refs[0], weights, sems, z)
        tile = 256

        def one(j, carry):
            first = pl.multiple_of(j * tile, tile)
            result = lax.dot_general(
                rows_all[...],
                weights[pl.ds(first, tile), :],
                (((1,), (1,)), ((), ())),
                preferred_element_type=F32,
            )
            acc[:, pl.ds(first, tile)] = result
            total = squares[...]
            for t in range(0, tile, LANES):
                total = total + result[:, t : t + LANES] * result[:, t : t + LANES]
            squares[...] = total
            return carry

        lax.fori_loop(0, channels // tile, one, 0)
    mean = jnp.sum(squares[...], axis=1, keepdims=True) / channels
    inverse[...] = jnp.broadcast_to(lax.rsqrt(mean + EPSILON), inverse.shape)
    squares[...] = jnp.zeros_like(squares)

    def rows_of_slot(i):
        edge_slots = halo // rows
        if i < edge_slots:
            first = i * rows
        elif i < edge_slots + slots:
            first = own_row + (i - edge_slots) * rows
        else:
            first = halo + (i - edge_slots - slots) * rows
        return slice(first, first + rows)

    def columns(t, carry):
        lanes = pl.ds(pl.multiple_of(t * LANES, LANES), LANES)
        gain = acc[body : body + 1, lanes]
        taps = [acc[body + 1 + k : body + 2 + k, lanes] for k in range(5)]

        def normed(i):
            here = rows_of_slot(i)
            return (acc[here, lanes] * inverse[here] * gain).astype(BF16).astype(F32)

        window = [normed(i) for i in range(4)]
        sums = [jnp.zeros((8, LANES), F32) for _ in range(5)]
        for i in range(slots + 4):
            window.append(normed(i + 4))
            mixed = mixed_at(window, taps, mask_ref, 5 * i)
            gate = gate_of(mixed)
            smooth = mixed * gate
            here = slice(i * rows, (i + 1) * rows)
            up = cots[here, lanes].astype(F32)
            slope = (up * (gate + smooth - smooth * gate)).astype(BF16).astype(F32)
            slopes[here] = slope
            if 2 <= i < slots + 2:
                own = slice((i - 2) * rows, (i - 1) * rows)
                stem = acc[rows_of_slot(i + 2), lanes]
                feats[own, lanes] = (stem + smooth).astype(BF16)
                for k in range(5):
                    product = (slope * window[k]).reshape(rows // 8, 8, LANES)
                    sums[k] = sums[k] + jnp.sum(product, axis=0) * mask_ref[5 * i + k]
            window = window[1:]
        for k in range(5):
            part_ref[1 + k : 2 + k, lanes] = jnp.sum(sums[k], axis=0, keepdims=True)
        part_ref[6:8, lanes] = jnp.zeros((2, LANES), F32)
        total = jnp.zeros((8, LANES), F32)
        for p in range(slots):
            window = [slopes[(p + o) * rows : (p + o + 1) * rows] for o in range(5)]
            own = slice(p * rows, (p + 1) * rows)
            here = rows_of_slot(p + 4)
            d_normed = mixed_at(window, taps[::-1], mask_ref, 5 * (p + 2))
            product = d_normed * (acc[here, lanes] * inverse[here])
            total = total + jnp.sum(product.reshape(rows // 8, 8, LANES), axis=0)
            gated[own, lanes] = d_normed * gain
            squares[own] = squares[own] + product * gain
        part_ref[0:1, lanes] = jnp.sum(total, axis=0, keepdims=True)
        return carry

    copies = []
    for i in range(parts):
        for copy in cot_loads[3 * i : 3 * i + 3]:
            copy.wait()
        if pairs:

            @pl.when(place_ref[1 + pairs] != i)
            def _(i=i):
                pltpu.make_async_copy(
                    early_ref.at[0],
                    acc.at[pl.ds(own_row, early_ref.shape[1]), pl.ds(i * group, group)],
                    in_sems.at[i],
                ).wait()

        lax.fori_loop(i * size // LANES, (i + 1) * size // LANES, columns, 0)
        lanes = pl.ds(i * size, size)
        copy = pltpu.make_async_copy(feats.at[:, lanes], feat_ref.at[:, lanes], out_sems.at[i])
        copy.start()
        copies.append(copy)
    mean = jnp.sum(squares[0:tokens], axis=1, keepdims=True) / channels
    squares[0:tokens] = jnp.broadcast_to(mean, (tokens, LANES))

    def finish_columns(t, carry):
        lanes = pl.ds(pl.multiple_of(t * LANES, LANES), LANES)
        inv = inverse[own_row:body]
        unit = acc[own_row:body, lanes] * inv
        value = cots[edge : edge + tokens, lanes].astype(F32) + inv * (
            gated[:, lanes] - unit * squares[0:tokens]
        )
        d_stem[:, lanes] = value.astype(BF16)
        return carry

    shard = group // 2
    room = lanes_of_core.shape[2] // chips
    steps = chips if group % LANES == 0 else 1
    for i in range(steps):
        lax.fori_loop(
            i * channels // steps // LANES, (i + 1) * channels // steps // LANES, finish_columns, 0
        )
        lanes = pl.ds(i * (channels // steps), channels // steps)
        copies.append(
            pltpu.make_async_copy(d_stem.at[:, lanes], stem_ref.at[:, lanes], stem_sems.at[i, 0])
        )
        copies[-1].start()
        for z in range(i * chips // steps, (i + 1) * chips // steps):
            for h in range(2):
                first = (2 * z + h) * shard
                lanes_of_core[h, :, z * room : z * room + shard] = d_stem[:, first : first + shard]
                if room > shard:
                    lanes_of_core[h, :, z * room + shard : (z + 1) * room] = jnp.zeros(
                        (tokens, room - shard), BF16
                    )
        width = chips // steps * room
        lanes = pl.ds(i * width, width)
        for h, ref in enumerate((keep_ref, give_ref)):
            copies.append(
                pltpu.make_async_copy(
                    lanes_of_core.at[(core + h) % 2, :, lanes],
                    ref.at[:, lanes],
                    stem_sems.at[i, 1 + h],
                )
            )
            copies[-1].start()
    for copy in copies:
        copy.wait()


def layer(main, low, high, cot, cot_low, cot_high, shards, early, places, mask, slots, channels):
    tokens = cot.shape[0]
    padded = main.shape[1]
    halo, edge = low.shape[0], cot_low.shape[0]
    total = main.shape[0] + 2 * halo
    pairs = early[0].shape[0] if early else 0
    late = len(shards) // 2 - pairs
    shard = shards[0].shape[0]
    half = channels // (2 * shard) * round_up(shard, LANES)
    return pl.pallas_call(
        functools.partial(layer_kernel, pairs=pairs, late=late, slots=slots, channels=channels),
        grid_spec=pltpu.PrefetchScalarGridSpec(
            num_scalar_prefetch=2,
            grid=(),
            in_specs=[VMEM_SPEC] * 3
            + [ANY_SPEC] * 3
            + [ANY_SPEC] * len(shards)
            + ([ANY_SPEC, VMEM_SPEC] if pairs else []),
            out_specs=[VMEM_SPEC] + [ANY_SPEC] * 4,
            scratch_shapes=[
                pltpu.VMEM((channels, padded), BF16),
                pltpu.VMEM((total, padded), BF16),
                pltpu.VMEM((total, channels), F32),
                pltpu.VMEM((tokens + 2 * edge, channels), BF16),
                pltpu.VMEM((tokens, channels), BF16),
                pltpu.VMEM((tokens, channels), BF16),
                pltpu.VMEM((2, tokens, half), BF16),
                pltpu.VMEM((tokens, channels), F32),
                pltpu.VMEM((tokens + 2 * edge, LANES), F32),
                pltpu.VMEM((total, LANES), F32),
                pltpu.VMEM((total, LANES), F32),
                pltpu.SemaphoreType.DMA((len(shards),)),
                pltpu.SemaphoreType.DMA((len(shards) // 2,)),
                pltpu.SemaphoreType.DMA((4, 3)),
                pltpu.SemaphoreType.DMA((4,)),
                pltpu.SemaphoreType.DMA((len(shards) // 2, 3)),
            ],
        ),
        out_shape=[
            jax.ShapeDtypeStruct((8, channels), F32),
            jax.ShapeDtypeStruct((tokens, channels), BF16),
            jax.ShapeDtypeStruct((tokens, channels), BF16),
            jax.ShapeDtypeStruct((tokens, half), BF16),
            jax.ShapeDtypeStruct((tokens, half), BF16),
        ],
        compiler_params=kernel_params(60),
    )(places, mask, main, low, high, cot, cot_low, cot_high, *shards, *early)


def pixel_kernel(place_ref, d_stem_ref, *refs, chips, begin, tile):
    shard_refs, refs = refs[: 2 * chips], refs[2 * chips :]
    before = refs[0] if begin else None
    out_ref, weights, sems = refs[1:] if begin else refs
    width = out_ref.shape[1] - begin
    lanes = pl.ds(begin, weights.shape[1])
    load_weights(place_ref, [r.at[:, lanes] for r in shard_refs], weights, sems, True)
    for z in range(chips):
        wait_weights(shard_refs[0].at[:, lanes], weights, sems, z)
    if begin:
        out_ref[:, :begin] = before[...]
    for first in range(0, width, tile):
        size = min(tile, width - first)
        columns = slice(first, first + round_up(size, LANES))
        value = jnp.dot(d_stem_ref[...], weights[:, columns], preferred_element_type=F32)
        out_ref[:, begin + first : begin + first + size] = value[:, :size].astype(BF16)


def pixel_grads(d_stem, shards, places, begin, end, before=None):
    tokens, channels = d_stem.shape
    chips = len(shards) // 2
    lanes = round_up(end - begin, LANES)
    return pl.pallas_call(
        functools.partial(pixel_kernel, chips=chips, begin=begin, tile=256),
        grid_spec=pltpu.PrefetchScalarGridSpec(
            num_scalar_prefetch=1,
            grid=(),
            in_specs=[VMEM_SPEC]
            + [ANY_SPEC] * len(shards)
            + ([VMEM_SPEC] if begin else []),
            out_specs=VMEM_SPEC,
            scratch_shapes=[
                pltpu.VMEM((channels, lanes), BF16),
                pltpu.SemaphoreType.DMA((2 * chips,)),
            ],
        ),
        out_shape=jax.ShapeDtypeStruct((tokens, end), BF16),
        compiler_params=kernel_params(60),
    )(places, d_stem, *shards, *([before] if begin else []))


def turn_kernel(first_ref, second_ref, out_ref, *, tokens):
    height, depth = out_ref.shape
    out_ref[:, 2 * tokens :] = jnp.zeros((height, depth - 2 * tokens), BF16)
    both = jnp.concatenate([first_ref[:tokens], second_ref[:tokens]], axis=0)
    for m in range(0, first_ref.shape[1], LANES):
        count = min(LANES, height - m)
        if count > 0:
            out_ref[m : m + count, : 2 * tokens] = both[:, m : m + LANES].T[:count]


def turned(packed, packed_other, height, tokens):
    return pl.pallas_call(
        functools.partial(turn_kernel, tokens=tokens),
        in_specs=[VMEM_SPEC] * 2,
        out_specs=VMEM_SPEC,
        out_shape=jax.ShapeDtypeStruct((height, round_up(2 * tokens, LANES)), BF16),
        compiler_params=kernel_params(16),
    )(packed, packed_other)


def halves_beside(value, shard):
    rows = value.shape[0] // 2
    return value[:rows, :shard], value[rows:, :shard]


def weight_kernel(where_ref, pixels_ref, keep_ref, got_ref, *refs, bits, share, line_share, shard, give):
    outs, (d_stem, left, line, sems, left_sems) = refs[:3], refs[3:]
    tokens = keep_ref.shape[0]
    seq_index, chip = where_ref[0], where_ref[1]
    seq_size = 2 * outs[0].shape[1]
    half = seq_size // 2
    chips = 2 * outs[0].shape[0]
    room = d_stem.shape[1] // chips
    arrive = [[] for _ in range(chips + 1)]
    for g, bit in enumerate(bits):
        mine = (seq_index // bit) % 2
        wanted = 1 - mine if give else mine
        for i in range(half):
            p = (i // bit) * (2 * bit) + i % bit + bit * wanted
            arrive[g * (chips // 2)].append(
                pltpu.make_async_copy(
                    pixels_ref.at[pl.ds(pl.multiple_of(p * share, 16), share), :],
                    left.at[g, pl.ds(i * share, share), :],
                    left_sems.at[g, i],
                )
            )
        for z in range(g * (chips // 2), (g + 1) * (chips // 2)):
            lanes = pl.ds(z * room, room)
            for h, ref in enumerate((keep_ref, got_ref)):
                arrive[z].append(
                    pltpu.make_async_copy(
                        ref.at[:, lanes],
                        d_stem.at[pl.ds(h * tokens, tokens), lanes],
                        sems.at[2 * z + h],
                    )
                )
    arrive[chips].append(
        pltpu.make_async_copy(
            pixels_ref.at[pl.ds(seq_size * share, line.shape[0]), :], line, sems.at[2 * chips]
        )
    )
    for copy in sum(arrive, []):
        copy.start()
    extra = d_stem.shape[0] - 2 * tokens
    d_stem[2 * tokens :, :] = jnp.zeros((extra, d_stem.shape[1]), BF16)

    def fill(out, value, count, rows):
        for i in range(count):
            low, high = halves_beside(value[i * rows : (i + 1) * rows], shard)
            out[i, :, :shard] = low.astype(out.dtype)
            out[i, :, shard:] = high.astype(out.dtype)

    for g in range(2):
        for z in range(chips // 2):
            for copy in arrive[g * (chips // 2) + z]:
                copy.wait()
            first = (g * (chips // 2) + z) * room
            value = jnp.dot(
                left[g], d_stem[:, first : first + room], preferred_element_type=F32
            )
            fill(outs[g].at[z], value, half, share)
    for copy in arrive[chips]:
        copy.wait()
    mine = chip % 2
    wanted = 1 - mine if give else mine
    for i in range(chips // 2):
        columns = pl.ds(pl.multiple_of((2 * i + wanted) * room, LANES), room)
        value = jnp.dot(line[...], d_stem[:, columns], preferred_element_type=F32)
        fill(outs[2].at[i], value, seq_size, line_share)


def weight_part(pixels, keep, got, where, chips, seq_size, shard, share, line_share, bits, give):
    half = keep.shape[1]
    height, depth = pixels.shape
    kind = BF16 if give else F32
    plane = jax.ShapeDtypeStruct((chips // 2, seq_size // 2, share // 2, 2 * shard), kind)
    line = jax.ShapeDtypeStruct((chips // 2, seq_size, line_share // 2, 2 * shard), kind)
    return pl.pallas_call(
        functools.partial(
            weight_kernel, bits=bits, share=share, line_share=line_share, shard=shard, give=give
        ),
        grid_spec=pltpu.PrefetchScalarGridSpec(
            num_scalar_prefetch=1,
            grid=(),
            in_specs=[ANY_SPEC] * 3,
            out_specs=[VMEM_SPEC] * 3,
            scratch_shapes=[
                pltpu.VMEM((depth, half), BF16),
                pltpu.VMEM((2, seq_size // 2 * share, depth), BF16),
                pltpu.VMEM((seq_size * line_share, depth), BF16),
                pltpu.SemaphoreType.DMA((2 * chips + 1,)),
                pltpu.SemaphoreType.DMA((2, seq_size // 2)),
            ],
        ),
        out_shape=[plane, plane, line],
        compiler_params=kernel_params(24 if give else 60),
    )(where, pixels, keep, got)


def bit_at(index, bit):
    return (index // bit) % 2


def fetched(at_ref, refs, buffers, sems, indices):
    copies = []
    for n, (ref, buffer, index) in enumerate(zip(refs, buffers, indices)):
        place = tuple(slice(None) if p is None else at_ref[p] for p in index)
        source = ref.at[place] if place else ref
        copies.append(pltpu.make_async_copy(source, buffer, sems.at[n]))
        copies[-1].start()
    return copies


def total_of(copies, buffers):
    total = None
    for copy, buffer in zip(copies, buffers):
        copy.wait()
        value = buffer[...].astype(F32)
        total = value if total is None else total + value
    return total


def sums_kernel(at_ref, *refs, plan, indices):
    count = len(indices)
    results = sum(2 if keep else 1 for _, _, keep in plan)
    ins, outs = refs[:count], refs[count : count + results]
    buffers = list(refs[count + results : 2 * count + results])
    stores = list(refs[2 * count + results : 2 * count + 2 * results])
    sems, out_sems = refs[2 * count + 2 * results :]
    copies = fetched(at_ref, ins, buffers, sems, indices)
    written = []

    def write(value):
        n = len(written)
        stores[n][...] = value.astype(stores[n].dtype)
        written.append(pltpu.make_async_copy(stores[n], outs[n], out_sems.at[n]))
        written[-1].start()

    for alternatives, selector, keep in plan:
        totals = []
        for n in alternatives:
            totals.append(total_of(copies[:n], buffers[:n]))
            copies, buffers = copies[n:], buffers[n:]
        if keep:
            upper = at_ref[selector] == 1
            write(jnp.where(upper, totals[0], totals[1]))
            write(jnp.where(upper, totals[1], totals[0]))
        elif len(totals) == 1:
            write(totals[0])
        else:
            write(jnp.stack(totals, axis=0))
    for copy in written:
        copy.wait()


def part_shape(array, index):
    return tuple(array.shape[d] for d, at in enumerate(index) if at is None) + tuple(
        array.shape[-2:]
    )


def sums(units):
    scalars, arrays, indices, buffers, outs, plan = [], [], [], [], [], []

    def scalar(value):
        scalars.append(value)
        return len(scalars) - 1

    for alternatives, selector, kind in units:
        for terms in alternatives:
            for array, index in terms:
                shape = part_shape(array, index)
                arrays.append(array)
                indices.append([None if at is None else scalar(at) for at in index])
                buffers.append(pltpu.VMEM(shape, array.dtype))
        keep = selector is not None
        plan.append(([len(t) for t in alternatives], scalar(selector) if keep else None, keep))
        stacked = () if keep or len(alternatives) == 1 else (len(alternatives),)
        outs.append(jax.ShapeDtypeStruct(stacked + shape, kind))
        if keep:
            outs.append(jax.ShapeDtypeStruct(shape, F32))
    if not scalars:
        scalars = [jnp.int32(0)]
    results = list(
        pl.pallas_call(
            functools.partial(sums_kernel, plan=plan, indices=indices),
            grid_spec=pltpu.PrefetchScalarGridSpec(
                num_scalar_prefetch=1,
                grid=(),
                in_specs=[ANY_SPEC] * len(arrays),
                out_specs=[ANY_SPEC] * len(outs),
                scratch_shapes=buffers
                + [pltpu.VMEM(o.shape, o.dtype) for o in outs]
                + [pltpu.SemaphoreType.DMA((len(arrays),)), pltpu.SemaphoreType.DMA((len(outs),))],
            ),
            out_shape=outs,
            compiler_params=kernel_params(60),
        )(jnp.stack([jnp.asarray(s, jnp.int32) for s in scalars]), *arrays)
    )
    return [(results.pop(0), results.pop(0) if keep else None) for _, _, keep in plan]


def at_own(terms, mine, done, label=None):
    def place(b):
        if isinstance(b, int):
            return b
        return 1 - mine[b] if b == label else mine[b] if b in done else None

    return [(array, [place(b) for b in labels]) for array, labels in terms]


def split_view(array, labels):
    return array.reshape((2,) * len(labels) + tuple(array.shape[-2:]))


def route_of(label):
    axis, bit = label
    if axis == "seq":
        return lambda s, f: (s ^ bit, f)
    return lambda s, f: (s, f ^ (2 * bit))


def without(labels, done):
    return [label for label in labels if label not in done]


def halving(gives, keeps, labels, orders, mine, last=None):
    came = yield gives, [route_of(order[0]) for order in orders]
    terms = []
    for keep, (arrived, _, _), order in zip(keeps, came, orders):
        rest = without(labels, order[:1])
        terms.append([(split_view(keep, rest), rest), (split_view(arrived, rest), rest)])
    for i in range(1, len(orders[0])):
        parts = [at_own(t, mine, order[:i], order[i]) for t, order in zip(terms, orders)]
        if len(orders) == 2 and orders[0][i] == orders[1][i]:
            ((arrived, _, _),) = yield [(parts, None, BF16)], [route_of(orders[0][i])]
            for g, (t, order) in enumerate(zip(terms, orders)):
                rest = without(labels, order[: i + 1])
                t.append((split_view(arrived, [g] + rest), [g] + rest))
            continue
        came = yield [([p], None, BF16) for p in parts], [route_of(order[i]) for order in orders]
        for t, (arrived, _, _), order in zip(terms, came, orders):
            rest = without(labels, order[: i + 1])
            t.append((split_view(arrived, rest), rest))
    final = [at_own(t, mine, order) for t, order in zip(terms, orders)]
    if last is not None:
        ((arrived, kept, _),) = yield [(final, mine[last], BF16)], [route_of(last)]
        final = [[(kept, []), (arrived, [])]]
    yield final[0], None


def all_sum(value, routes):
    ((came, _, give),) = yield [value], routes[:1]
    for route in routes[1:]:
        ((came, _, give),) = yield [([[(give, []), (came, [])]], None, F32)], [route]
    yield (give, came), None


def in_rounds(chains, beside):
    waiting = [next(chain) for chain in chains]
    count, done = 0, None
    while any(routes is not None for _, routes in waiting):
        units = [u for values, routes in waiting if routes is not None for u in values]
        routes = [r for _, some in waiting if some is not None for r in some]
        ready = sums(units) if count else [(value, None) for value in units]
        came = [sent(give, route) for (give, _), route in zip(ready, routes)]
        if count in beside:
            ready, done = beside[count](ready, done)
            came, done = together(came, done)
        else:
            (came,) = together(came)
        count += 1
        arrived = [(value, kept, give) for value, (give, kept) in zip(came, ready)]
        for i, (values, some) in enumerate(waiting):
            if some is not None:
                mine, arrived = arrived[: len(values)], arrived[len(values) :]
                waiting[i] = chains[i].send(mine)
    return [values for values, _ in waiting], done


def unpack_kernel(at_ref, *refs, share, line_share):
    pieces, (out_ref, rows_all) = refs[:-2], refs[-2:]
    width = out_ref.shape[1]
    for o, piece in enumerate(pieces):
        p = at_ref[0] ^ o
        first = pl.multiple_of(p * share, 16)
        rows_all[pl.ds(first, share), :] = piece[0:share]
        first = pl.multiple_of(len(pieces) * share + p * line_share, 16)
        rows_all[pl.ds(first, line_share), :] = piece[share:]
    for first in range(0, width, LANES):
        size = min(LANES, width - first)
        out_ref[:, first : first + size] = rows_all[first : first + LANES].T[:, :size]


def unpacked(pieces, seq_index, width, share, line_share):
    height, shard = pieces[0].shape
    return pl.pallas_call(
        functools.partial(unpack_kernel, share=share, line_share=line_share),
        grid_spec=pltpu.PrefetchScalarGridSpec(
            num_scalar_prefetch=1,
            grid=(),
            in_specs=[VMEM_SPEC] * len(pieces),
            out_specs=VMEM_SPEC,
            scratch_shapes=[pltpu.VMEM((len(pieces) * height, shard), BF16)],
        ),
        out_shape=jax.ShapeDtypeStruct((shard, width), BF16),
        compiler_params=kernel_params(60),
    )(seq_index.astype(jnp.int32).reshape(1), *pieces)


def finish_kernel(at_ref, *refs, counts, indices, scale):
    count = len(indices)
    ins, out_ref = refs[:count], refs[count]
    buffers, sems = list(refs[count + 1 : -1]), refs[-1]
    copies = fetched(at_ref, ins, buffers, sems, indices)
    shard = out_ref.shape[1]
    begin = 0
    for n in counts:
        total = (total_of(copies[:n], buffers[:n]) * scale).astype(BF16)
        copies, buffers = copies[n:], buffers[n:]
        for part in (total[:, :shard], total[:, shard:]):
            out_ref[begin : begin + part.shape[0], :] = part
            begin += part.shape[0]


def finish(chains, scale):
    scalars, arrays, indices, buffers, height = [], [], [], [], 0
    for terms in chains:
        for array, index in terms:
            indices.append(list(range(len(scalars), len(scalars) + len(index))))
            scalars += index
            arrays.append(array)
            buffers.append(pltpu.VMEM(tuple(array.shape[-2:]), array.dtype))
        height += 2 * terms[0][0].shape[-2]
    shard = arrays[0].shape[-1] // 2
    return pl.pallas_call(
        functools.partial(
            finish_kernel, counts=[len(t) for t in chains], indices=indices, scale=scale
        ),
        grid_spec=pltpu.PrefetchScalarGridSpec(
            num_scalar_prefetch=1,
            grid=(),
            in_specs=[ANY_SPEC] * len(arrays),
            out_specs=VMEM_SPEC,
            scratch_shapes=buffers + [pltpu.SemaphoreType.DMA((len(arrays),))],
        ),
        out_shape=jax.ShapeDtypeStruct((height, shard), BF16),
        compiler_params=kernel_params(60),
    )(jnp.stack([jnp.asarray(s, jnp.int32) for s in scalars]), *arrays)


def shards(patches, send_slot, segments, stem_weight, norm_gain, conv_kernel, cotangent):
    seq_size, fsdp_size = lax.axis_size("seq"), lax.axis_size("fsdp")
    seq_index, fsdp_index = lax.axis_index("seq"), lax.axis_index("fsdp")
    chips, chip, core = fsdp_size // 2, fsdp_index // 2, fsdp_index % 2
    slots = send_slot.shape[1]
    tokens, width = patches.shape[1], patches.shape[2]
    rows = tokens // slots
    edge = 2 * rows
    shard = stem_weight.shape[0]
    channels = shard * fsdp_size
    padded = round_up(width + 6, LANES)
    capacity = 2 * slots // seq_size
    cot = cotangent[0]
    core_id = core.astype(jnp.int32).reshape(1)

    def following(s, f):
        return (s + 1, f) if s + 1 < seq_size else None

    def preceding(s, f):
        return (s - 1, f) if s > 0 else None

    own = jnp.concatenate(
        [
            stem_weight,
            norm_gain[:, None],
            conv_kernel.T,
            jnp.zeros((shard, padded - width - 6), BF16),
        ],
        axis=1,
    )
    own, cot, patches = together(own, cot, patches)
    tail, head = cot[tokens - edge :], cot[:edge]
    frames = patches[0].reshape(slots, rows, width)
    boxes = outgoing(frames, send_slot[0], seq_index, seq_size, padded)
    rising, falling = {0: own}, {0: own}
    own_core = swapped(own, 0, 1)
    boxes, own_core = together(boxes, own_core)
    inbox = [None] * (seq_size - 1)
    direct = [o for o in range(1, seq_size) if o.bit_count() % 2 == 1]
    others = [o for o in range(1, seq_size) if o.bit_count() % 2 == 0]
    split = 2 * shard % LANES == 0 and chips == 4
    lane_shards, core_shards, chip_of = [own], [own_core], [chip]
    early = []
    spots = [None] * (seq_size - 1)

    def arrive(numbers, boxes):
        for o, box in zip(numbers, boxes):
            inbox[o - 1], spots[o - 1] = box, box[:, 0, width]

    def add_shard(k, rising, falling):
        options, which, origin = chain_slot(rising, falling, k, chip, chips)
        lane_shards.append(chosen(options, which))
        core_shards.append(swapped(lane_shards[-1], 0, 1))
        chip_of.append(origin)

    for k in range(1, chips):
        rising[k], falling[k] = chain_step(rising[k - 1], falling[k - 1], k, chips)
        if k == 1:
            came = [swapped(boxes[o - 1], o, 0) for o in direct]
            rising, falling, came, boxes, tail, head = together(
                rising, falling, came, boxes, tail, head
            )
            arrive(direct, came)
        elif k == 2:
            came = [swapped(boxes[o - 1], o, 0) for o in others]
            cot_low = sent(tail, following)
            if split:
                rising[1], falling[1], spots = together(rising[1], falling[1], spots)
                add_shard(1, rising, falling)
            rising, falling, cot_low, came, core_shards, lane_shards, spots, head = together(
                rising, falling, cot_low, came, core_shards, lane_shards, spots, head
            )
            arrive(others, came)
            cot_high = sent(head, preceding)
            pick = arrivals(send_slot[0], jnp.stack(spots, axis=0), seq_index)
            main, main_head, main_tail = scalar_call(
                place_kernel,
                [
                    jax.ShapeDtypeStruct((count, padded), BF16)
                    for count in (tokens + 16, 2 * edge, 2 * edge)
                ],
                [pick],
                [frames] + inbox,
            )
            if split:
                add_shard(2, rising, falling)
                main, main_head, main_tail, lane_shards, core_shards = together(
                    main, main_head, main_tail, lane_shards, core_shards
                )
            low = sent(main_tail, following)
            high = sent(main_head, preceding)
        elif k == 3 and split:
            pairs = [v for both in zip(lane_shards, core_shards) for v in both]
            early_main, main_squares = stem_early(main, pairs, core_id)
            rising, falling, early_main, low, high, main, cot_high = together(
                rising, falling, early_main, low, high, main, cot_high
            )
        else:
            rising, falling = together(rising, falling)
    for k in range(len(lane_shards), chips):
        add_shard(k, rising, falling)
    height = round_up(width, 64 * seq_size)
    main_other = swapped(main, 0, 1)
    places = jnp.stack([core] + chip_of).astype(jnp.int32)
    all_pairs = [v for both in zip(lane_shards, core_shards) for v in both]
    if split:
        all_pairs, main_other = together(all_pairs, main_other)
        early = [early_main, main_squares]

    ids = segments[0]
    total_slots = ids.shape[0]
    centre = seq_index * slots + jnp.arange(-2, slots + 2, dtype=jnp.int32)
    near = centre[:, None] + jnp.arange(-2, 3, dtype=jnp.int32)[None, :]
    inside = (near >= 0) & (near < total_slots) & ((centre >= 0) & (centre < total_slots))[:, None]
    same = (
        ids[jnp.clip(near, 0, total_slots - 1)] == ids[jnp.clip(centre, 0, total_slots - 1)][:, None]
    )
    mask = (inside & same).astype(F32).reshape(-1)
    chan_part, features, d_stem, give, keep = layer(
        main, low, high, cot, cot_low, cot_high, all_pairs, early, places, mask, slots, channels
    )
    chan_part = chan_part + swapped(chan_part, 0, 1)
    got = swapped(give, 0, 1)
    pixels = turned(main, main_other, height, tokens)
    middle = round_up(width // 2, LANES)

    seq_bits = bits_of(seq_size)
    chip_bits = bits_of(chips)
    line_share = height // seq_size // 4 // 32 * 32
    share = height // seq_size - line_share
    where = jnp.stack([seq_index, chip]).astype(jnp.int32)
    first_bits = [seq_bits[0], seq_bits[-1]]
    sizes = (chips, seq_size, shard, share, line_share, first_bits)
    gives = weight_part(pixels, keep, got, where, *sizes, True)
    keeps = weight_part(pixels, keep, got, where, *sizes, False)
    scale = 1.0 / math.sqrt(tokens * seq_size * fsdp_size)
    mine = {("seq", b): bit_at(seq_index, b) for b in seq_bits}
    mine |= {("chip", b): bit_at(chip, b) for b in chip_bits}
    seq_labels = [("seq", b) for b in seq_bits]
    chip_labels = [("chip", b) for b in chip_bits]
    orders = [order + chip_labels[:-1] for order in (seq_labels, seq_labels[::-1])]
    chains = [
        halving(
            gives[:2],
            keeps[:2],
            chip_labels[:-1][::-1] + seq_labels[::-1],
            orders,
            mine,
            chip_labels[-1],
        ),
        halving(
            gives[2:],
            keeps[2:],
            chip_labels[::-1] + seq_labels[::-1],
            [chip_labels + seq_labels],
            mine,
        ),
        all_sum(chan_part, [route_of(label) for label in seq_labels + chip_labels]),
    ]
    last_round = len(seq_bits) + len(chip_bits) - 1

    def left_pixels(ready, _):
        inputs, ready = together(d_stem, ready)
        return ready, pixel_grads(inputs, all_pairs, places, 0, middle)

    (plane, line, chan), grad_rows = in_rounds(chains, {last_round: left_pixels})
    rows_mine = finish([plane, line], scale)
    d_stem, rows_mine = together(d_stem, rows_mine)
    pieces = [rows_mine] + [swapped(rows_mine, o, 0) for o in range(1, seq_size)]
    grad_rows = pixel_grads(d_stem, all_pairs, places, middle, width, grad_rows)
    pieces, grad_rows = together(pieces, grad_rows)
    grad_weight = unpacked(pieces, seq_index, width, share, line_share)
    first = fsdp_index * shard
    grad_channels = scale * (
        lax.dynamic_slice_in_dim(chan[0], first, shard, axis=1)[:6]
        + lax.dynamic_slice_in_dim(chan[1], first, shard, axis=1)[:6]
    )
    return (features[None], grad_rows[None], grad_weight, grad_channels)


def solution(mesh):
    in_specs = (
        P("fsdp", "seq", None),
        P("fsdp", "seq"),
        P("fsdp", None),
        P("fsdp", None),
        P("fsdp"),
        P(None, "fsdp"),
        P("fsdp", "seq", None),
    )
    out_specs = (P("fsdp", "seq", None), P("fsdp", "seq", None), P("fsdp", None), P(None, "fsdp"))
    return jax.shard_map(shards, mesh=mesh, in_specs=in_specs, out_specs=out_specs, check_vma=False)
```

```python
import functools
import math

import jax
import jax.numpy as jnp
from jax import lax
from jax.experimental import pallas as pl
from jax.experimental.pallas import tpu as pltpu
from jax.sharding import PartitionSpec as P

EPSILON = 1e-06
BF16 = jnp.bfloat16
F32 = jnp.float32
LANES = 128
AXES = ("seq", "fsdp")


def round_up(value, unit):
    return (value + unit - 1) // unit * unit


def kernel_params(mebibytes):
    return pltpu.CompilerParams(vmem_limit_bytes=mebibytes * 1024 * 1024)


def sent(value, route):
    seq_size, fsdp_size = lax.axis_size("seq"), lax.axis_size("fsdp")
    pairs = []
    for s in range(seq_size):
        for f in range(fsdp_size):
            target = route(s, f)
            if target is not None:
                pairs.append((s * fsdp_size + f, target[0] * fsdp_size + target[1]))
    return lax.ppermute(value, AXES, pairs)


def swapped(value, seq_bits, fsdp_bits):
    return sent(value, lambda s, f: (s ^ seq_bits, f ^ fsdp_bits))


def together(*values):
    flat, tree = jax.tree.flatten(values)
    return jax.tree.unflatten(tree, lax.optimization_barrier(tuple(flat)))


def bits_of(size):
    return [1 << i for i in range(size.bit_length() - 1)]


def by_position(pieces, me):
    stack = jnp.stack(pieces, axis=0)
    count = len(pieces)
    tail = stack.shape[1:]
    for bit in bits_of(count):
        view = stack.reshape((count // (2 * bit), 2, bit) + tail)
        flipped = jnp.concatenate([view[:, 1:], view[:, :1]], axis=1)
        stack = jnp.where((me & bit) != 0, flipped, view).reshape((count,) + tail)
    return stack


def outbox_kernel(order_ref, spot_ref, frames_ref, *out_refs):
    rows, width = frames_ref.shape[1:]
    for peer, out in enumerate(out_refs):
        capacity, _, padded = out.shape
        lane = lax.broadcasted_iota(jnp.int32, (rows, LANES), 1) + (padded - LANES)
        for k in range(capacity):
            spot = spot_ref[peer * capacity + k]
            out[k, :, padded - LANES :] = jnp.where(lane == width, spot, 0.0).astype(BF16)
            out[k, :, :width] = frames_ref[order_ref[peer * capacity + k]]


def place_kernel(pick_ref, frames_ref, *refs):
    inbox, (out, head, tail) = refs[:-3], refs[-3:]
    slots, rows, width = frames_ref.shape
    total, padded = out.shape
    tokens = slots * rows
    capacity = inbox[0].shape[0]
    out[:tokens, padded - LANES :] = jnp.zeros((tokens, LANES), out.dtype)
    row = lax.broadcasted_iota(jnp.int32, (total - tokens, padded), 0)
    column = lax.broadcasted_iota(jnp.int32, (total - tokens, padded), 1)
    out[tokens:, :] = jnp.where((column == row + width) & (row < 6), 1.0, 0.0).astype(BF16)

    def one(p, carry):
        index = pick_ref[p]
        here = pl.ds(pl.multiple_of(p * rows, 16), rows)

        @pl.when(index < slots)
        def _():
            out[here, :width] = frames_ref[index]

        for peer, box in enumerate(inbox):
            first = slots + peer * capacity

            @pl.when((index >= first) & (index < first + capacity))
            def _():
                out[here, :width] = box[index - first, :, :width]

        return carry

    lax.fori_loop(0, slots, one, 0)
    head[...] = out[: head.shape[0]]
    tail[...] = out[tokens - tail.shape[0] : tokens]


def scalar_call(kernel, out_shape, scalars, arrays):
    return pl.pallas_call(
        kernel,
        grid_spec=pltpu.PrefetchScalarGridSpec(
            num_scalar_prefetch=len(scalars),
            grid=(),
            in_specs=[pl.BlockSpec(memory_space=pltpu.VMEM)] * len(arrays),
            out_specs=jax.tree.map(lambda _: pl.BlockSpec(memory_space=pltpu.VMEM), out_shape),
        ),
        out_shape=out_shape,
        compiler_params=kernel_params(60),
    )(*scalars, *arrays)


def outgoing(frames, destination, seq_index, seq_size, padded):
    slots, rows, _ = frames.shape
    capacity = 2 * slots // seq_size
    owner = (destination // slots) ^ seq_index
    rank = jnp.sum(
        ((owner[:, None] == owner[None, :]) & (destination[None, :] < destination[:, None])).astype(
            jnp.int32
        ),
        axis=1,
    )
    peers = jnp.arange(1, seq_size, dtype=jnp.int32)
    places = jnp.arange(capacity, dtype=jnp.int32)
    hit = (owner[None, None, :] == peers[:, None, None]) & (
        rank[None, None, :] == places[None, :, None]
    )
    order = jnp.sum(jnp.where(hit, jnp.arange(slots, dtype=jnp.int32), 0), axis=2).reshape(-1)
    spot = jnp.sum(jnp.where(hit, destination % slots + 1, 0), axis=2).reshape(-1) - 1
    return scalar_call(
        outbox_kernel,
        [jax.ShapeDtypeStruct((capacity, rows, padded), BF16)] * (seq_size - 1),
        [order, spot.astype(F32)],
        [frames],
    )


def arrivals(destination, spots, seq_index):
    slots = destination.shape[0]
    numbers = jnp.arange(slots, dtype=jnp.int32)
    local = (destination == seq_index * slots + numbers[:, None]).astype(jnp.int32)
    boxed = (spots.astype(jnp.int32).reshape(-1) == numbers[:, None]).astype(jnp.int32)
    places = slots + jnp.arange(boxed.shape[1], dtype=jnp.int32)
    return jnp.sum(local * numbers, axis=1) + jnp.sum(boxed * places, axis=1)


def chain_step(rising, falling, k, chips):
    return (
        sent(rising, lambda s, f: (s, f + 2) if k - 1 <= f // 2 < chips - 1 else None),
        sent(falling, lambda s, f: (s, f - 2) if 0 < f // 2 <= chips - k else None),
    )


def chain_slot(rising, falling, k, chip, chips):
    low = chip < chips // 2
    far = jnp.maximum(chip, chips - 1 - chip)
    towards = jnp.where(low, 1, -1)
    options = [falling[k], rising[k]]
    which = jnp.where(low, 0, 1)
    origin = chip + towards * k
    for reach in range(chips // 2, k):
        which = jnp.where(far == reach, len(options) + jnp.where(low, 1, 0), which)
        options += [falling[k - reach], rising[k - reach]]
        origin = jnp.where(far == reach, chip - towards * (k - reach), origin)
    return options, which, origin


def chosen(options, which):
    value = options[0]
    for i, option in enumerate(options[1:], 1):
        value = jnp.where(which == i, option, value)
    return value


def load_weights(place_ref, shard_refs, weights, sems, by_chip):
    pairs = len(shard_refs) // 2
    shard = shard_refs[0].shape[0]
    core = place_ref[0]
    for k in range(pairs)[::-1]:
        for h in range(2):
            lane = core if h == 0 else 1 - core
            row = 2 * (place_ref[1 + k] if by_chip else k) + lane
            first = pl.multiple_of(row * shard, 16)
            pltpu.make_async_copy(
                shard_refs[2 * k + h], weights.at[pl.ds(first, shard), :], sems.at[row]
            ).start()


def wait_weights(shard_ref, weights, sems, pair):
    shard = shard_ref.shape[0]
    for row in (2 * pair, 2 * pair + 1):
        pltpu.make_async_copy(
            shard_ref, weights.at[pl.ds(row * shard, shard), :], sems.at[row]
        ).wait()


def pair_product(inputs, weights, first, count, store, squares):
    total = squares[...]
    for begin in range(0, count, 256):
        size = min(256, count - begin)
        result = lax.dot_general(
            inputs[...],
            weights[first + begin : first + begin + size, :],
            (((1,), (1,)), ((), ())),
            preferred_element_type=F32,
        )
        store(begin, size, result)
        for t in range(0, size, LANES):
            part = result[:, t : t + LANES]
            total = total + part * part
    squares[...] = total


def early_kernel(place_ref, rows_ref, *refs, pairs):
    shard_refs = refs[: 2 * pairs]
    acc_ref, squares, weights, sems = refs[2 * pairs :]
    group = acc_ref.shape[2]
    load_weights(place_ref, shard_refs, weights, sems, False)
    squares[...] = jnp.zeros_like(squares)
    for k in range(pairs):
        wait_weights(shard_refs[0], weights, sems, k)

        def store(begin, size, result, k=k):
            acc_ref[k, :, begin : begin + size] = result

        pair_product(rows_ref, weights, k * group, group, store, squares)


VMEM_SPEC = pl.BlockSpec(memory_space=pltpu.VMEM)
ANY_SPEC = pl.BlockSpec(memory_space=pl.ANY)


def stem_early(rows_in, shards, core_id):
    rows, padded = rows_in.shape
    pairs = len(shards) // 2
    group = 2 * shards[0].shape[0]
    return pl.pallas_call(
        functools.partial(early_kernel, pairs=pairs),
        grid_spec=pltpu.PrefetchScalarGridSpec(
            num_scalar_prefetch=1,
            grid=(),
            in_specs=[VMEM_SPEC] + [ANY_SPEC] * len(shards),
            out_specs=[VMEM_SPEC] * 2,
            scratch_shapes=[
                pltpu.VMEM((pairs * group, padded), BF16),
                pltpu.SemaphoreType.DMA((2 * pairs,)),
            ],
        ),
        out_shape=[
            jax.ShapeDtypeStruct((pairs, rows, group), F32),
            jax.ShapeDtypeStruct((rows, LANES), F32),
        ],
        compiler_params=kernel_params(24),
    )(core_id, rows_in, *shards)


def gate_of(value):
    return 0.5 * jnp.tanh(0.5 * value) + 0.5


def mixed_at(window, taps, mask_ref, first):
    total = window[0] * (taps[0] * mask_ref[first])
    for k in range(1, 5):
        total = total + window[k] * (taps[k] * mask_ref[first + k])
    return total


def layer_kernel(
    place_ref, mask_ref, main_ref, low_ref, high_ref, cot_ref, cot_low_ref, cot_high_ref, *refs,
    pairs, late, slots, channels
):
    shard_refs, refs = refs[: 2 * (pairs + late)], refs[2 * (pairs + late) :]
    if pairs:
        early_ref, early_squares, refs = refs[0], refs[1], refs[2:]
    feat_ref, stem_ref, give_ref, keep_ref = refs[:4]
    weights, rows_all, acc, cots, feats, d_stem, lanes_of_core, gated, slopes, squares, inverse = refs[4:15]
    part_ref, sems, in_sems, cot_sems, out_sems, stem_sems = refs[15:]
    group = 2 * shard_refs[0].shape[0]
    chips = channels // group
    tokens = cot_ref.shape[0]
    rows = tokens // slots
    halo, edge = low_ref.shape[0], cot_low_ref.shape[0]
    own_row = 2 * halo
    body = own_row + tokens
    core = place_ref[0]
    load_weights(place_ref, shard_refs, weights, sems, not pairs)
    if pairs:
        for k in range(pairs):
            lanes = pl.ds(pl.multiple_of(place_ref[1 + k] * group, LANES), group)
            pltpu.make_async_copy(
                early_ref.at[k],
                acc.at[pl.ds(own_row, early_ref.shape[1]), lanes],
                in_sems.at[place_ref[1 + k]],
            ).start()
    parts = 4
    size = channels // parts
    cot_loads = []
    for i in range(parts):
        lanes = pl.ds(i * size, size)
        first = 0
        for h, ref in enumerate((cot_low_ref, cot_ref, cot_high_ref)):
            count = ref.shape[0]
            cot_loads.append(
                pltpu.make_async_copy(
                    ref.at[:, lanes], cots.at[pl.ds(first, count), lanes], cot_sems.at[i, h]
                )
            )
            first += count
    for copy in cot_loads:
        copy.start()
    rows_all[0:halo] = low_ref[...]
    rows_all[halo:own_row] = high_ref[...]
    rows_all[own_row:] = main_ref[...]
    squares[...] = jnp.zeros_like(squares)
    if pairs:
        squares[own_row:] = early_squares[...]
        for k in [pairs] + list(range(pairs)):
            count = rows_all.shape[0] if k == pairs else own_row
            wait_weights(shard_refs[0], weights, sems, k)

            def store(begin, width, result, k=k, count=count):
                first = pl.multiple_of(place_ref[1 + k] * group + begin, LANES)
                acc[0:count, pl.ds(first, width)] = result

            pair_product(
                rows_all.at[0:count], weights, k * group, group, store, squares.at[0:count]
            )
    else:
        for z in range(late):
            wait_weights(shard_refs[0], weights, sems, z)
        tile = 256

        def one(j, carry):
            first = pl.multiple_of(j * tile, tile)
            result = lax.dot_general(
                rows_all[...],
                weights[pl.ds(first, tile), :],
                (((1,), (1,)), ((), ())),
                preferred_element_type=F32,
            )
            acc[:, pl.ds(first, tile)] = result
            total = squares[...]
            for t in range(0, tile, LANES):
                total = total + result[:, t : t + LANES] * result[:, t : t + LANES]
            squares[...] = total
            return carry

        lax.fori_loop(0, channels // tile, one, 0)
    mean = jnp.sum(squares[...], axis=1, keepdims=True) / channels
    inverse[...] = jnp.broadcast_to(lax.rsqrt(mean + EPSILON), inverse.shape)
    squares[...] = jnp.zeros_like(squares)

    def rows_of_slot(i):
        edge_slots = halo // rows
        if i < edge_slots:
            first = i * rows
        elif i < edge_slots + slots:
            first = own_row + (i - edge_slots) * rows
        else:
            first = halo + (i - edge_slots - slots) * rows
        return slice(first, first + rows)

    def columns(t, carry):
        lanes = pl.ds(pl.multiple_of(t * LANES, LANES), LANES)
        gain = acc[body : body + 1, lanes]
        taps = [acc[body + 1 + k : body + 2 + k, lanes] for k in range(5)]

        def normed(i):
            here = rows_of_slot(i)
            return (acc[here, lanes] * inverse[here] * gain).astype(BF16).astype(F32)

        window = [normed(i) for i in range(4)]
        sums = [jnp.zeros((8, LANES), F32) for _ in range(5)]
        for i in range(slots + 4):
            window.append(normed(i + 4))
            mixed = mixed_at(window, taps, mask_ref, 5 * i)
            gate = gate_of(mixed)
            smooth = mixed * gate
            here = slice(i * rows, (i + 1) * rows)
            up = cots[here, lanes].astype(F32)
            slope = (up * (gate + smooth - smooth * gate)).astype(BF16).astype(F32)
            slopes[here] = slope
            if 2 <= i < slots + 2:
                own = slice((i - 2) * rows, (i - 1) * rows)
                stem = acc[rows_of_slot(i + 2), lanes]
                feats[own, lanes] = (stem + smooth).astype(BF16)
                for k in range(5):
                    product = (slope * window[k]).reshape(rows // 8, 8, LANES)
                    sums[k] = sums[k] + jnp.sum(product, axis=0) * mask_ref[5 * i + k]
            window = window[1:]
        for k in range(5):
            part_ref[1 + k : 2 + k, lanes] = jnp.sum(sums[k], axis=0, keepdims=True)
        part_ref[6:8, lanes] = jnp.zeros((2, LANES), F32)
        total = jnp.zeros((8, LANES), F32)
        for p in range(slots):
            window = [slopes[(p + o) * rows : (p + o + 1) * rows] for o in range(5)]
            own = slice(p * rows, (p + 1) * rows)
            here = rows_of_slot(p + 4)
            d_normed = mixed_at(window, taps[::-1], mask_ref, 5 * (p + 2))
            product = d_normed * (acc[here, lanes] * inverse[here])
            total = total + jnp.sum(product.reshape(rows // 8, 8, LANES), axis=0)
            gated[own, lanes] = d_normed * gain
            squares[own] = squares[own] + product * gain
        part_ref[0:1, lanes] = jnp.sum(total, axis=0, keepdims=True)
        return carry

    copies = []
    for i in range(parts):
        for copy in cot_loads[3 * i : 3 * i + 3]:
            copy.wait()
        if pairs:

            @pl.when(place_ref[1 + pairs] != i)
            def _(i=i):
                pltpu.make_async_copy(
                    early_ref.at[0],
                    acc.at[pl.ds(own_row, early_ref.shape[1]), pl.ds(i * group, group)],
                    in_sems.at[i],
                ).wait()

        lax.fori_loop(i * size // LANES, (i + 1) * size // LANES, columns, 0)
        lanes = pl.ds(i * size, size)
        copy = pltpu.make_async_copy(feats.at[:, lanes], feat_ref.at[:, lanes], out_sems.at[i])
        copy.start()
        copies.append(copy)
    mean = jnp.sum(squares[0:tokens], axis=1, keepdims=True) / channels
    squares[0:tokens] = jnp.broadcast_to(mean, (tokens, LANES))

    def finish_columns(t, carry):
        lanes = pl.ds(pl.multiple_of(t * LANES, LANES), LANES)
        inv = inverse[own_row:body]
        unit = acc[own_row:body, lanes] * inv
        value = cots[edge : edge + tokens, lanes].astype(F32) + inv * (
            gated[:, lanes] - unit * squares[0:tokens]
        )
        d_stem[:, lanes] = value.astype(BF16)
        return carry

    shard = group // 2
    room = lanes_of_core.shape[2] // chips
    steps = chips if group % LANES == 0 else 1
    for i in range(steps):
        lax.fori_loop(
            i * channels // steps // LANES, (i + 1) * channels // steps // LANES, finish_columns, 0
        )
        lanes = pl.ds(i * (channels // steps), channels // steps)
        copies.append(
            pltpu.make_async_copy(d_stem.at[:, lanes], stem_ref.at[:, lanes], stem_sems.at[i, 0])
        )
        copies[-1].start()
        for z in range(i * chips // steps, (i + 1) * chips // steps):
            for h in range(2):
                first = (2 * z + h) * shard
                part = part_ref[:, first : first + shard]
                rest = part - part.astype(BF16).astype(F32)
                lanes = slice(z * room, z * room + shard)
                lanes_of_core[h, :tokens, lanes] = d_stem[:, first : first + shard]
                lanes_of_core[h, tokens:, lanes] = jnp.concatenate([part, rest], axis=0).astype(BF16)
                if room > shard:
                    lanes_of_core[h, :, z * room + shard : (z + 1) * room] = jnp.zeros(
                        (tokens + 16, room - shard), BF16
                    )
        width = chips // steps * room
        lanes = pl.ds(i * width, width)
        for h, ref in enumerate((keep_ref, give_ref)):
            copies.append(
                pltpu.make_async_copy(
                    lanes_of_core.at[(core + h) % 2, :, lanes],
                    ref.at[:, lanes],
                    stem_sems.at[i, 1 + h],
                )
            )
            copies[-1].start()
    for copy in copies:
        copy.wait()


def layer(main, low, high, cot, cot_low, cot_high, shards, early, places, mask, slots, channels):
    tokens = cot.shape[0]
    padded = main.shape[1]
    halo, edge = low.shape[0], cot_low.shape[0]
    total = main.shape[0] + 2 * halo
    pairs = early[0].shape[0] if early else 0
    late = len(shards) // 2 - pairs
    shard = shards[0].shape[0]
    half = channels // (2 * shard) * round_up(shard, LANES)
    return pl.pallas_call(
        functools.partial(layer_kernel, pairs=pairs, late=late, slots=slots, channels=channels),
        grid_spec=pltpu.PrefetchScalarGridSpec(
            num_scalar_prefetch=2,
            grid=(),
            in_specs=[VMEM_SPEC] * 3
            + [ANY_SPEC] * 3
            + [ANY_SPEC] * len(shards)
            + ([ANY_SPEC, VMEM_SPEC] if pairs else []),
            out_specs=[ANY_SPEC] * 4,
            scratch_shapes=[
                pltpu.VMEM((channels, padded), BF16),
                pltpu.VMEM((total, padded), BF16),
                pltpu.VMEM((total, channels), F32),
                pltpu.VMEM((tokens + 2 * edge, channels), BF16),
                pltpu.VMEM((tokens, channels), BF16),
                pltpu.VMEM((tokens, channels), BF16),
                pltpu.VMEM((2, tokens + 16, half), BF16),
                pltpu.VMEM((tokens, channels), F32),
                pltpu.VMEM((tokens + 2 * edge, LANES), F32),
                pltpu.VMEM((total, LANES), F32),
                pltpu.VMEM((total, LANES), F32),
                pltpu.VMEM((8, channels), F32),
                pltpu.SemaphoreType.DMA((len(shards),)),
                pltpu.SemaphoreType.DMA((len(shards) // 2,)),
                pltpu.SemaphoreType.DMA((4, 3)),
                pltpu.SemaphoreType.DMA((4,)),
                pltpu.SemaphoreType.DMA((len(shards) // 2, 3)),
            ],
        ),
        out_shape=[
            jax.ShapeDtypeStruct((tokens, channels), BF16),
            jax.ShapeDtypeStruct((tokens, channels), BF16),
            jax.ShapeDtypeStruct((tokens + 16, half), BF16),
            jax.ShapeDtypeStruct((tokens + 16, half), BF16),
        ],
        compiler_params=kernel_params(60),
    )(places, mask, main, low, high, cot, cot_low, cot_high, *shards, *early)


def pixel_kernel(place_ref, d_stem_ref, *refs, chips, begin, tile):
    shard_refs, refs = refs[: 2 * chips], refs[2 * chips :]
    before = refs[0] if begin else None
    out_ref, weights, sems = refs[1:] if begin else refs
    width = out_ref.shape[1] - begin
    lanes = pl.ds(begin, weights.shape[1])
    load_weights(place_ref, [r.at[:, lanes] for r in shard_refs], weights, sems, True)
    for z in range(chips):
        wait_weights(shard_refs[0].at[:, lanes], weights, sems, z)
    if begin:
        out_ref[:, :begin] = before[...]
    for first in range(0, width, tile):
        size = min(tile, width - first)
        columns = slice(first, first + round_up(size, LANES))
        value = jnp.dot(d_stem_ref[...], weights[:, columns], preferred_element_type=F32)
        out_ref[:, begin + first : begin + first + size] = value[:, :size].astype(BF16)


def pixel_grads(d_stem, shards, places, begin, end, before=None):
    tokens, channels = d_stem.shape
    chips = len(shards) // 2
    lanes = round_up(end - begin, LANES)
    return pl.pallas_call(
        functools.partial(pixel_kernel, chips=chips, begin=begin, tile=256),
        grid_spec=pltpu.PrefetchScalarGridSpec(
            num_scalar_prefetch=1,
            grid=(),
            in_specs=[VMEM_SPEC]
            + [ANY_SPEC] * len(shards)
            + ([VMEM_SPEC] if begin else []),
            out_specs=VMEM_SPEC,
            scratch_shapes=[
                pltpu.VMEM((channels, lanes), BF16),
                pltpu.SemaphoreType.DMA((2 * chips,)),
            ],
        ),
        out_shape=jax.ShapeDtypeStruct((tokens, end), BF16),
        compiler_params=kernel_params(60),
    )(places, d_stem, *shards, *([before] if begin else []))


def turn_kernel(first_ref, second_ref, out_ref, *, tokens):
    height, depth = out_ref.shape
    padded = first_ref.shape[1]
    row = lax.broadcasted_iota(jnp.int32, (16, padded), 0) % 8
    column = lax.broadcasted_iota(jnp.int32, (16, padded), 1)
    extra = jnp.where((column == padded - 16 + row) & (row < 6), 1.0, 0.0).astype(BF16)
    out_ref[:, 2 * tokens + 32 :] = jnp.zeros((height, depth - 2 * tokens - 32), BF16)
    both = jnp.concatenate([first_ref[:tokens], extra, second_ref[:tokens], extra], axis=0)
    for m in range(0, height, LANES):
        count = min(LANES, height - m)
        if m < padded:
            out_ref[m : m + count, : 2 * tokens + 32] = both[:, m : m + LANES].T[:count]
        else:
            out_ref[m : m + count, :] = jnp.zeros((count, depth), BF16)


def turned(packed, packed_other, height, tokens):
    return pl.pallas_call(
        functools.partial(turn_kernel, tokens=tokens),
        in_specs=[VMEM_SPEC] * 2,
        out_specs=VMEM_SPEC,
        out_shape=jax.ShapeDtypeStruct((height, round_up(2 * tokens + 32, LANES)), BF16),
        compiler_params=kernel_params(16),
    )(packed, packed_other)


def halves_beside(value, shard):
    rows = value.shape[0] // 2
    return value[:rows, :shard], value[rows:, :shard]


def weight_kernel(where_ref, pixels_ref, keep_ref, got_ref, *refs, bits, share, line_share, shard, give):
    outs, (d_stem, left, line, sems, left_sems) = refs[:3], refs[3:]
    tokens = keep_ref.shape[0]
    seq_index, chip = where_ref[0], where_ref[1]
    seq_size = 2 * outs[0].shape[1]
    half = seq_size // 2
    chips = 2 * outs[0].shape[0]
    room = d_stem.shape[1] // chips
    arrive = [[] for _ in range(chips + 1)]
    for g, bit in enumerate(bits):
        mine = (seq_index // bit) % 2
        wanted = 1 - mine if give else mine
        for i in range(half):
            p = (i // bit) * (2 * bit) + i % bit + bit * wanted
            arrive[g * (chips // 2)].append(
                pltpu.make_async_copy(
                    pixels_ref.at[pl.ds(pl.multiple_of(p * share, 16), share), :],
                    left.at[g, pl.ds(i * share, share), :],
                    left_sems.at[g, i],
                )
            )
        for z in range(g * (chips // 2), (g + 1) * (chips // 2)):
            lanes = pl.ds(z * room, room)
            for h, ref in enumerate((keep_ref, got_ref)):
                arrive[z].append(
                    pltpu.make_async_copy(
                        ref.at[:, lanes],
                        d_stem.at[pl.ds(h * tokens, tokens), lanes],
                        sems.at[2 * z + h],
                    )
                )
    arrive[chips].append(
        pltpu.make_async_copy(
            pixels_ref.at[pl.ds(seq_size * share, line.shape[0]), :], line, sems.at[2 * chips]
        )
    )
    for copy in sum(arrive, []):
        copy.start()
    extra = d_stem.shape[0] - 2 * tokens
    d_stem[2 * tokens :, :] = jnp.zeros((extra, d_stem.shape[1]), BF16)

    def fill(out, value, count, rows):
        for i in range(count):
            low, high = halves_beside(value[i * rows : (i + 1) * rows], shard)
            out[i, :, :shard] = low.astype(out.dtype)
            out[i, :, shard:] = high.astype(out.dtype)

    for g in range(2):
        for z in range(chips // 2):
            for copy in arrive[g * (chips // 2) + z]:
                copy.wait()
            first = (g * (chips // 2) + z) * room
            value = jnp.dot(
                left[g], d_stem[:, first : first + room], preferred_element_type=F32
            )
            fill(outs[g].at[z], value, half, share)
    for copy in arrive[chips]:
        copy.wait()
    mine = chip % 2
    wanted = 1 - mine if give else mine
    for i in range(chips // 2):
        columns = pl.ds(pl.multiple_of((2 * i + wanted) * room, LANES), room)
        value = jnp.dot(line[...], d_stem[:, columns], preferred_element_type=F32)
        fill(outs[2].at[i], value, seq_size, line_share)


def weight_part(pixels, keep, got, where, chips, seq_size, shard, share, line_share, bits, give):
    half = keep.shape[1]
    height, depth = pixels.shape
    kind = BF16 if give else F32
    plane = jax.ShapeDtypeStruct((chips // 2, seq_size // 2, share // 2, 2 * shard), kind)
    line = jax.ShapeDtypeStruct((chips // 2, seq_size, line_share // 2, 2 * shard), kind)
    return pl.pallas_call(
        functools.partial(
            weight_kernel, bits=bits, share=share, line_share=line_share, shard=shard, give=give
        ),
        grid_spec=pltpu.PrefetchScalarGridSpec(
            num_scalar_prefetch=1,
            grid=(),
            in_specs=[ANY_SPEC] * 3,
            out_specs=[VMEM_SPEC] * 3,
            scratch_shapes=[
                pltpu.VMEM((depth, half), BF16),
                pltpu.VMEM((2, seq_size // 2 * share, depth), BF16),
                pltpu.VMEM((seq_size * line_share, depth), BF16),
                pltpu.SemaphoreType.DMA((2 * chips + 1,)),
                pltpu.SemaphoreType.DMA((2, seq_size // 2)),
            ],
        ),
        out_shape=[plane, plane, line],
        compiler_params=kernel_params(24 if give else 60),
    )(where, pixels, keep, got)


def bit_at(index, bit):
    return (index // bit) % 2


def fetched(at_ref, refs, buffers, sems, indices):
    copies = []
    for n, (ref, buffer, index) in enumerate(zip(refs, buffers, indices)):
        place = tuple(slice(None) if p is None else at_ref[p] for p in index)
        source = ref.at[place] if place else ref
        copies.append(pltpu.make_async_copy(source, buffer, sems.at[n]))
        copies[-1].start()
    return copies


def total_of(copies, buffers):
    total = None
    for copy, buffer in zip(copies, buffers):
        copy.wait()
        value = buffer[...].astype(F32)
        total = value if total is None else total + value
    return total


def sums_kernel(at_ref, *refs, plan, indices):
    count = len(indices)
    results = sum(2 if keep else 1 for _, _, keep in plan)
    ins, outs = refs[:count], refs[count : count + results]
    buffers = list(refs[count + results : 2 * count + results])
    stores = list(refs[2 * count + results : 2 * count + 2 * results])
    sems, out_sems = refs[2 * count + 2 * results :]
    copies = fetched(at_ref, ins, buffers, sems, indices)
    written = []

    def write(value):
        n = len(written)
        stores[n][...] = value.astype(stores[n].dtype)
        written.append(pltpu.make_async_copy(stores[n], outs[n], out_sems.at[n]))
        written[-1].start()

    for alternatives, selector, keep in plan:
        totals = []
        for n in alternatives:
            totals.append(total_of(copies[:n], buffers[:n]))
            copies, buffers = copies[n:], buffers[n:]
        if keep:
            upper = at_ref[selector] == 1
            write(jnp.where(upper, totals[0], totals[1]))
            write(jnp.where(upper, totals[1], totals[0]))
        elif len(totals) == 1:
            write(totals[0])
        else:
            write(jnp.stack(totals, axis=0))
    for copy in written:
        copy.wait()


def part_shape(array, index):
    return tuple(array.shape[d] for d, at in enumerate(index) if at is None) + tuple(
        array.shape[-2:]
    )


def sums(units):
    scalars, arrays, indices, buffers, outs, plan = [], [], [], [], [], []

    def scalar(value):
        scalars.append(value)
        return len(scalars) - 1

    for alternatives, selector, kind in units:
        for terms in alternatives:
            for array, index in terms:
                shape = part_shape(array, index)
                arrays.append(array)
                indices.append([None if at is None else scalar(at) for at in index])
                buffers.append(pltpu.VMEM(shape, array.dtype))
        keep = selector is not None
        plan.append(([len(t) for t in alternatives], scalar(selector) if keep else None, keep))
        stacked = () if keep or len(alternatives) == 1 else (len(alternatives),)
        outs.append(jax.ShapeDtypeStruct(stacked + shape, kind))
        if keep:
            outs.append(jax.ShapeDtypeStruct(shape, F32))
    if not scalars:
        scalars = [jnp.int32(0)]
    results = list(
        pl.pallas_call(
            functools.partial(sums_kernel, plan=plan, indices=indices),
            grid_spec=pltpu.PrefetchScalarGridSpec(
                num_scalar_prefetch=1,
                grid=(),
                in_specs=[ANY_SPEC] * len(arrays),
                out_specs=[ANY_SPEC] * len(outs),
                scratch_shapes=buffers
                + [pltpu.VMEM(o.shape, o.dtype) for o in outs]
                + [pltpu.SemaphoreType.DMA((len(arrays),)), pltpu.SemaphoreType.DMA((len(outs),))],
            ),
            out_shape=outs,
            compiler_params=kernel_params(60),
        )(jnp.stack([jnp.asarray(s, jnp.int32) for s in scalars]), *arrays)
    )
    return [(results.pop(0), results.pop(0) if keep else None) for _, _, keep in plan]


def at_own(terms, mine, done, label=None):
    def place(b):
        if isinstance(b, int):
            return b
        return 1 - mine[b] if b == label else mine[b] if b in done else None

    return [(array, [place(b) for b in labels]) for array, labels in terms]


def split_view(array, labels):
    return array.reshape((2,) * len(labels) + tuple(array.shape[-2:]))


def route_of(label):
    axis, bit = label
    if axis == "seq":
        return lambda s, f: (s ^ bit, f)
    return lambda s, f: (s, f ^ (2 * bit))


def without(labels, done):
    return [label for label in labels if label not in done]


def halving(gives, keeps, labels, orders, mine, last=None):
    came = yield gives, [route_of(order[0]) for order in orders]
    terms = []
    for keep, (arrived, _, _), order in zip(keeps, came, orders):
        rest = without(labels, order[:1])
        terms.append([(split_view(keep, rest), rest), (split_view(arrived, rest), rest)])
    for i in range(1, len(orders[0])):
        parts = [at_own(t, mine, order[:i], order[i]) for t, order in zip(terms, orders)]
        if len(orders) == 2 and orders[0][i] == orders[1][i]:
            ((arrived, _, _),) = yield [(parts, None, BF16)], [route_of(orders[0][i])]
            for g, (t, order) in enumerate(zip(terms, orders)):
                rest = without(labels, order[: i + 1])
                t.append((split_view(arrived, [g] + rest), [g] + rest))
            continue
        came = yield [([p], None, BF16) for p in parts], [route_of(order[i]) for order in orders]
        for t, (arrived, _, _), order in zip(terms, came, orders):
            rest = without(labels, order[: i + 1])
            t.append((split_view(arrived, rest), rest))
    final = [at_own(t, mine, order) for t, order in zip(terms, orders)]
    if last is not None:
        ((arrived, kept, _),) = yield [(final, mine[last], BF16)], [route_of(last)]
        final = [[(kept, []), (arrived, [])]]
    yield final[0], None


def in_rounds(chains, beside):
    waiting = [next(chain) for chain in chains]
    count, done = 0, None
    while any(routes is not None for _, routes in waiting):
        units = [u for values, routes in waiting if routes is not None for u in values]
        routes = [r for _, some in waiting if some is not None for r in some]
        ready = sums(units) if count else [(value, None) for value in units]
        came = [sent(give, route) for (give, _), route in zip(ready, routes)]
        if count in beside:
            ready, done = beside[count](ready, done)
            came, done = together(came, done)
        else:
            (came,) = together(came)
        count += 1
        arrived = [(value, kept, give) for value, (give, kept) in zip(came, ready)]
        for i, (values, some) in enumerate(waiting):
            if some is not None:
                mine, arrived = arrived[: len(values)], arrived[len(values) :]
                waiting[i] = chains[i].send(mine)
    return [values for values, _ in waiting], done


def unpack_kernel(at_ref, *refs, share, line_share, chan_row):
    pieces, (out_ref, chan_ref, rows_all) = refs[:-3], refs[-3:]
    shard, width = out_ref.shape
    for o, piece in enumerate(pieces):
        p = at_ref[0] ^ o
        begin = 0
        for base, count in ((p * share, share), (len(pieces) * share + p * line_share, line_share)):
            half = count // 2
            for h in range(2):
                first = pl.multiple_of(base + h * half, 16)
                rows_all[pl.ds(first, half), :] = piece[
                    begin : begin + half, h * shard : (h + 1) * shard
                ]
            begin += half
    for first in range(0, width, LANES):
        size = min(LANES, width - first)
        out_ref[:, first : first + size] = rows_all[first : first + LANES].T[:, :size]
    chan_ref[...] = rows_all[chan_row : chan_row + 16].astype(F32)[:6]


def unpacked(pieces, seq_index, width, share, line_share, chan_row):
    rows, lanes = pieces[0].shape
    shard = lanes // 2
    return pl.pallas_call(
        functools.partial(unpack_kernel, share=share, line_share=line_share, chan_row=chan_row),
        grid_spec=pltpu.PrefetchScalarGridSpec(
            num_scalar_prefetch=1,
            grid=(),
            in_specs=[VMEM_SPEC] * len(pieces),
            out_specs=[VMEM_SPEC] * 2,
            scratch_shapes=[pltpu.VMEM((2 * len(pieces) * rows, shard), BF16)],
        ),
        out_shape=[
            jax.ShapeDtypeStruct((shard, width), BF16),
            jax.ShapeDtypeStruct((6, shard), F32),
        ],
        compiler_params=kernel_params(60),
    )(seq_index.astype(jnp.int32).reshape(1), *pieces)


def finish_kernel(at_ref, *refs, counts, indices, scale):
    count = len(indices)
    ins, out_ref = refs[:count], refs[count]
    buffers, sems = list(refs[count + 1 : -1]), refs[-1]
    copies = fetched(at_ref, ins, buffers, sems, indices)
    begin = 0
    for n in counts:
        total = (total_of(copies[:n], buffers[:n]) * scale).astype(BF16)
        copies, buffers = copies[n:], buffers[n:]
        out_ref[begin : begin + total.shape[0], :] = total
        begin += total.shape[0]


def finish(chains, scale):
    scalars, arrays, indices, buffers, height = [], [], [], [], 0
    for terms in chains:
        for array, index in terms:
            indices.append(list(range(len(scalars), len(scalars) + len(index))))
            scalars += index
            arrays.append(array)
            buffers.append(pltpu.VMEM(tuple(array.shape[-2:]), array.dtype))
        height += terms[0][0].shape[-2]
    lanes = arrays[0].shape[-1]
    return pl.pallas_call(
        functools.partial(
            finish_kernel, counts=[len(t) for t in chains], indices=indices, scale=scale
        ),
        grid_spec=pltpu.PrefetchScalarGridSpec(
            num_scalar_prefetch=1,
            grid=(),
            in_specs=[ANY_SPEC] * len(arrays),
            out_specs=VMEM_SPEC,
            scratch_shapes=buffers + [pltpu.SemaphoreType.DMA((len(arrays),))],
        ),
        out_shape=jax.ShapeDtypeStruct((height, lanes), BF16),
        compiler_params=kernel_params(60),
    )(jnp.stack([jnp.asarray(s, jnp.int32) for s in scalars]), *arrays)


def shards(patches, send_slot, segments, stem_weight, norm_gain, conv_kernel, cotangent):
    seq_size, fsdp_size = lax.axis_size("seq"), lax.axis_size("fsdp")
    seq_index, fsdp_index = lax.axis_index("seq"), lax.axis_index("fsdp")
    chips, chip, core = fsdp_size // 2, fsdp_index // 2, fsdp_index % 2
    slots = send_slot.shape[1]
    tokens, width = patches.shape[1], patches.shape[2]
    rows = tokens // slots
    edge = 2 * rows
    shard = stem_weight.shape[0]
    channels = shard * fsdp_size
    padded = round_up(width + 6, LANES)
    capacity = 2 * slots // seq_size
    cot = cotangent[0]
    core_id = core.astype(jnp.int32).reshape(1)

    def following(s, f):
        return (s + 1, f) if s + 1 < seq_size else None

    def preceding(s, f):
        return (s - 1, f) if s > 0 else None

    own = jnp.concatenate(
        [
            stem_weight,
            norm_gain[:, None],
            conv_kernel.T,
            jnp.zeros((shard, padded - width - 6), BF16),
        ],
        axis=1,
    )
    own, cot, patches = together(own, cot, patches)
    tail, head = cot[tokens - edge :], cot[:edge]
    frames = patches[0].reshape(slots, rows, width)
    boxes = outgoing(frames, send_slot[0], seq_index, seq_size, padded)
    rising, falling = {0: own}, {0: own}
    own_core = swapped(own, 0, 1)
    boxes, own_core = together(boxes, own_core)
    inbox = [None] * (seq_size - 1)
    direct = [o for o in range(1, seq_size) if o.bit_count() % 2 == 1]
    others = [o for o in range(1, seq_size) if o.bit_count() % 2 == 0]
    split = 2 * shard % LANES == 0 and chips == 4
    lane_shards, core_shards, chip_of = [own], [own_core], [chip]
    early = []
    spots = [None] * (seq_size - 1)

    def arrive(numbers, boxes):
        for o, box in zip(numbers, boxes):
            inbox[o - 1], spots[o - 1] = box, box[:, 0, width]

    def add_shard(k, rising, falling):
        options, which, origin = chain_slot(rising, falling, k, chip, chips)
        lane_shards.append(chosen(options, which))
        core_shards.append(swapped(lane_shards[-1], 0, 1))
        chip_of.append(origin)

    for k in range(1, chips):
        if k < 3 or not split:
            rising[k], falling[k] = chain_step(rising[k - 1], falling[k - 1], k, chips)
        if k == 1:
            came = [swapped(boxes[o - 1], o, 0) for o in direct]
            rising, falling, came, boxes, tail, head = together(
                rising, falling, came, boxes, tail, head
            )
            arrive(direct, came)
        elif k == 2:
            came = [swapped(boxes[o - 1], o, 0) for o in others]
            cot_low = sent(tail, following)
            if split:
                rising[1], falling[1], spots = together(rising[1], falling[1], spots)
                add_shard(1, rising, falling)
                near = jnp.where(chip < chips // 2, rising[1], falling[1])
            rising, falling, cot_low, came, core_shards, lane_shards, spots, head = together(
                rising, falling, cot_low, came, core_shards, lane_shards, spots, head
            )
            arrive(others, came)
            cot_high = sent(head, preceding)
            pick = arrivals(send_slot[0], jnp.stack(spots, axis=0), seq_index)
            main, main_head, main_tail = scalar_call(
                place_kernel,
                [
                    jax.ShapeDtypeStruct((count, padded), BF16)
                    for count in (tokens + 16, 2 * edge, 2 * edge)
                ],
                [pick],
                [frames] + inbox,
            )
            if split:
                add_shard(2, rising, falling)
                final = sent(
                    lane_shards[2],
                    lambda s, f: (s, f + 2) if f // 2 == 2 else (s, f - 2) if f // 2 == 1 else None,
                )
                main, main_head, main_tail, lane_shards, core_shards = together(
                    main, main_head, main_tail, lane_shards, core_shards
                )
            low = sent(main_tail, following)
            high = sent(main_head, preceding)
        elif k == 3 and split:
            pairs = [v for both in zip(lane_shards, core_shards) for v in both]
            early_main, main_squares = stem_early(main, pairs, core_id)
            final, early_main, low, high, main, cot_high = together(
                final, early_main, low, high, main, cot_high
            )
            outer = (chip == 0) | (chip == chips - 1)
            lane_shards.append(jnp.where(outer, final, near))
            core_shards.append(swapped(lane_shards[-1], 0, 1))
            chip_of.append(jnp.where(outer, chips - 1 - chip, jnp.where(chip == 1, 0, chips - 1)))
        else:
            rising, falling = together(rising, falling)
    for k in range(len(lane_shards), chips):
        add_shard(k, rising, falling)
    height = round_up(width, 64 * seq_size)
    main_other = swapped(main, 0, 1)
    places = jnp.stack([core] + chip_of).astype(jnp.int32)
    all_pairs = [v for both in zip(lane_shards, core_shards) for v in both]
    if split:
        all_pairs, main_other = together(all_pairs, main_other)
        early = [early_main, main_squares]

    ids = segments[0]
    total_slots = ids.shape[0]
    centre = seq_index * slots + jnp.arange(-2, slots + 2, dtype=jnp.int32)
    near = centre[:, None] + jnp.arange(-2, 3, dtype=jnp.int32)[None, :]
    inside = (near >= 0) & (near < total_slots) & ((centre >= 0) & (centre < total_slots))[:, None]
    same = (
        ids[jnp.clip(near, 0, total_slots - 1)] == ids[jnp.clip(centre, 0, total_slots - 1)][:, None]
    )
    mask = (inside & same).astype(F32).reshape(-1)
    features, d_stem, give, keep = layer(
        main, low, high, cot, cot_low, cot_high, all_pairs, early, places, mask, slots, channels
    )
    got = swapped(give, 0, 1)
    pixels = turned(main, main_other, height, tokens)
    middle = round_up(width // 2, LANES)

    seq_bits = bits_of(seq_size)
    chip_bits = bits_of(chips)
    line_share = height // seq_size // 4 // 32 * 32
    share = height // seq_size - line_share
    where = jnp.stack([seq_index, chip]).astype(jnp.int32)
    first_bits = [seq_bits[0], seq_bits[-1]]
    sizes = (chips, seq_size, shard, share, line_share, first_bits)
    gives = weight_part(pixels, keep, got, where, *sizes, True)
    keeps = weight_part(pixels, keep, got, where, *sizes, False)
    scale = 1.0 / math.sqrt(tokens * seq_size * fsdp_size)
    mine = {("seq", b): bit_at(seq_index, b) for b in seq_bits}
    mine |= {("chip", b): bit_at(chip, b) for b in chip_bits}
    seq_labels = [("seq", b) for b in seq_bits]
    chip_labels = [("chip", b) for b in chip_bits]
    orders = [order + chip_labels[:-1] for order in (seq_labels, seq_labels[::-1])]
    chains = [
        halving(
            gives[:2],
            keeps[:2],
            chip_labels[:-1][::-1] + seq_labels[::-1],
            orders,
            mine,
            chip_labels[-1],
        ),
        halving(
            gives[2:],
            keeps[2:],
            chip_labels[::-1] + seq_labels[::-1],
            [chip_labels + seq_labels],
            mine,
        ),
    ]
    last_round = len(seq_bits) + len(chip_bits) - 1

    def left_pixels(ready, _):
        inputs, ready = together(d_stem, ready)
        return ready, pixel_grads(inputs, all_pairs, places, 0, middle)

    (plane, line), grad_rows = in_rounds(chains, {last_round: left_pixels})
    rows_mine = finish([plane, line], scale)
    d_stem, rows_mine = together(d_stem, rows_mine)
    pieces = [rows_mine] + [swapped(rows_mine, o, 0) for o in range(1, seq_size)]
    grad_rows = pixel_grads(d_stem, all_pairs, places, middle, width, grad_rows)
    pieces, grad_rows = together(pieces, grad_rows)
    grad_weight, grad_channels = unpacked(
        pieces, seq_index, width, share, line_share, padded - 16
    )
    return (features[None], grad_rows[None], grad_weight, grad_channels)


def solution(mesh):
    in_specs = (
        P("fsdp", "seq", None),
        P("fsdp", "seq"),
        P("fsdp", None),
        P("fsdp", None),
        P("fsdp"),
        P(None, "fsdp"),
        P("fsdp", "seq", None),
    )
    out_specs = (P("fsdp", "seq", None), P("fsdp", "seq", None), P("fsdp", None), P(None, "fsdp"))
    return jax.shard_map(shards, mesh=mesh, in_specs=in_specs, out_specs=out_specs, check_vma=False)
```

```python
import functools
import math

import jax
import jax.numpy as jnp
from jax import lax
from jax.experimental import pallas as pl
from jax.experimental.pallas import tpu as pltpu
from jax.sharding import PartitionSpec as P

EPSILON = 1e-06
BF16 = jnp.bfloat16
F32 = jnp.float32
LANES = 128
AXES = ("seq", "fsdp")


def round_up(value, unit):
    return (value + unit - 1) // unit * unit


def kernel_params(mebibytes):
    return pltpu.CompilerParams(vmem_limit_bytes=mebibytes * 1024 * 1024)


def sent(value, route):
    seq_size, fsdp_size = lax.axis_size("seq"), lax.axis_size("fsdp")
    pairs = []
    for s in range(seq_size):
        for f in range(fsdp_size):
            target = route(s, f)
            if target is not None:
                pairs.append((s * fsdp_size + f, target[0] * fsdp_size + target[1]))
    return lax.ppermute(value, AXES, pairs)


def swapped(value, seq_bits, fsdp_bits):
    return sent(value, lambda s, f: (s ^ seq_bits, f ^ fsdp_bits))


def together(*values):
    flat, tree = jax.tree.flatten(values)
    return jax.tree.unflatten(tree, lax.optimization_barrier(tuple(flat)))


def bits_of(size):
    return [1 << i for i in range(size.bit_length() - 1)]


def by_position(pieces, me):
    stack = jnp.stack(pieces, axis=0)
    count = len(pieces)
    tail = stack.shape[1:]
    for bit in bits_of(count):
        view = stack.reshape((count // (2 * bit), 2, bit) + tail)
        flipped = jnp.concatenate([view[:, 1:], view[:, :1]], axis=1)
        stack = jnp.where((me & bit) != 0, flipped, view).reshape((count,) + tail)
    return stack


def outbox_kernel(order_ref, spot_ref, frames_ref, *out_refs):
    rows, width = frames_ref.shape[1:]
    for peer, out in enumerate(out_refs):
        capacity, _, padded = out.shape
        lane = lax.broadcasted_iota(jnp.int32, (rows, LANES), 1) + (padded - LANES)
        for k in range(capacity):
            spot = spot_ref[peer * capacity + k]
            out[k, :, padded - LANES :] = jnp.where(lane == width, spot, 0.0).astype(BF16)
            out[k, :, :width] = frames_ref[order_ref[peer * capacity + k]]


def place_kernel(pick_ref, frames_ref, *refs):
    inbox, (out, head, tail) = refs[:-3], refs[-3:]
    slots, rows, width = frames_ref.shape
    total, padded = out.shape
    tokens = slots * rows
    capacity = inbox[0].shape[0]
    out[:tokens, padded - LANES :] = jnp.zeros((tokens, LANES), out.dtype)
    row = lax.broadcasted_iota(jnp.int32, (total - tokens, padded), 0)
    column = lax.broadcasted_iota(jnp.int32, (total - tokens, padded), 1)
    out[tokens:, :] = jnp.where((column == row + width) & (row < 6), 1.0, 0.0).astype(BF16)

    def one(p, carry):
        index = pick_ref[p]
        here = pl.ds(pl.multiple_of(p * rows, 16), rows)

        @pl.when(index < slots)
        def _():
            out[here, :width] = frames_ref[index]

        for peer, box in enumerate(inbox):
            first = slots + peer * capacity

            @pl.when((index >= first) & (index < first + capacity))
            def _():
                out[here, :width] = box[index - first, :, :width]

        return carry

    lax.fori_loop(0, slots, one, 0)
    head[...] = out[: head.shape[0]]
    tail[...] = out[tokens - tail.shape[0] : tokens]


def scalar_call(kernel, out_shape, scalars, arrays):
    return pl.pallas_call(
        kernel,
        grid_spec=pltpu.PrefetchScalarGridSpec(
            num_scalar_prefetch=len(scalars),
            grid=(),
            in_specs=[pl.BlockSpec(memory_space=pltpu.VMEM)] * len(arrays),
            out_specs=jax.tree.map(lambda _: pl.BlockSpec(memory_space=pltpu.VMEM), out_shape),
        ),
        out_shape=out_shape,
        compiler_params=kernel_params(60),
    )(*scalars, *arrays)


def outgoing(frames, destination, seq_index, seq_size, padded):
    slots, rows, _ = frames.shape
    capacity = 2 * slots // seq_size
    owner = (destination // slots) ^ seq_index
    rank = jnp.sum(
        ((owner[:, None] == owner[None, :]) & (destination[None, :] < destination[:, None])).astype(
            jnp.int32
        ),
        axis=1,
    )
    peers = jnp.arange(1, seq_size, dtype=jnp.int32)
    places = jnp.arange(capacity, dtype=jnp.int32)
    hit = (owner[None, None, :] == peers[:, None, None]) & (
        rank[None, None, :] == places[None, :, None]
    )
    order = jnp.sum(jnp.where(hit, jnp.arange(slots, dtype=jnp.int32), 0), axis=2).reshape(-1)
    spot = jnp.sum(jnp.where(hit, destination % slots + 1, 0), axis=2).reshape(-1) - 1
    return scalar_call(
        outbox_kernel,
        [jax.ShapeDtypeStruct((capacity, rows, padded), BF16)] * (seq_size - 1),
        [order, spot.astype(F32)],
        [frames],
    )


def arrivals(destination, spots, seq_index):
    slots = destination.shape[0]
    numbers = jnp.arange(slots, dtype=jnp.int32)
    local = (destination == seq_index * slots + numbers[:, None]).astype(jnp.int32)
    boxed = (spots.astype(jnp.int32).reshape(-1) == numbers[:, None]).astype(jnp.int32)
    places = slots + jnp.arange(boxed.shape[1], dtype=jnp.int32)
    return jnp.sum(local * numbers, axis=1) + jnp.sum(boxed * places, axis=1)


def chain_step(rising, falling, k, chips):
    return (
        sent(rising, lambda s, f: (s, f + 2) if k - 1 <= f // 2 < chips - 1 else None),
        sent(falling, lambda s, f: (s, f - 2) if 0 < f // 2 <= chips - k else None),
    )


def chain_slot(rising, falling, k, chip, chips):
    low = chip < chips // 2
    far = jnp.maximum(chip, chips - 1 - chip)
    towards = jnp.where(low, 1, -1)
    options = [falling[k], rising[k]]
    which = jnp.where(low, 0, 1)
    origin = chip + towards * k
    for reach in range(chips // 2, k):
        which = jnp.where(far == reach, len(options) + jnp.where(low, 1, 0), which)
        options += [falling[k - reach], rising[k - reach]]
        origin = jnp.where(far == reach, chip - towards * (k - reach), origin)
    return options, which, origin


def chosen(options, which):
    value = options[0]
    for i, option in enumerate(options[1:], 1):
        value = jnp.where(which == i, option, value)
    return value


def load_weights(place_ref, shard_refs, weights, sems, by_chip):
    pairs = len(shard_refs) // 2
    shard = shard_refs[0].shape[0]
    core = place_ref[0]
    for k in range(pairs)[::-1]:
        for h in range(2):
            lane = core if h == 0 else 1 - core
            row = 2 * (place_ref[1 + k] if by_chip else k) + lane
            first = pl.multiple_of(row * shard, 16)
            pltpu.make_async_copy(
                shard_refs[2 * k + h], weights.at[pl.ds(first, shard), :], sems.at[row]
            ).start()


def wait_weights(shard_ref, weights, sems, pair):
    shard = shard_ref.shape[0]
    for row in (2 * pair, 2 * pair + 1):
        pltpu.make_async_copy(
            shard_ref, weights.at[pl.ds(row * shard, shard), :], sems.at[row]
        ).wait()


def pair_product(inputs, weights, first, count, store, squares):
    total = squares[...]
    for begin in range(0, count, 256):
        size = min(256, count - begin)
        result = lax.dot_general(
            inputs[...],
            weights[first + begin : first + begin + size, :],
            (((1,), (1,)), ((), ())),
            preferred_element_type=F32,
        )
        store(begin, size, result)
        for t in range(0, size, LANES):
            part = result[:, t : t + LANES]
            total = total + part * part
    squares[...] = total


def early_kernel(place_ref, rows_ref, *refs, pairs):
    shard_refs = refs[: 2 * pairs]
    acc_ref, squares, weights, sems = refs[2 * pairs :]
    group = acc_ref.shape[2]
    load_weights(place_ref, shard_refs, weights, sems, False)
    squares[...] = jnp.zeros_like(squares)
    for k in range(pairs):
        wait_weights(shard_refs[0], weights, sems, k)

        def store(begin, size, result, k=k):
            acc_ref[k, :, begin : begin + size] = result

        pair_product(rows_ref, weights, k * group, group, store, squares)


VMEM_SPEC = pl.BlockSpec(memory_space=pltpu.VMEM)
ANY_SPEC = pl.BlockSpec(memory_space=pl.ANY)


def stem_early(rows_in, shards, core_id):
    rows, padded = rows_in.shape
    pairs = len(shards) // 2
    group = 2 * shards[0].shape[0]
    return pl.pallas_call(
        functools.partial(early_kernel, pairs=pairs),
        grid_spec=pltpu.PrefetchScalarGridSpec(
            num_scalar_prefetch=1,
            grid=(),
            in_specs=[VMEM_SPEC] + [ANY_SPEC] * len(shards),
            out_specs=[VMEM_SPEC] * 2,
            scratch_shapes=[
                pltpu.VMEM((pairs * group, padded), BF16),
                pltpu.SemaphoreType.DMA((2 * pairs,)),
            ],
        ),
        out_shape=[
            jax.ShapeDtypeStruct((pairs, rows, group), F32),
            jax.ShapeDtypeStruct((rows, LANES), F32),
        ],
        compiler_params=kernel_params(24),
    )(core_id, rows_in, *shards)


def gate_of(value):
    return 0.5 * jnp.tanh(0.5 * value) + 0.5


def mixed_at(window, taps, mask_ref, first):
    total = window[0] * (taps[0] * mask_ref[first])
    for k in range(1, 5):
        total = total + window[k] * (taps[k] * mask_ref[first + k])
    return total


def layer_kernel(
    place_ref, mask_ref, main_ref, low_ref, high_ref, cot_ref, cot_low_ref, cot_high_ref, *refs,
    pairs, late, slots, channels
):
    shard_refs, refs = refs[: 2 * (pairs + late)], refs[2 * (pairs + late) :]
    if pairs:
        early_ref, early_squares, refs = refs[0], refs[1], refs[2:]
    feat_ref, stem_ref, give_ref, keep_ref = refs[:4]
    weights, rows_all, acc, cots, feats, d_stem, lanes_of_core, gated, slopes, squares, inverse = refs[4:15]
    part_ref, sems, in_sems, cot_sems, out_sems, stem_sems = refs[15:]
    group = 2 * shard_refs[0].shape[0]
    chips = channels // group
    tokens = cot_ref.shape[0]
    rows = tokens // slots
    halo, edge = low_ref.shape[0], cot_low_ref.shape[0]
    own_row = 2 * halo
    body = own_row + tokens
    core = place_ref[0]
    load_weights(place_ref, shard_refs, weights, sems, not pairs)
    if pairs:
        for k in range(pairs):
            lanes = pl.ds(pl.multiple_of(place_ref[1 + k] * group, LANES), group)
            pltpu.make_async_copy(
                early_ref.at[k],
                acc.at[pl.ds(own_row, early_ref.shape[1]), lanes],
                in_sems.at[place_ref[1 + k]],
            ).start()
    parts = 4
    size = channels // parts
    cot_loads = []
    for i in range(parts):
        lanes = pl.ds(i * size, size)
        first = 0
        for h, ref in enumerate((cot_low_ref, cot_ref, cot_high_ref)):
            count = ref.shape[0]
            cot_loads.append(
                pltpu.make_async_copy(
                    ref.at[:, lanes], cots.at[pl.ds(first, count), lanes], cot_sems.at[i, h]
                )
            )
            first += count
    for copy in cot_loads:
        copy.start()
    rows_all[0:halo] = low_ref[...]
    rows_all[halo:own_row] = high_ref[...]
    rows_all[own_row:] = main_ref[...]
    squares[...] = jnp.zeros_like(squares)
    if pairs:
        squares[own_row:] = early_squares[...]
        for k in [pairs] + list(range(pairs)):
            count = rows_all.shape[0] if k == pairs else own_row
            wait_weights(shard_refs[0], weights, sems, k)

            def store(begin, width, result, k=k, count=count):
                first = pl.multiple_of(place_ref[1 + k] * group + begin, LANES)
                acc[0:count, pl.ds(first, width)] = result

            pair_product(
                rows_all.at[0:count], weights, k * group, group, store, squares.at[0:count]
            )
    else:
        for z in range(late):
            wait_weights(shard_refs[0], weights, sems, z)
        tile = 256

        def one(j, carry):
            first = pl.multiple_of(j * tile, tile)
            result = lax.dot_general(
                rows_all[...],
                weights[pl.ds(first, tile), :],
                (((1,), (1,)), ((), ())),
                preferred_element_type=F32,
            )
            acc[:, pl.ds(first, tile)] = result
            total = squares[...]
            for t in range(0, tile, LANES):
                total = total + result[:, t : t + LANES] * result[:, t : t + LANES]
            squares[...] = total
            return carry

        lax.fori_loop(0, channels // tile, one, 0)
    mean = jnp.sum(squares[...], axis=1, keepdims=True) / channels
    inverse[...] = jnp.broadcast_to(lax.rsqrt(mean + EPSILON), inverse.shape)
    squares[...] = jnp.zeros_like(squares)

    def rows_of_slot(i):
        edge_slots = halo // rows
        if i < edge_slots:
            first = i * rows
        elif i < edge_slots + slots:
            first = own_row + (i - edge_slots) * rows
        else:
            first = halo + (i - edge_slots - slots) * rows
        return slice(first, first + rows)

    def columns(t, carry):
        lanes = pl.ds(pl.multiple_of(t * LANES, LANES), LANES)
        gain = acc[body : body + 1, lanes]
        taps = [acc[body + 1 + k : body + 2 + k, lanes] for k in range(5)]

        def normed(i):
            here = rows_of_slot(i)
            return (acc[here, lanes] * inverse[here] * gain).astype(BF16).astype(F32)

        window = [normed(i) for i in range(4)]
        sums = [jnp.zeros((8, LANES), F32) for _ in range(5)]
        for i in range(slots + 4):
            window.append(normed(i + 4))
            mixed = mixed_at(window, taps, mask_ref, 5 * i)
            gate = gate_of(mixed)
            smooth = mixed * gate
            here = slice(i * rows, (i + 1) * rows)
            up = cots[here, lanes].astype(F32)
            slope = (up * (gate + smooth - smooth * gate)).astype(BF16).astype(F32)
            slopes[here] = slope
            if 2 <= i < slots + 2:
                own = slice((i - 2) * rows, (i - 1) * rows)
                stem = acc[rows_of_slot(i + 2), lanes]
                feats[own, lanes] = (stem + smooth).astype(BF16)
                for k in range(5):
                    product = (slope * window[k]).reshape(rows // 8, 8, LANES)
                    sums[k] = sums[k] + jnp.sum(product, axis=0) * mask_ref[5 * i + k]
            window = window[1:]
        for k in range(5):
            part_ref[1 + k : 2 + k, lanes] = jnp.sum(sums[k], axis=0, keepdims=True)
        part_ref[6:8, lanes] = jnp.zeros((2, LANES), F32)
        total = jnp.zeros((8, LANES), F32)
        for p in range(slots):
            window = [slopes[(p + o) * rows : (p + o + 1) * rows] for o in range(5)]
            own = slice(p * rows, (p + 1) * rows)
            here = rows_of_slot(p + 4)
            d_normed = mixed_at(window, taps[::-1], mask_ref, 5 * (p + 2))
            product = d_normed * (acc[here, lanes] * inverse[here])
            total = total + jnp.sum(product.reshape(rows // 8, 8, LANES), axis=0)
            gated[own, lanes] = d_normed * gain
            squares[own] = squares[own] + product * gain
        part_ref[0:1, lanes] = jnp.sum(total, axis=0, keepdims=True)
        return carry

    copies = []
    for i in range(parts):
        for copy in cot_loads[3 * i : 3 * i + 3]:
            copy.wait()
        if pairs:

            @pl.when(place_ref[1 + pairs] != i)
            def _(i=i):
                pltpu.make_async_copy(
                    early_ref.at[0],
                    acc.at[pl.ds(own_row, early_ref.shape[1]), pl.ds(i * group, group)],
                    in_sems.at[i],
                ).wait()

        lax.fori_loop(i * size // LANES, (i + 1) * size // LANES, columns, 0)
        lanes = pl.ds(i * size, size)
        copy = pltpu.make_async_copy(feats.at[:, lanes], feat_ref.at[:, lanes], out_sems.at[i])
        copy.start()
        copies.append(copy)
    mean = jnp.sum(squares[0:tokens], axis=1, keepdims=True) / channels
    squares[0:tokens] = jnp.broadcast_to(mean, (tokens, LANES))

    def finish_columns(t, carry):
        lanes = pl.ds(pl.multiple_of(t * LANES, LANES), LANES)
        inv = inverse[own_row:body]
        unit = acc[own_row:body, lanes] * inv
        value = cots[edge : edge + tokens, lanes].astype(F32) + inv * (
            gated[:, lanes] - unit * squares[0:tokens]
        )
        d_stem[:, lanes] = value.astype(BF16)
        return carry

    shard = group // 2
    room = lanes_of_core.shape[2] // chips
    steps = chips if group % LANES == 0 else 1
    for i in range(steps):
        lax.fori_loop(
            i * channels // steps // LANES, (i + 1) * channels // steps // LANES, finish_columns, 0
        )
        lanes = pl.ds(i * (channels // steps), channels // steps)
        copies.append(
            pltpu.make_async_copy(d_stem.at[:, lanes], stem_ref.at[:, lanes], stem_sems.at[i, 0])
        )
        copies[-1].start()
        for z in range(i * chips // steps, (i + 1) * chips // steps):
            for h in range(2):
                first = (2 * z + h) * shard
                part = part_ref[:, first : first + shard]
                rest = part - part.astype(BF16).astype(F32)
                lanes = slice(z * room, z * room + shard)
                lanes_of_core[h, :tokens, lanes] = d_stem[:, first : first + shard]
                lanes_of_core[h, tokens:, lanes] = jnp.concatenate([part, rest], axis=0).astype(BF16)
                if room > shard:
                    lanes_of_core[h, :, z * room + shard : (z + 1) * room] = jnp.zeros(
                        (tokens + 16, room - shard), BF16
                    )
        width = chips // steps * room
        lanes = pl.ds(i * width, width)
        for h, ref in enumerate((keep_ref, give_ref)):
            copies.append(
                pltpu.make_async_copy(
                    lanes_of_core.at[(core + h) % 2, :, lanes],
                    ref.at[:, lanes],
                    stem_sems.at[i, 1 + h],
                )
            )
            copies[-1].start()
    for copy in copies:
        copy.wait()


def layer(main, low, high, cot, cot_low, cot_high, shards, early, places, mask, slots, channels):
    tokens = cot.shape[0]
    padded = main.shape[1]
    halo, edge = low.shape[0], cot_low.shape[0]
    total = main.shape[0] + 2 * halo
    pairs = early[0].shape[0] if early else 0
    late = len(shards) // 2 - pairs
    shard = shards[0].shape[0]
    half = channels // (2 * shard) * round_up(shard, LANES)
    return pl.pallas_call(
        functools.partial(layer_kernel, pairs=pairs, late=late, slots=slots, channels=channels),
        grid_spec=pltpu.PrefetchScalarGridSpec(
            num_scalar_prefetch=2,
            grid=(),
            in_specs=[VMEM_SPEC] * 3
            + [ANY_SPEC] * 3
            + [ANY_SPEC] * len(shards)
            + ([ANY_SPEC, VMEM_SPEC] if pairs else []),
            out_specs=[ANY_SPEC] * 4,
            scratch_shapes=[
                pltpu.VMEM((channels, padded), BF16),
                pltpu.VMEM((total, padded), BF16),
                pltpu.VMEM((total, channels), F32),
                pltpu.VMEM((tokens + 2 * edge, channels), BF16),
                pltpu.VMEM((tokens, channels), BF16),
                pltpu.VMEM((tokens, channels), BF16),
                pltpu.VMEM((2, tokens + 16, half), BF16),
                pltpu.VMEM((tokens, channels), F32),
                pltpu.VMEM((tokens + 2 * edge, LANES), F32),
                pltpu.VMEM((total, LANES), F32),
                pltpu.VMEM((total, LANES), F32),
                pltpu.VMEM((8, channels), F32),
                pltpu.SemaphoreType.DMA((len(shards),)),
                pltpu.SemaphoreType.DMA((len(shards) // 2,)),
                pltpu.SemaphoreType.DMA((4, 3)),
                pltpu.SemaphoreType.DMA((4,)),
                pltpu.SemaphoreType.DMA((len(shards) // 2, 3)),
            ],
        ),
        out_shape=[
            jax.ShapeDtypeStruct((tokens, channels), BF16),
            jax.ShapeDtypeStruct((tokens, channels), BF16),
            jax.ShapeDtypeStruct((tokens + 16, half), BF16),
            jax.ShapeDtypeStruct((tokens + 16, half), BF16),
        ],
        compiler_params=kernel_params(60),
    )(places, mask, main, low, high, cot, cot_low, cot_high, *shards, *early)


def pixel_kernel(place_ref, d_stem_ref, *refs, chips, begin, tile):
    shard_refs, refs = refs[: 2 * chips], refs[2 * chips :]
    before = refs[0] if begin else None
    out_ref, weights, sems = refs[1:] if begin else refs
    width = out_ref.shape[1] - begin
    lanes = pl.ds(begin, weights.shape[1])
    load_weights(place_ref, [r.at[:, lanes] for r in shard_refs], weights, sems, True)
    for z in range(chips):
        wait_weights(shard_refs[0].at[:, lanes], weights, sems, z)
    if begin:
        out_ref[:, :begin] = before[...]
    for first in range(0, width, tile):
        size = min(tile, width - first)
        columns = slice(first, first + round_up(size, LANES))
        value = jnp.dot(d_stem_ref[...], weights[:, columns], preferred_element_type=F32)
        out_ref[:, begin + first : begin + first + size] = value[:, :size].astype(BF16)


def pixel_grads(d_stem, shards, places, begin, end, before=None):
    tokens, channels = d_stem.shape
    chips = len(shards) // 2
    lanes = round_up(end - begin, LANES)
    return pl.pallas_call(
        functools.partial(pixel_kernel, chips=chips, begin=begin, tile=256),
        grid_spec=pltpu.PrefetchScalarGridSpec(
            num_scalar_prefetch=1,
            grid=(),
            in_specs=[VMEM_SPEC]
            + [ANY_SPEC] * len(shards)
            + ([VMEM_SPEC] if begin else []),
            out_specs=VMEM_SPEC,
            scratch_shapes=[
                pltpu.VMEM((channels, lanes), BF16),
                pltpu.SemaphoreType.DMA((2 * chips,)),
            ],
        ),
        out_shape=jax.ShapeDtypeStruct((tokens, end), BF16),
        compiler_params=kernel_params(60),
    )(places, d_stem, *shards, *([before] if begin else []))


def turn_kernel(first_ref, second_ref, out_ref, *, tokens):
    height, depth = out_ref.shape
    padded = first_ref.shape[1]
    row = lax.broadcasted_iota(jnp.int32, (16, padded), 0) % 8
    column = lax.broadcasted_iota(jnp.int32, (16, padded), 1)
    extra = jnp.where((column == padded - 16 + row) & (row < 6), 1.0, 0.0).astype(BF16)
    out_ref[:, 2 * tokens + 32 :] = jnp.zeros((height, depth - 2 * tokens - 32), BF16)
    both = jnp.concatenate([first_ref[:tokens], extra, second_ref[:tokens], extra], axis=0)
    for m in range(0, height, LANES):
        count = min(LANES, height - m)
        if m < padded:
            out_ref[m : m + count, : 2 * tokens + 32] = both[:, m : m + LANES].T[:count]
        else:
            out_ref[m : m + count, :] = jnp.zeros((count, depth), BF16)


def turned(packed, packed_other, height, tokens):
    return pl.pallas_call(
        functools.partial(turn_kernel, tokens=tokens),
        in_specs=[VMEM_SPEC] * 2,
        out_specs=VMEM_SPEC,
        out_shape=jax.ShapeDtypeStruct((height, round_up(2 * tokens + 32, LANES)), BF16),
        compiler_params=kernel_params(16),
    )(packed, packed_other)


def halves_beside(value, shard):
    rows = value.shape[0] // 2
    return value[:rows, :shard], value[rows:, :shard]


def weight_kernel(where_ref, pixels_ref, keep_ref, got_ref, *refs, bits, share, line_share, shard, give):
    outs, (d_stem, left, line, sems, left_sems) = refs[:3], refs[3:]
    tokens = keep_ref.shape[0]
    seq_index, chip = where_ref[0], where_ref[1]
    seq_size = 2 * outs[0].shape[1]
    half = seq_size // 2
    chips = 2 * outs[0].shape[0]
    room = d_stem.shape[1] // chips
    arrive = [[] for _ in range(chips + 1)]
    for g, bit in enumerate(bits):
        mine = (seq_index // bit) % 2
        wanted = 1 - mine if give else mine
        for i in range(half):
            p = (i // bit) * (2 * bit) + i % bit + bit * wanted
            arrive[g * (chips // 2)].append(
                pltpu.make_async_copy(
                    pixels_ref.at[pl.ds(pl.multiple_of(p * share, 16), share), :],
                    left.at[g, pl.ds(i * share, share), :],
                    left_sems.at[g, i],
                )
            )
        for z in range(g * (chips // 2), (g + 1) * (chips // 2)):
            lanes = pl.ds(z * room, room)
            for h, ref in enumerate((keep_ref, got_ref)):
                arrive[z].append(
                    pltpu.make_async_copy(
                        ref.at[:, lanes],
                        d_stem.at[pl.ds(h * tokens, tokens), lanes],
                        sems.at[2 * z + h],
                    )
                )
    arrive[chips].append(
        pltpu.make_async_copy(
            pixels_ref.at[pl.ds(seq_size * share, line.shape[0]), :], line, sems.at[2 * chips]
        )
    )
    for copy in sum(arrive, []):
        copy.start()
    extra = d_stem.shape[0] - 2 * tokens
    d_stem[2 * tokens :, :] = jnp.zeros((extra, d_stem.shape[1]), BF16)

    def fill(out, value, count, rows):
        for i in range(count):
            low, high = halves_beside(value[i * rows : (i + 1) * rows], shard)
            out[i, :, :shard] = low.astype(out.dtype)
            out[i, :, shard:] = high.astype(out.dtype)

    for g in range(2):
        for z in range(chips // 2):
            for copy in arrive[g * (chips // 2) + z]:
                copy.wait()
            first = (g * (chips // 2) + z) * room
            value = jnp.dot(
                left[g], d_stem[:, first : first + room], preferred_element_type=F32
            )
            fill(outs[g].at[z], value, half, share)
    for copy in arrive[chips]:
        copy.wait()
    mine = chip % 2
    wanted = 1 - mine if give else mine
    for i in range(chips // 2):
        columns = pl.ds(pl.multiple_of((2 * i + wanted) * room, LANES), room)
        value = jnp.dot(line[...], d_stem[:, columns], preferred_element_type=F32)
        fill(outs[2].at[i], value, seq_size, line_share)


def weight_part(pixels, keep, got, where, chips, seq_size, shard, share, line_share, bits, give):
    half = keep.shape[1]
    height, depth = pixels.shape
    kind = BF16 if give else F32
    plane = jax.ShapeDtypeStruct((chips // 2, seq_size // 2, share // 2, 2 * shard), kind)
    line = jax.ShapeDtypeStruct((chips // 2, seq_size, line_share // 2, 2 * shard), kind)
    return pl.pallas_call(
        functools.partial(
            weight_kernel, bits=bits, share=share, line_share=line_share, shard=shard, give=give
        ),
        grid_spec=pltpu.PrefetchScalarGridSpec(
            num_scalar_prefetch=1,
            grid=(),
            in_specs=[ANY_SPEC] * 3,
            out_specs=[VMEM_SPEC] * 3,
            scratch_shapes=[
                pltpu.VMEM((depth, half), BF16),
                pltpu.VMEM((2, seq_size // 2 * share, depth), BF16),
                pltpu.VMEM((seq_size * line_share, depth), BF16),
                pltpu.SemaphoreType.DMA((2 * chips + 1,)),
                pltpu.SemaphoreType.DMA((2, seq_size // 2)),
            ],
        ),
        out_shape=[plane, plane, line],
        compiler_params=kernel_params(24),
    )(where, pixels, keep, got)


def bit_at(index, bit):
    return (index // bit) % 2


def fetched(at_ref, refs, buffers, sems, indices):
    copies = []
    for n, (ref, buffer, index) in enumerate(zip(refs, buffers, indices)):
        place = tuple(slice(None) if p is None else at_ref[p] for p in index)
        source = ref.at[place] if place else ref
        copies.append(pltpu.make_async_copy(source, buffer, sems.at[n]))
        copies[-1].start()
    return copies


def total_of(copies, buffers):
    total = None
    for copy, buffer in zip(copies, buffers):
        copy.wait()
        value = buffer[...].astype(F32)
        total = value if total is None else total + value
    return total


def sums_kernel(at_ref, *refs, plan, indices):
    count = len(indices)
    results = sum(2 if keep else 1 for _, _, keep in plan)
    ins, outs = refs[:count], refs[count : count + results]
    buffers = list(refs[count + results : 2 * count + results])
    stores = list(refs[2 * count + results : 2 * count + 2 * results])
    sems, out_sems = refs[2 * count + 2 * results :]
    copies = fetched(at_ref, ins, buffers, sems, indices)
    written = []

    def write(value):
        n = len(written)
        stores[n][...] = value.astype(stores[n].dtype)
        written.append(pltpu.make_async_copy(stores[n], outs[n], out_sems.at[n]))
        written[-1].start()

    for alternatives, selector, keep in plan:
        totals = []
        for n in alternatives:
            totals.append(total_of(copies[:n], buffers[:n]))
            copies, buffers = copies[n:], buffers[n:]
        if keep:
            upper = at_ref[selector] == 1
            write(jnp.where(upper, totals[0], totals[1]))
            write(jnp.where(upper, totals[1], totals[0]))
        elif len(totals) == 1:
            write(totals[0])
        else:
            write(jnp.stack(totals, axis=0))
    for copy in written:
        copy.wait()


def part_shape(array, index):
    return tuple(array.shape[d] for d, at in enumerate(index) if at is None) + tuple(
        array.shape[-2:]
    )


def sums(units, mebibytes):
    scalars, arrays, indices, buffers, outs, plan = [], [], [], [], [], []

    def scalar(value):
        scalars.append(value)
        return len(scalars) - 1

    for alternatives, selector, kind in units:
        for terms in alternatives:
            for array, index in terms:
                shape = part_shape(array, index)
                arrays.append(array)
                indices.append([None if at is None else scalar(at) for at in index])
                buffers.append(pltpu.VMEM(shape, array.dtype))
        keep = selector is not None
        plan.append(([len(t) for t in alternatives], scalar(selector) if keep else None, keep))
        stacked = () if keep or len(alternatives) == 1 else (len(alternatives),)
        outs.append(jax.ShapeDtypeStruct(stacked + shape, kind))
        if keep:
            outs.append(jax.ShapeDtypeStruct(shape, F32))
    if not scalars:
        scalars = [jnp.int32(0)]
    results = list(
        pl.pallas_call(
            functools.partial(sums_kernel, plan=plan, indices=indices),
            grid_spec=pltpu.PrefetchScalarGridSpec(
                num_scalar_prefetch=1,
                grid=(),
                in_specs=[ANY_SPEC] * len(arrays),
                out_specs=[ANY_SPEC] * len(outs),
                scratch_shapes=buffers
                + [pltpu.VMEM(o.shape, o.dtype) for o in outs]
                + [pltpu.SemaphoreType.DMA((len(arrays),)), pltpu.SemaphoreType.DMA((len(outs),))],
            ),
            out_shape=outs,
            compiler_params=kernel_params(mebibytes),
        )(jnp.stack([jnp.asarray(s, jnp.int32) for s in scalars]), *arrays)
    )
    return [(results.pop(0), results.pop(0) if keep else None) for _, _, keep in plan]


def at_own(terms, mine, done, label=None):
    def place(b):
        if isinstance(b, int):
            return b
        return 1 - mine[b] if b == label else mine[b] if b in done else None

    return [(array, [place(b) for b in labels]) for array, labels in terms]


def split_view(array, labels):
    return array.reshape((2,) * len(labels) + tuple(array.shape[-2:]))


def route_of(label):
    axis, bit = label
    if axis == "seq":
        return lambda s, f: (s ^ bit, f)
    return lambda s, f: (s, f ^ (2 * bit))


def without(labels, done):
    return [label for label in labels if label not in done]


def halving(gives, keeps, labels, orders, mine, last=None):
    came = yield gives, [route_of(order[0]) for order in orders]
    terms = []
    for keep, (arrived, _, _), order in zip(keeps, came, orders):
        rest = without(labels, order[:1])
        terms.append([(split_view(keep, rest), rest), (split_view(arrived, rest), rest)])
    for i in range(1, len(orders[0])):
        parts = [at_own(t, mine, order[:i], order[i]) for t, order in zip(terms, orders)]
        if len(orders) == 2 and orders[0][i] == orders[1][i]:
            ((arrived, _, _),) = yield [(parts, None, BF16)], [route_of(orders[0][i])]
            for g, (t, order) in enumerate(zip(terms, orders)):
                rest = without(labels, order[: i + 1])
                t.append((split_view(arrived, [g] + rest), [g] + rest))
            continue
        came = yield [([p], None, BF16) for p in parts], [route_of(order[i]) for order in orders]
        for t, (arrived, _, _), order in zip(terms, came, orders):
            rest = without(labels, order[: i + 1])
            t.append((split_view(arrived, rest), rest))
    final = [at_own(t, mine, order) for t, order in zip(terms, orders)]
    if last is not None:
        ((arrived, kept, _),) = yield [(final, mine[last], BF16)], [route_of(last)]
        final = [[(kept, []), (arrived, [])]]
    yield final[0], None


def in_rounds(chains, beside):
    waiting = [next(chain) for chain in chains]
    count, done = 0, None
    while any(routes is not None for _, routes in waiting):
        units = [u for values, routes in waiting if routes is not None for u in values]
        routes = [r for _, some in waiting if some is not None for r in some]
        ready = sums(units, 24 if count == 1 else 60) if count else [(value, None) for value in units]
        came = [sent(give, route) for (give, _), route in zip(ready, routes)]
        if count in beside:
            ready, done = beside[count](ready, done)
            came, done = together(came, done)
        else:
            (came,) = together(came)
        count += 1
        arrived = [(value, kept, give) for value, (give, kept) in zip(came, ready)]
        for i, (values, some) in enumerate(waiting):
            if some is not None:
                mine, arrived = arrived[: len(values)], arrived[len(values) :]
                waiting[i] = chains[i].send(mine)
    return [values for values, _ in waiting], done


def unpack_kernel(at_ref, *refs, share, line_share, chan_row):
    pieces, (out_ref, chan_ref, rows_all) = refs[:-3], refs[-3:]
    shard, width = out_ref.shape
    for o, piece in enumerate(pieces):
        p = at_ref[0] ^ o
        begin = 0
        for base, count in ((p * share, share), (len(pieces) * share + p * line_share, line_share)):
            half = count // 2
            for h in range(2):
                first = pl.multiple_of(base + h * half, 16)
                rows_all[pl.ds(first, half), :] = piece[
                    begin : begin + half, h * shard : (h + 1) * shard
                ]
            begin += half
    for first in range(0, width, LANES):
        size = min(LANES, width - first)
        out_ref[:, first : first + size] = rows_all[first : first + LANES].T[:, :size]
    chan_ref[...] = rows_all[chan_row : chan_row + 16].astype(F32)[:6]


def unpacked(pieces, seq_index, width, share, line_share, chan_row):
    rows, lanes = pieces[0].shape
    shard = lanes // 2
    return pl.pallas_call(
        functools.partial(unpack_kernel, share=share, line_share=line_share, chan_row=chan_row),
        grid_spec=pltpu.PrefetchScalarGridSpec(
            num_scalar_prefetch=1,
            grid=(),
            in_specs=[VMEM_SPEC] * len(pieces),
            out_specs=[VMEM_SPEC] * 2,
            scratch_shapes=[pltpu.VMEM((2 * len(pieces) * rows, shard), BF16)],
        ),
        out_shape=[
            jax.ShapeDtypeStruct((shard, width), BF16),
            jax.ShapeDtypeStruct((6, shard), F32),
        ],
        compiler_params=kernel_params(24),
    )(seq_index.astype(jnp.int32).reshape(1), *pieces)


def finish_kernel(at_ref, *refs, counts, indices, scale):
    count = len(indices)
    ins, out_ref = refs[:count], refs[count]
    buffers, sems = list(refs[count + 1 : -1]), refs[-1]
    copies = fetched(at_ref, ins, buffers, sems, indices)
    begin = 0
    for n in counts:
        total = (total_of(copies[:n], buffers[:n]) * scale).astype(BF16)
        copies, buffers = copies[n:], buffers[n:]
        out_ref[begin : begin + total.shape[0], :] = total
        begin += total.shape[0]


def finish(chains, scale):
    scalars, arrays, indices, buffers, height = [], [], [], [], 0
    for terms in chains:
        for array, index in terms:
            indices.append(list(range(len(scalars), len(scalars) + len(index))))
            scalars += index
            arrays.append(array)
            buffers.append(pltpu.VMEM(tuple(array.shape[-2:]), array.dtype))
        height += terms[0][0].shape[-2]
    lanes = arrays[0].shape[-1]
    return pl.pallas_call(
        functools.partial(
            finish_kernel, counts=[len(t) for t in chains], indices=indices, scale=scale
        ),
        grid_spec=pltpu.PrefetchScalarGridSpec(
            num_scalar_prefetch=1,
            grid=(),
            in_specs=[ANY_SPEC] * len(arrays),
            out_specs=VMEM_SPEC,
            scratch_shapes=buffers + [pltpu.SemaphoreType.DMA((len(arrays),))],
        ),
        out_shape=jax.ShapeDtypeStruct((height, lanes), BF16),
        compiler_params=kernel_params(24),
    )(jnp.stack([jnp.asarray(s, jnp.int32) for s in scalars]), *arrays)


def shards(patches, send_slot, segments, stem_weight, norm_gain, conv_kernel, cotangent):
    seq_size, fsdp_size = lax.axis_size("seq"), lax.axis_size("fsdp")
    seq_index, fsdp_index = lax.axis_index("seq"), lax.axis_index("fsdp")
    chips, chip, core = fsdp_size // 2, fsdp_index // 2, fsdp_index % 2
    slots = send_slot.shape[1]
    tokens, width = patches.shape[1], patches.shape[2]
    rows = tokens // slots
    edge = 2 * rows
    shard = stem_weight.shape[0]
    channels = shard * fsdp_size
    padded = round_up(width + 6, LANES)
    capacity = 2 * slots // seq_size
    cot = cotangent[0]
    core_id = core.astype(jnp.int32).reshape(1)

    def following(s, f):
        return (s + 1, f) if s + 1 < seq_size else None

    def preceding(s, f):
        return (s - 1, f) if s > 0 else None

    own = jnp.concatenate(
        [
            stem_weight,
            norm_gain[:, None],
            conv_kernel.T,
            jnp.zeros((shard, padded - width - 6), BF16),
        ],
        axis=1,
    )
    own, cot, patches = together(own, cot, patches)
    tail, head = cot[tokens - edge :], cot[:edge]
    frames = patches[0].reshape(slots, rows, width)
    boxes = outgoing(frames, send_slot[0], seq_index, seq_size, padded)
    rising, falling = {0: own}, {0: own}
    own_core = swapped(own, 0, 1)
    boxes, own_core = together(boxes, own_core)
    inbox = [None] * (seq_size - 1)
    direct = [o for o in range(1, seq_size) if o.bit_count() % 2 == 1]
    others = [o for o in range(1, seq_size) if o.bit_count() % 2 == 0]
    split = 2 * shard % LANES == 0 and chips == 4
    lane_shards, core_shards, chip_of = [own], [own_core], [chip]
    early = []
    spots = [None] * (seq_size - 1)

    def arrive(numbers, boxes):
        for o, box in zip(numbers, boxes):
            inbox[o - 1], spots[o - 1] = box, box[:, 0, width]

    def add_shard(k, rising, falling):
        options, which, origin = chain_slot(rising, falling, k, chip, chips)
        lane_shards.append(chosen(options, which))
        core_shards.append(swapped(lane_shards[-1], 0, 1))
        chip_of.append(origin)

    for k in range(1, chips):
        if k < 3 or not split:
            rising[k], falling[k] = chain_step(rising[k - 1], falling[k - 1], k, chips)
        if k == 1:
            came = [swapped(boxes[o - 1], o, 0) for o in direct]
            rising, falling, came, boxes, tail, head = together(
                rising, falling, came, boxes, tail, head
            )
            arrive(direct, came)
        elif k == 2:
            came = [swapped(boxes[o - 1], o, 0) for o in others]
            cot_low = sent(tail, following)
            if split:
                rising[1], falling[1], spots = together(rising[1], falling[1], spots)
                add_shard(1, rising, falling)
                near = jnp.where(chip < chips // 2, rising[1], falling[1])
            rising, falling, cot_low, came, core_shards, lane_shards, spots, head = together(
                rising, falling, cot_low, came, core_shards, lane_shards, spots, head
            )
            arrive(others, came)
            cot_high = sent(head, preceding)
            pick = arrivals(send_slot[0], jnp.stack(spots, axis=0), seq_index)
            main, main_head, main_tail = scalar_call(
                place_kernel,
                [
                    jax.ShapeDtypeStruct((count, padded), BF16)
                    for count in (tokens + 16, 2 * edge, 2 * edge)
                ],
                [pick],
                [frames] + inbox,
            )
            if split:
                add_shard(2, rising, falling)
                final = sent(
                    lane_shards[2],
                    lambda s, f: (s, f + 2) if f // 2 == 2 else (s, f - 2) if f // 2 == 1 else None,
                )
                main, main_head, main_tail, lane_shards, core_shards = together(
                    main, main_head, main_tail, lane_shards, core_shards
                )
            low = sent(main_tail, following)
            high = sent(main_head, preceding)
        elif k == 3 and split:
            pairs = [v for both in zip(lane_shards, core_shards) for v in both]
            early_main, main_squares = stem_early(main, pairs, core_id)
            final, early_main, low, high, main, cot_high = together(
                final, early_main, low, high, main, cot_high
            )
            outer = (chip == 0) | (chip == chips - 1)
            lane_shards.append(jnp.where(outer, final, near))
            core_shards.append(swapped(lane_shards[-1], 0, 1))
            chip_of.append(jnp.where(outer, chips - 1 - chip, jnp.where(chip == 1, 0, chips - 1)))
        else:
            rising, falling = together(rising, falling)
    for k in range(len(lane_shards), chips):
        add_shard(k, rising, falling)
    height = round_up(width, 64 * seq_size)
    main_other = swapped(main, 0, 1)
    places = jnp.stack([core] + chip_of).astype(jnp.int32)
    all_pairs = [v for both in zip(lane_shards, core_shards) for v in both]
    if split:
        all_pairs, main_other = together(all_pairs, main_other)
        early = [early_main, main_squares]

    ids = segments[0]
    total_slots = ids.shape[0]
    centre = seq_index * slots + jnp.arange(-2, slots + 2, dtype=jnp.int32)
    near = centre[:, None] + jnp.arange(-2, 3, dtype=jnp.int32)[None, :]
    inside = (near >= 0) & (near < total_slots) & ((centre >= 0) & (centre < total_slots))[:, None]
    same = (
        ids[jnp.clip(near, 0, total_slots - 1)] == ids[jnp.clip(centre, 0, total_slots - 1)][:, None]
    )
    mask = (inside & same).astype(F32).reshape(-1)
    features, d_stem, give, keep = layer(
        main, low, high, cot, cot_low, cot_high, all_pairs, early, places, mask, slots, channels
    )
    got = swapped(give, 0, 1)
    pixels = turned(main, main_other, height, tokens)
    middle = round_up(width // 2, LANES)

    seq_bits = bits_of(seq_size)
    chip_bits = bits_of(chips)
    line_share = height // seq_size // 4 // 32 * 32
    share = height // seq_size - line_share
    where = jnp.stack([seq_index, chip]).astype(jnp.int32)
    first_bits = [seq_bits[0], seq_bits[-1]]
    sizes = (chips, seq_size, shard, share, line_share, first_bits)
    gives = weight_part(pixels, keep, got, where, *sizes, True)
    keeps = weight_part(pixels, keep, got, where, *sizes, False)
    scale = 1.0 / math.sqrt(tokens * seq_size * fsdp_size)
    mine = {("seq", b): bit_at(seq_index, b) for b in seq_bits}
    mine |= {("chip", b): bit_at(chip, b) for b in chip_bits}
    seq_labels = [("seq", b) for b in seq_bits]
    chip_labels = [("chip", b) for b in chip_bits]
    orders = [order + chip_labels[:-1] for order in (seq_labels, seq_labels[::-1])]
    chains = [
        halving(
            gives[:2],
            keeps[:2],
            chip_labels[:-1][::-1] + seq_labels[::-1],
            orders,
            mine,
            chip_labels[-1],
        ),
        halving(
            gives[2:],
            keeps[2:],
            chip_labels[::-1] + seq_labels[::-1],
            [chip_labels + seq_labels],
            mine,
        ),
    ]
    last_round = len(seq_bits) + len(chip_bits) - 1

    def left_pixels(ready, _):
        inputs, ready = together(d_stem, ready)
        return ready, pixel_grads(inputs, all_pairs, places, 0, middle)

    (plane, line), grad_rows = in_rounds(chains, {last_round: left_pixels})
    rows_mine = finish([plane, line], scale)
    d_stem, rows_mine = together(d_stem, rows_mine)
    pieces = [rows_mine] + [swapped(rows_mine, o, 0) for o in range(1, seq_size)]
    grad_rows = pixel_grads(d_stem, all_pairs, places, middle, width, grad_rows)
    pieces, grad_rows = together(pieces, grad_rows)
    grad_weight, grad_channels = unpacked(
        pieces, seq_index, width, share, line_share, padded - 16
    )
    return (features[None], grad_rows[None], grad_weight, grad_channels)


def solution(mesh):
    in_specs = (
        P("fsdp", "seq", None),
        P("fsdp", "seq"),
        P("fsdp", None),
        P("fsdp", None),
        P("fsdp"),
        P(None, "fsdp"),
        P("fsdp", "seq", None),
    )
    out_specs = (P("fsdp", "seq", None), P("fsdp", "seq", None), P("fsdp", None), P(None, "fsdp"))
    return jax.shard_map(shards, mesh=mesh, in_specs=in_specs, out_specs=out_specs, check_vma=False)
```

```python
import functools
import math

import jax
import jax.numpy as jnp
from jax import lax
from jax.experimental import pallas as pl
from jax.experimental.pallas import tpu as pltpu
from jax.sharding import PartitionSpec as P

EPSILON = 1e-06
BF16 = jnp.bfloat16
F32 = jnp.float32
LANES = 128
AXES = ("seq", "fsdp")


def round_up(value, unit):
    return (value + unit - 1) // unit * unit


def kernel_params(mebibytes):
    return pltpu.CompilerParams(vmem_limit_bytes=mebibytes * 1024 * 1024)


def sent(value, route):
    seq_size, fsdp_size = lax.axis_size("seq"), lax.axis_size("fsdp")
    pairs = []
    for s in range(seq_size):
        for f in range(fsdp_size):
            target = route(s, f)
            if target is not None:
                pairs.append((s * fsdp_size + f, target[0] * fsdp_size + target[1]))
    return lax.ppermute(value, AXES, pairs)


def swapped(value, seq_bits, fsdp_bits):
    return sent(value, lambda s, f: (s ^ seq_bits, f ^ fsdp_bits))


def together(*values):
    flat, tree = jax.tree.flatten(values)
    return jax.tree.unflatten(tree, lax.optimization_barrier(tuple(flat)))


def bits_of(size):
    return [1 << i for i in range(size.bit_length() - 1)]


def by_position(pieces, me):
    stack = jnp.stack(pieces, axis=0)
    count = len(pieces)
    tail = stack.shape[1:]
    for bit in bits_of(count):
        view = stack.reshape((count // (2 * bit), 2, bit) + tail)
        flipped = jnp.concatenate([view[:, 1:], view[:, :1]], axis=1)
        stack = jnp.where((me & bit) != 0, flipped, view).reshape((count,) + tail)
    return stack


def outbox_kernel(order_ref, spot_ref, frames_ref, *out_refs):
    rows, width = frames_ref.shape[1:]
    for peer, out in enumerate(out_refs):
        capacity, _, padded = out.shape
        lane = lax.broadcasted_iota(jnp.int32, (rows, LANES), 1) + (padded - LANES)
        for k in range(capacity):
            spot = spot_ref[peer * capacity + k]
            out[k, :, padded - LANES :] = jnp.where(lane == width, spot, 0.0).astype(BF16)
            out[k, :, :width] = frames_ref[order_ref[peer * capacity + k]]


def place_kernel(pick_ref, frames_ref, *refs):
    inbox, (out, head, tail) = refs[:-3], refs[-3:]
    slots, rows, width = frames_ref.shape
    total, padded = out.shape
    tokens = slots * rows
    capacity = inbox[0].shape[0]
    out[:tokens, padded - LANES :] = jnp.zeros((tokens, LANES), out.dtype)
    row = lax.broadcasted_iota(jnp.int32, (total - tokens, padded), 0)
    column = lax.broadcasted_iota(jnp.int32, (total - tokens, padded), 1)
    out[tokens:, :] = jnp.where((column == row + width) & (row < 6), 1.0, 0.0).astype(BF16)

    def one(p, carry):
        index = pick_ref[p]
        here = pl.ds(pl.multiple_of(p * rows, 16), rows)

        @pl.when(index < slots)
        def _():
            out[here, :width] = frames_ref[index]

        for peer, box in enumerate(inbox):
            first = slots + peer * capacity

            @pl.when((index >= first) & (index < first + capacity))
            def _():
                out[here, :width] = box[index - first, :, :width]

        return carry

    lax.fori_loop(0, slots, one, 0)
    head[...] = out[: head.shape[0]]
    tail[...] = out[tokens - tail.shape[0] : tokens]


def scalar_call(kernel, out_shape, scalars, arrays):
    return pl.pallas_call(
        kernel,
        grid_spec=pltpu.PrefetchScalarGridSpec(
            num_scalar_prefetch=len(scalars),
            grid=(),
            in_specs=[pl.BlockSpec(memory_space=pltpu.VMEM)] * len(arrays),
            out_specs=jax.tree.map(lambda _: pl.BlockSpec(memory_space=pltpu.VMEM), out_shape),
        ),
        out_shape=out_shape,
        compiler_params=kernel_params(60),
    )(*scalars, *arrays)


def outgoing(frames, destination, seq_index, seq_size, padded):
    slots, rows, _ = frames.shape
    capacity = 2 * slots // seq_size
    owner = (destination // slots) ^ seq_index
    rank = jnp.sum(
        ((owner[:, None] == owner[None, :]) & (destination[None, :] < destination[:, None])).astype(
            jnp.int32
        ),
        axis=1,
    )
    peers = jnp.arange(1, seq_size, dtype=jnp.int32)
    places = jnp.arange(capacity, dtype=jnp.int32)
    hit = (owner[None, None, :] == peers[:, None, None]) & (
        rank[None, None, :] == places[None, :, None]
    )
    order = jnp.sum(jnp.where(hit, jnp.arange(slots, dtype=jnp.int32), 0), axis=2).reshape(-1)
    spot = jnp.sum(jnp.where(hit, destination % slots + 1, 0), axis=2).reshape(-1) - 1
    return scalar_call(
        outbox_kernel,
        [jax.ShapeDtypeStruct((capacity, rows, padded), BF16)] * (seq_size - 1),
        [order, spot.astype(F32)],
        [frames],
    )


def arrivals(destination, spots, seq_index):
    slots = destination.shape[0]
    numbers = jnp.arange(slots, dtype=jnp.int32)
    local = (destination == seq_index * slots + numbers[:, None]).astype(jnp.int32)
    boxed = (spots.astype(jnp.int32).reshape(-1) == numbers[:, None]).astype(jnp.int32)
    places = slots + jnp.arange(boxed.shape[1], dtype=jnp.int32)
    return jnp.sum(local * numbers, axis=1) + jnp.sum(boxed * places, axis=1)


def chain_step(rising, falling, k, chips):
    return (
        sent(rising, lambda s, f: (s, f + 2) if k - 1 <= f // 2 < chips - 1 else None),
        sent(falling, lambda s, f: (s, f - 2) if 0 < f // 2 <= chips - k else None),
    )


def chain_slot(rising, falling, k, chip, chips):
    low = chip < chips // 2
    far = jnp.maximum(chip, chips - 1 - chip)
    towards = jnp.where(low, 1, -1)
    options = [falling[k], rising[k]]
    which = jnp.where(low, 0, 1)
    origin = chip + towards * k
    for reach in range(chips // 2, k):
        which = jnp.where(far == reach, len(options) + jnp.where(low, 1, 0), which)
        options += [falling[k - reach], rising[k - reach]]
        origin = jnp.where(far == reach, chip - towards * (k - reach), origin)
    return options, which, origin


def chosen(options, which):
    value = options[0]
    for i, option in enumerate(options[1:], 1):
        value = jnp.where(which == i, option, value)
    return value


def load_weights(place_ref, shard_refs, weights, sems, by_chip):
    pairs = len(shard_refs) // 2
    shard = shard_refs[0].shape[0]
    core = place_ref[0]
    for k in range(pairs)[::-1]:
        for h in range(2):
            lane = core if h == 0 else 1 - core
            row = 2 * (place_ref[1 + k] if by_chip else k) + lane
            first = pl.multiple_of(row * shard, 16)
            pltpu.make_async_copy(
                shard_refs[2 * k + h], weights.at[pl.ds(first, shard), :], sems.at[row]
            ).start()


def wait_weights(shard_ref, weights, sems, pair):
    shard = shard_ref.shape[0]
    for row in (2 * pair, 2 * pair + 1):
        pltpu.make_async_copy(
            shard_ref, weights.at[pl.ds(row * shard, shard), :], sems.at[row]
        ).wait()


def pair_product(inputs, weights, first, count, store, squares):
    total = squares[...]
    for begin in range(0, count, 256):
        size = min(256, count - begin)
        result = lax.dot_general(
            inputs[...],
            weights[first + begin : first + begin + size, :],
            (((1,), (1,)), ((), ())),
            preferred_element_type=F32,
        )
        store(begin, size, result)
        for t in range(0, size, LANES):
            part = result[:, t : t + LANES]
            total = total + part * part
    squares[...] = total


def early_kernel(place_ref, rows_ref, *refs, pairs):
    shard_refs = refs[: 2 * pairs]
    acc_ref, squares, weights, sems = refs[2 * pairs :]
    group = acc_ref.shape[2]
    load_weights(place_ref, shard_refs, weights, sems, False)
    squares[...] = jnp.zeros_like(squares)
    for k in range(pairs):
        wait_weights(shard_refs[0], weights, sems, k)

        def store(begin, size, result, k=k):
            acc_ref[k, :, begin : begin + size] = result

        pair_product(rows_ref, weights, k * group, group, store, squares)


VMEM_SPEC = pl.BlockSpec(memory_space=pltpu.VMEM)
ANY_SPEC = pl.BlockSpec(memory_space=pl.ANY)


def stem_early(rows_in, shards, core_id):
    rows, padded = rows_in.shape
    pairs = len(shards) // 2
    group = 2 * shards[0].shape[0]
    return pl.pallas_call(
        functools.partial(early_kernel, pairs=pairs),
        grid_spec=pltpu.PrefetchScalarGridSpec(
            num_scalar_prefetch=1,
            grid=(),
            in_specs=[VMEM_SPEC] + [ANY_SPEC] * len(shards),
            out_specs=[VMEM_SPEC] * 2,
            scratch_shapes=[
                pltpu.VMEM((pairs * group, padded), BF16),
                pltpu.SemaphoreType.DMA((2 * pairs,)),
            ],
        ),
        out_shape=[
            jax.ShapeDtypeStruct((pairs, rows, group), F32),
            jax.ShapeDtypeStruct((rows, LANES), F32),
        ],
        compiler_params=kernel_params(24),
    )(core_id, rows_in, *shards)


def gate_of(value):
    return 0.5 * jnp.tanh(0.5 * value) + 0.5


def mixed_at(window, taps, mask_ref, first):
    total = window[0] * (taps[0] * mask_ref[first])
    for k in range(1, 5):
        total = total + window[k] * (taps[k] * mask_ref[first + k])
    return total


def layer_kernel(
    place_ref, mask_ref, main_ref, low_ref, high_ref, cot_ref, cot_low_ref, cot_high_ref, *refs,
    pairs, late, slots, channels
):
    shard_refs, refs = refs[: 2 * (pairs + late)], refs[2 * (pairs + late) :]
    if pairs:
        early_ref, early_squares, refs = refs[0], refs[1], refs[2:]
    feat_ref, stem_ref, give_ref, keep_ref = refs[:4]
    weights, rows_all, acc, cots, feats, d_stem, lanes_of_core, gated, slopes, squares, inverse = refs[4:15]
    part_ref, sems, in_sems, cot_sems, out_sems, stem_sems = refs[15:]
    group = 2 * shard_refs[0].shape[0]
    chips = channels // group
    tokens = cot_ref.shape[0]
    rows = tokens // slots
    halo, edge = low_ref.shape[0], cot_low_ref.shape[0]
    own_row = 2 * halo
    body = own_row + tokens
    core = place_ref[0]
    load_weights(place_ref, shard_refs, weights, sems, not pairs)
    if pairs:
        for k in range(pairs):
            lanes = pl.ds(pl.multiple_of(place_ref[1 + k] * group, LANES), group)
            pltpu.make_async_copy(
                early_ref.at[k],
                acc.at[pl.ds(own_row, early_ref.shape[1]), lanes],
                in_sems.at[place_ref[1 + k]],
            ).start()
    parts = 4
    size = channels // parts
    cot_loads = []
    for i in range(parts):
        lanes = pl.ds(i * size, size)
        first = 0
        for h, ref in enumerate((cot_low_ref, cot_ref, cot_high_ref)):
            count = ref.shape[0]
            cot_loads.append(
                pltpu.make_async_copy(
                    ref.at[:, lanes], cots.at[pl.ds(first, count), lanes], cot_sems.at[i, h]
                )
            )
            first += count
    for copy in cot_loads:
        copy.start()
    rows_all[0:halo] = low_ref[...]
    rows_all[halo:own_row] = high_ref[...]
    rows_all[own_row:] = main_ref[...]
    squares[...] = jnp.zeros_like(squares)
    if pairs:
        squares[own_row:] = early_squares[...]
        for k in [pairs] + list(range(pairs)):
            count = rows_all.shape[0] if k == pairs else own_row
            wait_weights(shard_refs[0], weights, sems, k)

            def store(begin, width, result, k=k, count=count):
                first = pl.multiple_of(place_ref[1 + k] * group + begin, LANES)
                acc[0:count, pl.ds(first, width)] = result

            pair_product(
                rows_all.at[0:count], weights, k * group, group, store, squares.at[0:count]
            )
    else:
        for z in range(late):
            wait_weights(shard_refs[0], weights, sems, z)
        tile = 256

        def one(j, carry):
            first = pl.multiple_of(j * tile, tile)
            result = lax.dot_general(
                rows_all[...],
                weights[pl.ds(first, tile), :],
                (((1,), (1,)), ((), ())),
                preferred_element_type=F32,
            )
            acc[:, pl.ds(first, tile)] = result
            total = squares[...]
            for t in range(0, tile, LANES):
                total = total + result[:, t : t + LANES] * result[:, t : t + LANES]
            squares[...] = total
            return carry

        lax.fori_loop(0, channels // tile, one, 0)
    mean = jnp.sum(squares[...], axis=1, keepdims=True) / channels
    inverse[...] = jnp.broadcast_to(lax.rsqrt(mean + EPSILON), inverse.shape)
    squares[...] = jnp.zeros_like(squares)

    def rows_of_slot(i):
        edge_slots = halo // rows
        if i < edge_slots:
            first = i * rows
        elif i < edge_slots + slots:
            first = own_row + (i - edge_slots) * rows
        else:
            first = halo + (i - edge_slots - slots) * rows
        return slice(first, first + rows)

    def columns(t, carry):
        lanes = pl.ds(pl.multiple_of(t * LANES, LANES), LANES)
        gain = acc[body : body + 1, lanes]
        taps = [acc[body + 1 + k : body + 2 + k, lanes] for k in range(5)]

        def normed(i):
            here = rows_of_slot(i)
            return (acc[here, lanes] * inverse[here] * gain).astype(BF16).astype(F32)

        window = [normed(i) for i in range(4)]
        sums = [jnp.zeros((8, LANES), F32) for _ in range(5)]
        for i in range(slots + 4):
            window.append(normed(i + 4))
            mixed = mixed_at(window, taps, mask_ref, 5 * i)
            gate = gate_of(mixed)
            smooth = mixed * gate
            here = slice(i * rows, (i + 1) * rows)
            up = cots[here, lanes].astype(F32)
            slope = (up * (gate + smooth - smooth * gate)).astype(BF16).astype(F32)
            slopes[here] = slope
            if 2 <= i < slots + 2:
                own = slice((i - 2) * rows, (i - 1) * rows)
                stem = acc[rows_of_slot(i + 2), lanes]
                feats[own, lanes] = (stem + smooth).astype(BF16)
                for k in range(5):
                    product = (slope * window[k]).reshape(rows // 8, 8, LANES)
                    sums[k] = sums[k] + jnp.sum(product, axis=0) * mask_ref[5 * i + k]
            window = window[1:]
        for k in range(5):
            part_ref[1 + k : 2 + k, lanes] = jnp.sum(sums[k], axis=0, keepdims=True)
        part_ref[6:8, lanes] = jnp.zeros((2, LANES), F32)
        total = jnp.zeros((8, LANES), F32)
        for p in range(slots):
            window = [slopes[(p + o) * rows : (p + o + 1) * rows] for o in range(5)]
            own = slice(p * rows, (p + 1) * rows)
            here = rows_of_slot(p + 4)
            d_normed = mixed_at(window, taps[::-1], mask_ref, 5 * (p + 2))
            product = d_normed * (acc[here, lanes] * inverse[here])
            total = total + jnp.sum(product.reshape(rows // 8, 8, LANES), axis=0)
            gated[own, lanes] = d_normed * gain
            squares[own] = squares[own] + product * gain
        part_ref[0:1, lanes] = jnp.sum(total, axis=0, keepdims=True)
        return carry

    copies = []
    for i in range(parts):
        for copy in cot_loads[3 * i : 3 * i + 3]:
            copy.wait()
        if pairs:

            @pl.when(place_ref[1 + pairs] != i)
            def _(i=i):
                pltpu.make_async_copy(
                    early_ref.at[0],
                    acc.at[pl.ds(own_row, early_ref.shape[1]), pl.ds(i * group, group)],
                    in_sems.at[i],
                ).wait()

        lax.fori_loop(i * size // LANES, (i + 1) * size // LANES, columns, 0)
        lanes = pl.ds(i * size, size)
        copy = pltpu.make_async_copy(feats.at[:, lanes], feat_ref.at[:, lanes], out_sems.at[i])
        copy.start()
        copies.append(copy)
    mean = jnp.sum(squares[0:tokens], axis=1, keepdims=True) / channels
    squares[0:tokens] = jnp.broadcast_to(mean, (tokens, LANES))

    def finish_columns(t, carry):
        lanes = pl.ds(pl.multiple_of(t * LANES, LANES), LANES)
        inv = inverse[own_row:body]
        unit = acc[own_row:body, lanes] * inv
        value = cots[edge : edge + tokens, lanes].astype(F32) + inv * (
            gated[:, lanes] - unit * squares[0:tokens]
        )
        d_stem[:, lanes] = value.astype(BF16)
        return carry

    shard = group // 2
    room = lanes_of_core.shape[2] // chips
    steps = chips if group % LANES == 0 else 1
    for i in range(steps):
        lax.fori_loop(
            i * channels // steps // LANES, (i + 1) * channels // steps // LANES, finish_columns, 0
        )
        lanes = pl.ds(i * (channels // steps), channels // steps)
        copies.append(
            pltpu.make_async_copy(d_stem.at[:, lanes], stem_ref.at[:, lanes], stem_sems.at[i, 0])
        )
        copies[-1].start()
        for z in range(i * chips // steps, (i + 1) * chips // steps):
            for h in range(2):
                first = (2 * z + h) * shard
                part = part_ref[:, first : first + shard]
                rest = part - part.astype(BF16).astype(F32)
                lanes = slice(z * room, z * room + shard)
                lanes_of_core[h, :tokens, lanes] = d_stem[:, first : first + shard]
                lanes_of_core[h, tokens:, lanes] = jnp.concatenate([part, rest], axis=0).astype(BF16)
                if room > shard:
                    lanes_of_core[h, :, z * room + shard : (z + 1) * room] = jnp.zeros(
                        (tokens + 16, room - shard), BF16
                    )
        width = chips // steps * room
        lanes = pl.ds(i * width, width)
        for h, ref in enumerate((keep_ref, give_ref)):
            copies.append(
                pltpu.make_async_copy(
                    lanes_of_core.at[(core + h) % 2, :, lanes],
                    ref.at[:, lanes],
                    stem_sems.at[i, 1 + h],
                )
            )
            copies[-1].start()
    for copy in copies:
        copy.wait()


def layer(main, low, high, cot, cot_low, cot_high, shards, early, places, mask, slots, channels):
    tokens = cot.shape[0]
    padded = main.shape[1]
    halo, edge = low.shape[0], cot_low.shape[0]
    total = main.shape[0] + 2 * halo
    pairs = early[0].shape[0] if early else 0
    late = len(shards) // 2 - pairs
    shard = shards[0].shape[0]
    half = channels // (2 * shard) * round_up(shard, LANES)
    return pl.pallas_call(
        functools.partial(layer_kernel, pairs=pairs, late=late, slots=slots, channels=channels),
        grid_spec=pltpu.PrefetchScalarGridSpec(
            num_scalar_prefetch=2,
            grid=(),
            in_specs=[VMEM_SPEC] * 3
            + [ANY_SPEC] * 3
            + [ANY_SPEC] * len(shards)
            + ([ANY_SPEC, VMEM_SPEC] if pairs else []),
            out_specs=[ANY_SPEC] * 4,
            scratch_shapes=[
                pltpu.VMEM((channels, padded), BF16),
                pltpu.VMEM((total, padded), BF16),
                pltpu.VMEM((total, channels), F32),
                pltpu.VMEM((tokens + 2 * edge, channels), BF16),
                pltpu.VMEM((tokens, channels), BF16),
                pltpu.VMEM((tokens, channels), BF16),
                pltpu.VMEM((2, tokens + 16, half), BF16),
                pltpu.VMEM((tokens, channels), F32),
                pltpu.VMEM((tokens + 2 * edge, LANES), F32),
                pltpu.VMEM((total, LANES), F32),
                pltpu.VMEM((total, LANES), F32),
                pltpu.VMEM((8, channels), F32),
                pltpu.SemaphoreType.DMA((len(shards),)),
                pltpu.SemaphoreType.DMA((len(shards) // 2,)),
                pltpu.SemaphoreType.DMA((4, 3)),
                pltpu.SemaphoreType.DMA((4,)),
                pltpu.SemaphoreType.DMA((len(shards) // 2, 3)),
            ],
        ),
        out_shape=[
            jax.ShapeDtypeStruct((tokens, channels), BF16),
            jax.ShapeDtypeStruct((tokens, channels), BF16),
            jax.ShapeDtypeStruct((tokens + 16, half), BF16),
            jax.ShapeDtypeStruct((tokens + 16, half), BF16),
        ],
        compiler_params=kernel_params(60),
    )(places, mask, main, low, high, cot, cot_low, cot_high, *shards, *early)


def pixel_kernel(place_ref, d_stem_ref, *refs, chips, begin, tile):
    shard_refs, refs = refs[: 2 * chips], refs[2 * chips :]
    before = refs[0] if begin else None
    out_ref, weights, sems = refs[1:] if begin else refs
    width = out_ref.shape[1] - begin
    lanes = pl.ds(begin, weights.shape[1])
    load_weights(place_ref, [r.at[:, lanes] for r in shard_refs], weights, sems, True)
    for z in range(chips):
        wait_weights(shard_refs[0].at[:, lanes], weights, sems, z)
    if begin:
        out_ref[:, :begin] = before[...]
    for first in range(0, width, tile):
        size = min(tile, width - first)
        columns = slice(first, first + round_up(size, LANES))
        value = jnp.dot(d_stem_ref[...], weights[:, columns], preferred_element_type=F32)
        out_ref[:, begin + first : begin + first + size] = value[:, :size].astype(BF16)


def pixel_grads(d_stem, shards, places, begin, end, before=None):
    tokens, channels = d_stem.shape
    chips = len(shards) // 2
    lanes = round_up(end - begin, LANES)
    return pl.pallas_call(
        functools.partial(pixel_kernel, chips=chips, begin=begin, tile=256),
        grid_spec=pltpu.PrefetchScalarGridSpec(
            num_scalar_prefetch=1,
            grid=(),
            in_specs=[VMEM_SPEC]
            + [ANY_SPEC] * len(shards)
            + ([VMEM_SPEC] if begin else []),
            out_specs=VMEM_SPEC,
            scratch_shapes=[
                pltpu.VMEM((channels, lanes), BF16),
                pltpu.SemaphoreType.DMA((2 * chips,)),
            ],
        ),
        out_shape=jax.ShapeDtypeStruct((tokens, end), BF16),
        compiler_params=kernel_params(60),
    )(places, d_stem, *shards, *([before] if begin else []))


def turn_kernel(first_ref, second_ref, out_ref, *, tokens):
    height, depth = out_ref.shape
    padded = first_ref.shape[1]
    row = lax.broadcasted_iota(jnp.int32, (16, padded), 0) % 8
    column = lax.broadcasted_iota(jnp.int32, (16, padded), 1)
    extra = jnp.where((column == padded - 16 + row) & (row < 6), 1.0, 0.0).astype(BF16)
    out_ref[:, 2 * tokens + 32 :] = jnp.zeros((height, depth - 2 * tokens - 32), BF16)
    both = jnp.concatenate([first_ref[:tokens], extra, second_ref[:tokens], extra], axis=0)
    for m in range(0, height, LANES):
        count = min(LANES, height - m)
        if m < padded:
            out_ref[m : m + count, : 2 * tokens + 32] = both[:, m : m + LANES].T[:count]
        else:
            out_ref[m : m + count, :] = jnp.zeros((count, depth), BF16)


def turned(packed, packed_other, height, tokens):
    return pl.pallas_call(
        functools.partial(turn_kernel, tokens=tokens),
        in_specs=[VMEM_SPEC] * 2,
        out_specs=VMEM_SPEC,
        out_shape=jax.ShapeDtypeStruct((height, round_up(2 * tokens + 32, LANES)), BF16),
        compiler_params=kernel_params(16),
    )(packed, packed_other)


def halves_beside(value, shard):
    rows = value.shape[0] // 2
    return value[:rows, :shard], value[rows:, :shard]


def weight_kernel(where_ref, pixels_ref, keep_ref, got_ref, *refs, bits, share, line_share, shard, give):
    outs, (d_stem, left, line, sems, left_sems) = refs[:3], refs[3:]
    tokens = keep_ref.shape[0]
    seq_index, chip = where_ref[0], where_ref[1]
    seq_size = 2 * outs[0].shape[1]
    half = seq_size // 2
    chips = 2 * outs[0].shape[0]
    room = d_stem.shape[1] // chips
    arrive = [[] for _ in range(chips + 1)]
    for g, bit in enumerate(bits):
        mine = (seq_index // bit) % 2
        wanted = 1 - mine if give else mine
        for i in range(half):
            p = (i // bit) * (2 * bit) + i % bit + bit * wanted
            arrive[g * (chips // 2)].append(
                pltpu.make_async_copy(
                    pixels_ref.at[pl.ds(pl.multiple_of(p * share, 16), share), :],
                    left.at[g, pl.ds(i * share, share), :],
                    left_sems.at[g, i],
                )
            )
        for z in range(g * (chips // 2), (g + 1) * (chips // 2)):
            lanes = pl.ds(z * room, room)
            for h, ref in enumerate((keep_ref, got_ref)):
                arrive[z].append(
                    pltpu.make_async_copy(
                        ref.at[:, lanes],
                        d_stem.at[pl.ds(h * tokens, tokens), lanes],
                        sems.at[2 * z + h],
                    )
                )
    arrive[chips].append(
        pltpu.make_async_copy(
            pixels_ref.at[pl.ds(seq_size * share, line.shape[0]), :], line, sems.at[2 * chips]
        )
    )
    for copy in sum(arrive, []):
        copy.start()
    extra = d_stem.shape[0] - 2 * tokens
    d_stem[2 * tokens :, :] = jnp.zeros((extra, d_stem.shape[1]), BF16)

    def fill(out, value, count, rows):
        for i in range(count):
            low, high = halves_beside(value[i * rows : (i + 1) * rows], shard)
            out[i, :, :shard] = low.astype(out.dtype)
            out[i, :, shard:] = high.astype(out.dtype)

    for g in range(2):
        for z in range(chips // 2):
            for copy in arrive[g * (chips // 2) + z]:
                copy.wait()
            first = (g * (chips // 2) + z) * room
            value = jnp.dot(
                left[g], d_stem[:, first : first + room], preferred_element_type=F32
            )
            fill(outs[g].at[z], value, half, share)
    for copy in arrive[chips]:
        copy.wait()
    mine = chip // (chips // 2)
    wanted = 1 - mine if give else mine
    for i in range(chips // 2):
        columns = pl.ds(pl.multiple_of((wanted * (chips // 2) + i) * room, LANES), room)
        value = jnp.dot(line[...], d_stem[:, columns], preferred_element_type=F32)
        fill(outs[2].at[i], value, seq_size, line_share)


def weight_part(pixels, keep, got, where, chips, seq_size, shard, share, line_share, bits, give):
    half = keep.shape[1]
    height, depth = pixels.shape
    kind = BF16 if give else F32
    plane = jax.ShapeDtypeStruct((chips // 2, seq_size // 2, share // 2, 2 * shard), kind)
    line = jax.ShapeDtypeStruct((chips // 2, seq_size, line_share // 2, 2 * shard), kind)
    return pl.pallas_call(
        functools.partial(
            weight_kernel, bits=bits, share=share, line_share=line_share, shard=shard, give=give
        ),
        grid_spec=pltpu.PrefetchScalarGridSpec(
            num_scalar_prefetch=1,
            grid=(),
            in_specs=[ANY_SPEC] * 3,
            out_specs=[VMEM_SPEC] * 3,
            scratch_shapes=[
                pltpu.VMEM((depth, half), BF16),
                pltpu.VMEM((2, seq_size // 2 * share, depth), BF16),
                pltpu.VMEM((seq_size * line_share, depth), BF16),
                pltpu.SemaphoreType.DMA((2 * chips + 1,)),
                pltpu.SemaphoreType.DMA((2, seq_size // 2)),
            ],
        ),
        out_shape=[plane, plane, line],
        compiler_params=kernel_params(24),
    )(where, pixels, keep, got)


def bit_at(index, bit):
    return (index // bit) % 2


def fetched(at_ref, refs, buffers, sems, indices):
    copies = []
    for n, (ref, buffer, index) in enumerate(zip(refs, buffers, indices)):
        place = tuple(slice(None) if p is None else at_ref[p] for p in index)
        source = ref.at[place] if place else ref
        copies.append(pltpu.make_async_copy(source, buffer, sems.at[n]))
        copies[-1].start()
    return copies


def total_of(copies, buffers):
    total = None
    for copy, buffer in zip(copies, buffers):
        copy.wait()
        value = buffer[...].astype(F32)
        total = value if total is None else total + value
    return total


def sums_kernel(at_ref, *refs, plan, indices):
    count = len(indices)
    results = sum(2 if keep else 1 for _, _, keep in plan)
    ins, outs = refs[:count], refs[count : count + results]
    buffers = list(refs[count + results : 2 * count + results])
    stores = list(refs[2 * count + results : 2 * count + 2 * results])
    sems, out_sems = refs[2 * count + 2 * results :]
    copies = fetched(at_ref, ins, buffers, sems, indices)
    written = []

    def write(value):
        n = len(written)
        stores[n][...] = value.astype(stores[n].dtype)
        written.append(pltpu.make_async_copy(stores[n], outs[n], out_sems.at[n]))
        written[-1].start()

    for alternatives, selector, keep in plan:
        totals = []
        for n in alternatives:
            totals.append(total_of(copies[:n], buffers[:n]))
            copies, buffers = copies[n:], buffers[n:]
        if keep:
            upper = at_ref[selector] == 1
            write(jnp.where(upper, totals[0], totals[1]))
            write(jnp.where(upper, totals[1], totals[0]))
        elif len(totals) == 1:
            write(totals[0])
        else:
            write(jnp.stack(totals, axis=0))
    for copy in written:
        copy.wait()


def part_shape(array, index):
    return tuple(array.shape[d] for d, at in enumerate(index) if at is None) + tuple(
        array.shape[-2:]
    )


def sums(units, mebibytes):
    scalars, arrays, indices, buffers, outs, plan = [], [], [], [], [], []

    def scalar(value):
        scalars.append(value)
        return len(scalars) - 1

    for alternatives, selector, kind in units:
        for terms in alternatives:
            for array, index in terms:
                shape = part_shape(array, index)
                arrays.append(array)
                indices.append([None if at is None else scalar(at) for at in index])
                buffers.append(pltpu.VMEM(shape, array.dtype))
        keep = selector is not None
        plan.append(([len(t) for t in alternatives], scalar(selector) if keep else None, keep))
        stacked = () if keep or len(alternatives) == 1 else (len(alternatives),)
        outs.append(jax.ShapeDtypeStruct(stacked + shape, kind))
        if keep:
            outs.append(jax.ShapeDtypeStruct(shape, F32))
    if not scalars:
        scalars = [jnp.int32(0)]
    results = list(
        pl.pallas_call(
            functools.partial(sums_kernel, plan=plan, indices=indices),
            grid_spec=pltpu.PrefetchScalarGridSpec(
                num_scalar_prefetch=1,
                grid=(),
                in_specs=[ANY_SPEC] * len(arrays),
                out_specs=[ANY_SPEC] * len(outs),
                scratch_shapes=buffers
                + [pltpu.VMEM(o.shape, o.dtype) for o in outs]
                + [pltpu.SemaphoreType.DMA((len(arrays),)), pltpu.SemaphoreType.DMA((len(outs),))],
            ),
            out_shape=outs,
            compiler_params=kernel_params(mebibytes),
        )(jnp.stack([jnp.asarray(s, jnp.int32) for s in scalars]), *arrays)
    )
    return [(results.pop(0), results.pop(0) if keep else None) for _, _, keep in plan]


def at_own(terms, mine, done, label=None):
    def place(b):
        if isinstance(b, int):
            return b
        return 1 - mine[b] if b == label else mine[b] if b in done else None

    return [(array, [place(b) for b in labels]) for array, labels in terms]


def split_view(array, labels):
    return array.reshape((2,) * len(labels) + tuple(array.shape[-2:]))


def route_of(label):
    axis, bit = label
    if axis == "seq":
        return lambda s, f: (s ^ bit, f)
    return lambda s, f: (s, f ^ (2 * bit))


def without(labels, done):
    return [label for label in labels if label not in done]


def halving(gives, keeps, labels, orders, mine, last=None):
    came = yield gives, [route_of(order[0]) for order in orders]
    terms = []
    for keep, (arrived, _, _), order in zip(keeps, came, orders):
        rest = without(labels, order[:1])
        terms.append([(split_view(keep, rest), rest), (split_view(arrived, rest), rest)])
    for i in range(1, len(orders[0])):
        parts = [at_own(t, mine, order[:i], order[i]) for t, order in zip(terms, orders)]
        if len(orders) == 2 and orders[0][i] == orders[1][i]:
            ((arrived, _, _),) = yield [(parts, None, BF16)], [route_of(orders[0][i])]
            for g, (t, order) in enumerate(zip(terms, orders)):
                rest = without(labels, order[: i + 1])
                t.append((split_view(arrived, [g] + rest), [g] + rest))
            continue
        came = yield [([p], None, BF16) for p in parts], [route_of(order[i]) for order in orders]
        for t, (arrived, _, _), order in zip(terms, came, orders):
            rest = without(labels, order[: i + 1])
            t.append((split_view(arrived, rest), rest))
    final = [at_own(t, mine, order) for t, order in zip(terms, orders)]
    if last is not None:
        ((arrived, kept, _),) = yield [(final, mine[last], BF16)], [route_of(last)]
        final = [[(kept, []), (arrived, [])]]
    yield final[0], None


def in_rounds(chains, beside):
    waiting = [next(chain) for chain in chains]
    count, done = 0, None
    while any(routes is not None for _, routes in waiting):
        units = [u for values, routes in waiting if routes is not None for u in values]
        routes = [r for _, some in waiting if some is not None for r in some]
        ready = sums(units, 24 if count == 1 else 60) if count else [(value, None) for value in units]
        came = [sent(give, route) for (give, _), route in zip(ready, routes)]
        if count in beside:
            ready, done = beside[count](ready, done)
            came, done = together(came, done)
        else:
            (came,) = together(came)
        count += 1
        arrived = [(value, kept, give) for value, (give, kept) in zip(came, ready)]
        for i, (values, some) in enumerate(waiting):
            if some is not None:
                mine, arrived = arrived[: len(values)], arrived[len(values) :]
                waiting[i] = chains[i].send(mine)
    return [values for values, _ in waiting], done


def unpack_kernel(at_ref, *refs, share, line_share, chan_row):
    pieces, (out_ref, chan_ref, rows_all) = refs[:-3], refs[-3:]
    shard, width = out_ref.shape
    for o, piece in enumerate(pieces):
        p = at_ref[0] ^ o
        begin = 0
        for base, count in ((p * share, share), (len(pieces) * share + p * line_share, line_share)):
            half = count // 2
            for h in range(2):
                first = pl.multiple_of(base + h * half, 16)
                rows_all[pl.ds(first, half), :] = piece[
                    begin : begin + half, h * shard : (h + 1) * shard
                ]
            begin += half
    for first in range(0, width, LANES):
        size = min(LANES, width - first)
        out_ref[:, first : first + size] = rows_all[first : first + LANES].T[:, :size]
    chan_ref[...] = rows_all[chan_row : chan_row + 16].astype(F32)[:6]


def unpacked(pieces, seq_index, width, share, line_share, chan_row):
    rows, lanes = pieces[0].shape
    shard = lanes // 2
    return pl.pallas_call(
        functools.partial(unpack_kernel, share=share, line_share=line_share, chan_row=chan_row),
        grid_spec=pltpu.PrefetchScalarGridSpec(
            num_scalar_prefetch=1,
            grid=(),
            in_specs=[VMEM_SPEC] * len(pieces),
            out_specs=[VMEM_SPEC] * 2,
            scratch_shapes=[pltpu.VMEM((2 * len(pieces) * rows, shard), BF16)],
        ),
        out_shape=[
            jax.ShapeDtypeStruct((shard, width), BF16),
            jax.ShapeDtypeStruct((6, shard), F32),
        ],
        compiler_params=kernel_params(24),
    )(seq_index.astype(jnp.int32).reshape(1), *pieces)


def finish_kernel(at_ref, *refs, counts, indices, scale):
    count = len(indices)
    ins, out_ref = refs[:count], refs[count]
    buffers, sems = list(refs[count + 1 : -1]), refs[-1]
    copies = fetched(at_ref, ins, buffers, sems, indices)
    begin = 0
    for n in counts:
        total = (total_of(copies[:n], buffers[:n]) * scale).astype(BF16)
        copies, buffers = copies[n:], buffers[n:]
        out_ref[begin : begin + total.shape[0], :] = total
        begin += total.shape[0]


def finish(chains, scale):
    scalars, arrays, indices, buffers, height = [], [], [], [], 0
    for terms in chains:
        for array, index in terms:
            indices.append(list(range(len(scalars), len(scalars) + len(index))))
            scalars += index
            arrays.append(array)
            buffers.append(pltpu.VMEM(tuple(array.shape[-2:]), array.dtype))
        height += terms[0][0].shape[-2]
    lanes = arrays[0].shape[-1]
    return pl.pallas_call(
        functools.partial(
            finish_kernel, counts=[len(t) for t in chains], indices=indices, scale=scale
        ),
        grid_spec=pltpu.PrefetchScalarGridSpec(
            num_scalar_prefetch=1,
            grid=(),
            in_specs=[ANY_SPEC] * len(arrays),
            out_specs=VMEM_SPEC,
            scratch_shapes=buffers + [pltpu.SemaphoreType.DMA((len(arrays),))],
        ),
        out_shape=jax.ShapeDtypeStruct((height, lanes), BF16),
        compiler_params=kernel_params(24),
    )(jnp.stack([jnp.asarray(s, jnp.int32) for s in scalars]), *arrays)


def shards(patches, send_slot, segments, stem_weight, norm_gain, conv_kernel, cotangent):
    seq_size, fsdp_size = lax.axis_size("seq"), lax.axis_size("fsdp")
    seq_index, fsdp_index = lax.axis_index("seq"), lax.axis_index("fsdp")
    chips, chip, core = fsdp_size // 2, fsdp_index // 2, fsdp_index % 2
    slots = send_slot.shape[1]
    tokens, width = patches.shape[1], patches.shape[2]
    rows = tokens // slots
    edge = 2 * rows
    shard = stem_weight.shape[0]
    channels = shard * fsdp_size
    padded = round_up(width + 6, LANES)
    capacity = 2 * slots // seq_size
    cot = cotangent[0]
    core_id = core.astype(jnp.int32).reshape(1)

    def following(s, f):
        return (s + 1, f) if s + 1 < seq_size else None

    def preceding(s, f):
        return (s - 1, f) if s > 0 else None

    own = jnp.concatenate(
        [
            stem_weight,
            norm_gain[:, None],
            conv_kernel.T,
            jnp.zeros((shard, padded - width - 6), BF16),
        ],
        axis=1,
    )
    own, cot, patches = together(own, cot, patches)
    tail, head = cot[tokens - edge :], cot[:edge]
    frames = patches[0].reshape(slots, rows, width)
    boxes = outgoing(frames, send_slot[0], seq_index, seq_size, padded)
    rising, falling = {0: own}, {0: own}
    own_core = swapped(own, 0, 1)
    boxes, own_core = together(boxes, own_core)
    inbox = [None] * (seq_size - 1)
    direct = [o for o in range(1, seq_size) if o.bit_count() % 2 == 1]
    others = [o for o in range(1, seq_size) if o.bit_count() % 2 == 0]
    split = 2 * shard % LANES == 0 and chips == 4
    lane_shards, core_shards, chip_of = [own], [own_core], [chip]
    early = []
    spots = [None] * (seq_size - 1)

    def arrive(numbers, boxes):
        for o, box in zip(numbers, boxes):
            inbox[o - 1], spots[o - 1] = box, box[:, 0, width]

    def add_shard(k, rising, falling):
        options, which, origin = chain_slot(rising, falling, k, chip, chips)
        lane_shards.append(chosen(options, which))
        core_shards.append(swapped(lane_shards[-1], 0, 1))
        chip_of.append(origin)

    for k in range(1, chips):
        if k < 3 or not split:
            rising[k], falling[k] = chain_step(rising[k - 1], falling[k - 1], k, chips)
        if k == 1:
            came = [swapped(boxes[o - 1], o, 0) for o in direct]
            rising, falling, came, boxes, tail, head = together(
                rising, falling, came, boxes, tail, head
            )
            arrive(direct, came)
        elif k == 2:
            came = [swapped(boxes[o - 1], o, 0) for o in others]
            cot_low = sent(tail, following)
            if split:
                rising[1], falling[1], spots = together(rising[1], falling[1], spots)
                add_shard(1, rising, falling)
                near = jnp.where(chip < chips // 2, rising[1], falling[1])
            rising, falling, cot_low, came, core_shards, lane_shards, spots, head = together(
                rising, falling, cot_low, came, core_shards, lane_shards, spots, head
            )
            arrive(others, came)
            cot_high = sent(head, preceding)
            pick = arrivals(send_slot[0], jnp.stack(spots, axis=0), seq_index)
            main, main_head, main_tail = scalar_call(
                place_kernel,
                [
                    jax.ShapeDtypeStruct((count, padded), BF16)
                    for count in (tokens + 16, 2 * edge, 2 * edge)
                ],
                [pick],
                [frames] + inbox,
            )
            if split:
                add_shard(2, rising, falling)
                final = sent(
                    lane_shards[2],
                    lambda s, f: (s, f + 2) if f // 2 == 2 else (s, f - 2) if f // 2 == 1 else None,
                )
                main, main_head, main_tail, lane_shards, core_shards = together(
                    main, main_head, main_tail, lane_shards, core_shards
                )
            low = sent(main_tail, following)
            high = sent(main_head, preceding)
        elif k == 3 and split:
            pairs = [v for both in zip(lane_shards, core_shards) for v in both]
            early_main, main_squares = stem_early(main, pairs, core_id)
            final, early_main, low, high, main, cot_high = together(
                final, early_main, low, high, main, cot_high
            )
            outer = (chip == 0) | (chip == chips - 1)
            lane_shards.append(jnp.where(outer, final, near))
            core_shards.append(swapped(lane_shards[-1], 0, 1))
            chip_of.append(jnp.where(outer, chips - 1 - chip, jnp.where(chip == 1, 0, chips - 1)))
        else:
            rising, falling = together(rising, falling)
    for k in range(len(lane_shards), chips):
        add_shard(k, rising, falling)
    height = round_up(width, 64 * seq_size)
    main_other = swapped(main, 0, 1)
    places = jnp.stack([core] + chip_of).astype(jnp.int32)
    all_pairs = [v for both in zip(lane_shards, core_shards) for v in both]
    if split:
        all_pairs, main_other = together(all_pairs, main_other)
        early = [early_main, main_squares]

    ids = segments[0]
    total_slots = ids.shape[0]
    centre = seq_index * slots + jnp.arange(-2, slots + 2, dtype=jnp.int32)
    near = centre[:, None] + jnp.arange(-2, 3, dtype=jnp.int32)[None, :]
    inside = (near >= 0) & (near < total_slots) & ((centre >= 0) & (centre < total_slots))[:, None]
    same = (
        ids[jnp.clip(near, 0, total_slots - 1)] == ids[jnp.clip(centre, 0, total_slots - 1)][:, None]
    )
    mask = (inside & same).astype(F32).reshape(-1)
    features, d_stem, give, keep = layer(
        main, low, high, cot, cot_low, cot_high, all_pairs, early, places, mask, slots, channels
    )
    got = swapped(give, 0, 1)
    pixels = turned(main, main_other, height, tokens)
    middle = round_up(width // 2, LANES)

    seq_bits = bits_of(seq_size)
    chip_bits = bits_of(chips)
    line_share = height // seq_size // 4 // 32 * 32
    share = height // seq_size - line_share
    where = jnp.stack([seq_index, chip]).astype(jnp.int32)
    first_bits = [seq_bits[0], seq_bits[-1]]
    sizes = (chips, seq_size, shard, share, line_share, first_bits)
    gives = weight_part(pixels, keep, got, where, *sizes, True)
    keeps = weight_part(pixels, keep, got, where, *sizes, False)
    scale = 1.0 / math.sqrt(tokens * seq_size * fsdp_size)
    mine = {("seq", b): bit_at(seq_index, b) for b in seq_bits}
    mine |= {("chip", b): bit_at(chip, b) for b in chip_bits}
    seq_labels = [("seq", b) for b in seq_bits]
    chip_labels = [("chip", b) for b in chip_bits]
    orders = [order + chip_labels[:-1] for order in (seq_labels, seq_labels[::-1])]
    chains = [
        halving(
            gives[:2],
            keeps[:2],
            chip_labels[:-1][::-1] + seq_labels[::-1],
            orders,
            mine,
            chip_labels[-1],
        ),
        halving(
            gives[2:],
            keeps[2:],
            chip_labels[::-1] + seq_labels[::-1],
            [chip_labels[::-1] + seq_labels],
            mine,
        ),
    ]
    last_round = len(seq_bits) + len(chip_bits) - 1

    def left_pixels(ready, _):
        inputs, ready = together(d_stem, ready)
        return ready, pixel_grads(inputs, all_pairs, places, 0, middle)

    (plane, line), grad_rows = in_rounds(chains, {last_round: left_pixels})
    rows_mine = finish([plane, line], scale)
    d_stem, rows_mine = together(d_stem, rows_mine)
    pieces = [rows_mine] + [swapped(rows_mine, o, 0) for o in range(1, seq_size)]
    grad_rows = pixel_grads(d_stem, all_pairs, places, middle, width, grad_rows)
    pieces, grad_rows = together(pieces, grad_rows)
    grad_weight, grad_channels = unpacked(
        pieces, seq_index, width, share, line_share, padded - 16
    )
    return (features[None], grad_rows[None], grad_weight, grad_channels)


def solution(mesh):
    in_specs = (
        P("fsdp", "seq", None),
        P("fsdp", "seq"),
        P("fsdp", None),
        P("fsdp", None),
        P("fsdp"),
        P(None, "fsdp"),
        P("fsdp", "seq", None),
    )
    out_specs = (P("fsdp", "seq", None), P("fsdp", "seq", None), P("fsdp", None), P(None, "fsdp"))
    return jax.shard_map(shards, mesh=mesh, in_specs=in_specs, out_specs=out_specs, check_vma=False)
```
